32 devices in a mesh: dp: 4 (over y, x), blk: 8 (over z, core).
Axes of the slice: x: 2, y: 2, z: 4, core: 2. Of those that a mesh axis runs over, the one named last changes fastest.
Arguments:
- tokens: bfloat16 [2, 4, 1024, 768], P(None, 'dp', 'blk'), may hold values from -6 to 6
- lengths: int32 [2, 4], P(None, 'dp'), may hold values from 256 to 1024, as said below
- w_query: bfloat16 [768, 768], P('dp'), may hold values from -0.21875 to 0.21875
- w_key: bfloat16 [768, 768], P('dp'), may hold values from -0.21875 to 0.21875
- w_value: bfloat16 [768, 768], P('dp'), may hold values from -0.21875 to 0.21875
- w_output: bfloat16 [768, 768], P('dp'), may hold values from -4 to 4
- w_gate: bfloat16 [768, 3072], P('dp'), may hold values from -0.21875 to 0.21875
- w_up: bfloat16 [768, 3072], P('dp'), may hold values from -0.21875 to 0.21875
- w_down: bfloat16 [3072, 768], P('dp'), may hold values from -0.109375 to 0.109375
- first_gain: bfloat16 [768], P('dp'), may hold values from 0.5 to 1.5
- first_bias: bfloat16 [768], P('dp'), may hold values from -3 to 3
- second_gain: bfloat16 [768], P('dp'), may hold values from 0.5 to 1.5
- second_bias: bfloat16 [768], P('dp'), may hold values from -3 to 3
- cotangent: bfloat16 [2, 4, 1024, 768], P(None, 'dp', 'blk'), may hold values from -6 to 6
Outputs:
- layer_out: bfloat16 [2, 4, 1024, 768], P(None, 'dp', 'blk')
- grad_tokens: float32 [2, 4, 1024, 768], P(None, 'dp', 'blk')
- grad_query: float32 [768, 768], P('dp')
- grad_key: float32 [768, 768], P('dp')
- grad_value: float32 [768, 768], P('dp')
- grad_output: float32 [768, 768], P('dp')
- grad_gate: float32 [768, 3072], P('dp')
- grad_up: float32 [768, 3072], P('dp')
- grad_down: float32 [3072, 768], P('dp')
- grad_first_gain: float32 [768], P('dp')
- grad_first_bias: float32 [768], P('dp')
- grad_second_gain: float32 [768], P('dp')
- grad_second_bias: float32 [768], P('dp')
The draws below stay inside these ranges and needn't reach their ends.
Inputs may be any that keep to these rules, and one draw needn't show every extreme that they name: `lengths`: each entry is the number of valid leading slots of its sequence. Among the 2 sequences that share an index of dp, at least one has all 1024 slots valid.
All inputs are finite; a program needn't handle non-finite values.
Results may differ from the reference program's by a relative error of at most 0.025.
Values may be sent and summed in bfloat16 or wider, within the bound.
No kernel may reach another device: no remote copies, remote signals or barrier semaphores. Data moves between devices by JAX's collectives and lax.ppermute only.
A program may use at most 256 MiB of HBM per device.

```python
import math
import jax
import jax.numpy as jnp
from jax import lax

D = 768
HEADS = 12
HEAD_DIM = 64
FF = 3072
SEQ_MB = 1
MICRO = 2
SEQ_LEN = 1024
SEQ_ALL = 4


def draw_lengths(key, part):
    key = jax.random.fold_in(key, 7)
    key_values, key_choose = jax.random.split(key)
    groups = SEQ_ALL // SEQ_MB
    drawn = jax.random.randint(key_values, (MICRO, groups, SEQ_MB), SEQ_LEN // 4, SEQ_LEN + 1)
    chosen = jax.random.randint(key_choose, (groups,), 0, MICRO * SEQ_MB)
    micro_pos = jax.lax.broadcasted_iota(jnp.int32, (MICRO, groups, SEQ_MB), 0)
    member_pos = jax.lax.broadcasted_iota(jnp.int32, (MICRO, groups, SEQ_MB), 2)
    flat_pos = micro_pos * SEQ_MB + member_pos
    filled = jnp.where(flat_pos == chosen[None, :, None], SEQ_LEN, drawn)
    return filled.reshape(MICRO, SEQ_ALL).astype(jnp.int32)


def block_scale(rng, shape, pieces, least, top_value):
    level, own = 1.0, jax.random.fold_in(rng, 6)
    for axis_at, parts in pieces:
        steps = jnp.exp(jax.random.uniform(jax.random.fold_in(own, axis_at), (parts,), jnp.float32, least / len(pieces), top_value / len(pieces)))
        level = level * jnp.repeat(steps, shape[axis_at] // parts).reshape([-1 if axis == axis_at else 1 for axis in range(len(shape))])
    return level


def bell_draw(own_key, dims, width, bound, shards=(), held_as=jnp.bfloat16):
    entries = width * jax.random.normal(own_key, dims, jnp.float32)
    if shards:
        entries = entries * block_scale(own_key, dims, shards, -0.22, 0.18)
    return jnp.clip(entries, -bound, bound).astype(held_as)


def setup_inputs(seed: int = 0) -> dict:
    keys = jax.random.split(jax.random.key(seed), 15)
    return {
        "tokens": bell_draw(keys[0], (MICRO, SEQ_ALL, SEQ_LEN, D), 1.0, 6.0, ((1, 4), (2, 8))),
        "lengths": draw_lengths(jax.random.fold_in(keys[14], 71), 0),
        "w_query": bell_draw(keys[2], (D, D), D ** -0.5, 0.21875, ((0, 4),)),
        "w_key": bell_draw(keys[3], (D, D), D ** -0.5, 0.21875, ((0, 4),)),
        "w_value": bell_draw(keys[4], (D, D), D ** -0.5, 0.21875, ((0, 4),)),
        "w_output": bell_draw(keys[5], (D, D), (max(1, 3 * D // SEQ_LEN)) ** -0.5, 4.0, ((0, 4),)),
        "w_gate": bell_draw(keys[6], (D, FF), D ** -0.5, 0.21875, ((0, 4),)),
        "w_up": bell_draw(keys[7], (D, FF), D ** -0.5, 0.21875, ((0, 4),)),
        "w_down": bell_draw(keys[8], (FF, D), FF ** -0.5, 0.109375, ((0, 4),)),
        "first_gain": jnp.clip(1.0 + 0.1 * jax.random.normal(keys[9], (D,), jnp.float32), 0.5, 1.5).astype(jnp.bfloat16),
        "first_bias": bell_draw(keys[10], (D,), 0.5, 3.0, ((0, 4),)),
        "second_gain": jnp.clip(1.0 + 0.1 * jax.random.normal(keys[11], (D,), jnp.float32), 0.5, 1.5).astype(jnp.bfloat16),
        "second_bias": bell_draw(keys[12], (D,), 0.5, 3.0, ((0, 4),)),
        "cotangent": bell_draw(keys[13], (MICRO, SEQ_ALL, SEQ_LEN, D), 1.0, 6.0, ((1, 4), (2, 8))),
    }


PRECISE = lax.Precision.HIGHEST

@jax.custom_vjp
def low(v):
    return lax.optimization_barrier(v.astype(jnp.bfloat16)).astype(jnp.float32)

@jax.custom_vjp
def low_back(v):
    return v

def low_keep(v):
    return (low(v), None)

def low_pass(kept, grad):
    return (grad,)

def back_keep(v):
    return (v, None)

def back_low(kept, grad):
    return (low(grad),)
low.defvjp(low_keep, low_pass)
low_back.defvjp(back_keep, back_low)

def rotary(positions, head_dim):
    half_dim = head_dim // 2
    frequency = 1000.0 ** (-(jnp.arange(half_dim).astype(jnp.float32) * 2.0 / head_dim))
    angles = positions.astype(jnp.float32)[:, None] * frequency[None, :]
    return (jnp.cos(angles), jnp.sin(angles))

def rotate(values, cosine_table, sine_table):
    half_dim = values.shape[-1] // 2
    first_half = values[..., :half_dim]
    second_half = values[..., half_dim:]
    cosine_b = cosine_table[:, None, :]
    sine_b = sine_table[:, None, :]
    return jnp.concatenate([first_half * cosine_b - second_half * sine_b, second_half * cosine_b + first_half * sine_b], axis=-1)

def layer_norm(features):
    average = lax.optimization_barrier(jnp.mean(features, axis=-1, keepdims=True))
    centred = features - average
    variance = lax.optimization_barrier(jnp.mean(centred * centred, axis=-1, keepdims=True))
    return centred * lax.rsqrt(variance + 1e-05)

def attend(query_block, keys_rot, values_rot, valid_mask):
    scores = jnp.einsum('qhd,khd->hqk', query_block, keys_rot, precision=PRECISE) * 0.125
    scores = low_back(scores)
    scores = jnp.where(valid_mask[None, None, :], scores, -1e+30)
    probability = low(jax.nn.softmax(scores, axis=-1))
    return jnp.einsum('hqk,khd->qhd', probability, values_rot, precision=PRECISE)

def sequence_out(hidden_rows, length, w_query, w_key, w_value, w_output, w_gate, w_up, w_down, first_gain, first_bias, second_gain, second_bias):
    slot_index = jnp.arange(SEQ_LEN)
    valid_mask = slot_index < length
    cosine_table, sine_table = rotary(slot_index, HEAD_DIM)

    def split_heads(source):
        return source.reshape(SEQ_LEN, HEADS, HEAD_DIM)
    queries = low(rotate(split_heads(low_back(jnp.dot(hidden_rows, w_query, precision=PRECISE))), cosine_table, sine_table))
    keys_rot = low(rotate(split_heads(low_back(jnp.dot(hidden_rows, w_key, precision=PRECISE))), cosine_table, sine_table))
    values_rot = split_heads(low(low_back(jnp.dot(hidden_rows, w_value, precision=PRECISE))))
    block_rows = math.gcd(SEQ_LEN, 512)
    checked = jax.checkpoint(attend)
    query_blocks = queries.reshape(SEQ_LEN // block_rows, block_rows, HEADS, HEAD_DIM)
    attended = lax.map(lambda query_block: checked(query_block, keys_rot, values_rot, valid_mask), query_blocks)
    attended = low(low_back(attended.reshape(SEQ_LEN, D)))
    branch_out = low_back(jnp.dot(attended, w_output, precision=PRECISE))
    normed = layer_norm(hidden_rows + branch_out) * first_gain + first_bias
    normed_low = low(normed)
    gate_pre = low_back(jnp.dot(normed_low, w_gate, precision=PRECISE))
    up_pre = low_back(jnp.dot(normed_low, w_up, precision=PRECISE))
    hidden = low(jax.nn.silu(gate_pre) * up_pre)
    ffn_out = low_back(jnp.dot(hidden, w_down, precision=PRECISE))
    layer_rows = layer_norm(normed + ffn_out) * second_gain + second_bias
    return jnp.where(valid_mask[:, None], layer_rows, 0.0)

def reference(tokens, lengths, w_query, w_key, w_value, w_output, w_gate, w_up, w_down, first_gain, first_bias, second_gain, second_bias, cotangent):
    flat_tokens = tokens.reshape(-1, SEQ_LEN, D).astype(jnp.float32)
    flat_cotangent = cotangent.reshape(-1, SEQ_LEN, D).astype(jnp.float32)
    flat_lengths = lengths.reshape(-1)
    weight_list = tuple((weight.astype(jnp.float32) for weight in (w_query, w_key, w_value, w_output, w_gate, w_up, w_down, first_gain, first_bias, second_gain, second_bias)))

    def scan_step(totals, scan_item):
        hidden_rows, length, upstream = scan_item
        result, pullback = jax.vjp(lambda rows_in, *weights_in: sequence_out(rows_in, length, *weights_in), hidden_rows, *weight_list)
        gradients = pullback(upstream)
        totals = tuple((running + gradient for running, gradient in zip(totals, gradients[1:])))
        return (totals, (result.astype(jnp.bfloat16), gradients[0]))
    initial = tuple((jnp.zeros_like(weight) for weight in weight_list))
    totals, (results, grad_rows) = lax.scan(scan_step, initial, (flat_tokens, flat_lengths, flat_cotangent))
    return (results.reshape(tokens.shape), grad_rows.reshape(tokens.shape), totals[0], totals[1], totals[2], totals[3], totals[4], totals[5], totals[6], totals[7], totals[8], totals[9], totals[10])
```

```python
import functools

import jax
import jax.numpy as jnp
import numpy as np
from jax import lax
from jax.experimental import pallas as pl
from jax.experimental.pallas import tpu as pltpu
from jax.sharding import PartitionSpec as P

HEAD_DIM = 64
WIDE = 128
PARTS = 4
LOW, FULL = jnp.bfloat16, jnp.float32
VMEM_BYTES = 60 * 1024 * 1024


def mm(left, right):
    return jnp.dot(left, right, preferred_element_type=FULL)


def mm_nt(left, right):
    return lax.dot_general(left, right, (((1,), (1,)), ((), ())), preferred_element_type=FULL)


def mm_tn(left, right):
    return lax.dot_general(left, right, (((0,), (0,)), ((), ())), preferred_element_type=FULL)


def hop(value, axis, bit):
    size = lax.axis_size(axis)
    return lax.ppermute(value, axis, [(at, at ^ bit) for at in range(size)])


def position_table(seq_len):
    half = HEAD_DIM // 2
    frequency = np.float32(1000.0) ** (-(np.arange(half, dtype=np.float32) * np.float32(2.0) / np.float32(HEAD_DIM)))
    angles = np.arange(seq_len, dtype=np.float32)[:, None] * frequency[None, :]
    cosine = np.cos(angles).astype(np.float32)
    sine = np.sin(angles).astype(np.float32)
    place = np.broadcast_to(np.arange(seq_len, dtype=np.float32)[:, None], (seq_len, WIDE))
    return np.concatenate([cosine] * 4 + [sine, sine, -sine, -sine, place], axis=1)


def swap_matrix(heads):
    half = HEAD_DIM // 2
    out = np.zeros((heads * HEAD_DIM, heads * WIDE), np.float32)
    for h in range(heads):
        for f in range(HEAD_DIM):
            out[h * HEAD_DIM + f, h * WIDE + f] = 1.0
        for f in range(half):
            out[h * HEAD_DIM + half + f, h * WIDE + HEAD_DIM + f] = -1.0
            out[h * HEAD_DIM + f, h * WIDE + HEAD_DIM + half + f] = 1.0
    return out


def spread_matrix(heads):
    out = np.zeros((heads * HEAD_DIM, heads * WIDE), np.float32)
    for h in range(heads):
        for f in range(HEAD_DIM):
            out[h * HEAD_DIM + f, h * WIDE + f] = 1.0
    return out


def project_kernel(heads, block, x_ref, w_ref, swap_ref, spread_ref, table_ref, q_ref, k_ref, v_ref):
    parts = w_ref.shape[0]

    def weight(which, matrix):
        rows = jnp.concatenate([w_ref[d, which] for d in range(parts)], axis=0)
        return mm(rows, matrix).astype(LOW)

    w_q = weight(0, swap_ref[...])
    w_k = weight(1, swap_ref[...])
    w_v = weight(2, spread_ref[...])
    for start in range(0, x_ref.shape[0], block):
        rows = slice(start, start + block)
        x = x_ref[rows, :]
        cosine, sine = table_ref[rows, :WIDE], table_ref[rows, WIDE : 2 * WIDE]
        for out_ref, w, scale in ((q_ref, w_q, 0.0625), (k_ref, w_k, None)):
            made = mm(x, w)
            for h in range(heads):
                one = made[:, h * WIDE : (h + 1) * WIDE]
                turned = (one * cosine + pltpu.roll(one, HEAD_DIM, 1) * sine).astype(LOW)
                if scale is not None:
                    turned = turned * jnp.asarray(scale, LOW)
                out_ref[h, rows, :] = turned
        made = mm(x, w_v).astype(LOW)
        for h in range(heads):
            v_ref[h, rows, :] = made[:, h * WIDE : (h + 1) * WIDE]


def attend_kernel(heads, block, len_ref, q_ref, k_ref, v_ref, table_ref, spread_ref, out_ref, lse_ref, bias_ref, wide_ref):
    row_count = q_ref.shape[1]
    place = table_ref[:, 2 * WIDE :]
    bias_ref[...] = jnp.where(place < len_ref[0, 0], 0.0, -1e30)
    for h in range(heads):
        keys = k_ref[h]
        values_t = v_ref[h].T

        def step(number, carry, h=h, keys=keys, values_t=values_t):
            rows = pl.ds(pl.multiple_of(number * block, block), block)
            bias = jnp.concatenate([bias_ref[...]] * (block // WIDE), axis=1)
            scores = mm_nt(keys, q_ref[h, rows, :]) + bias
            top = jnp.max(scores, axis=0, keepdims=True)
            weights = jnp.exp(scores - top)
            total = jnp.sum(weights, axis=0, keepdims=True)
            lse_ref[h, :, rows] = top + jnp.log(total)
            summed = mm(values_t, weights.astype(LOW)) / total
            wide_ref[rows, h * WIDE : (h + 1) * WIDE] = summed.T.astype(LOW)
            return carry

        lax.fori_loop(0, row_count // block, step, 0)
    out_ref[...] = mm_nt(wide_ref[...], spread_ref[...]).astype(LOW)


def attend_back_kernel(
    heads, block, len_ref, q_ref, k_ref, v_ref, table_ref, spread_ref, lse_ref, grad_ref,
    dq_ref, dk_ref, dv_ref, bias_ref, grad_wide_ref, dq_wide_ref, dk_wide_ref, dv_wide_ref, dk_sum_ref, dv_sum_ref,
):
    row_count = q_ref.shape[1]
    place = table_ref[:, 2 * WIDE :]
    bias_ref[...] = jnp.where(place < len_ref[0, 0], 0.0, -1e30)
    grad_wide_ref[...] = mm(grad_ref[...], spread_ref[...]).astype(LOW)

    def unturn(value, rows):
        cosine, sine = table_ref[rows, :WIDE], table_ref[rows, WIDE : 2 * WIDE]
        return (value * cosine - pltpu.roll(value, HEAD_DIM, 1) * sine).astype(LOW)

    for h in range(heads):
        lanes = slice(h * WIDE, (h + 1) * WIDE)
        keys, values = k_ref[h], v_ref[h]
        keys_t = keys.T
        dk_sum_ref[...] = jnp.zeros_like(dk_sum_ref)
        dv_sum_ref[...] = jnp.zeros_like(dv_sum_ref)

        def step(number, carry, h=h, lanes=lanes, keys=keys, values=values, keys_t=keys_t):
            rows = pl.ds(pl.multiple_of(number * block, block), block)
            bias = jnp.concatenate([bias_ref[...]] * (block // WIDE), axis=1)
            queries, grads = q_ref[h, rows, :], grad_wide_ref[rows, lanes]
            probs = jnp.exp(mm_nt(keys, queries) + bias - lse_ref[h, :, rows])
            grad_probs = mm_nt(values, grads)
            delta = jnp.sum(probs * grad_probs, axis=0, keepdims=True)
            grad_scores = (probs * (grad_probs - delta)).astype(LOW)
            dv_sum_ref[...] += mm(probs.astype(LOW), grads)
            dk_sum_ref[...] += mm(grad_scores, queries)
            dq = mm(keys_t, grad_scores).T * 0.125
            dq_wide_ref[rows, lanes] = unturn(dq, rows)
            return carry

        lax.fori_loop(0, row_count // block, step, 0)
        dk_wide_ref[:, lanes] = unturn(dk_sum_ref[...] * 2.0, slice(None))
        dv_wide_ref[:, lanes] = dv_sum_ref[...].astype(LOW)
    for out_ref, wide_ref in ((dq_ref, dq_wide_ref), (dk_ref, dk_wide_ref), (dv_ref, dv_wide_ref)):
        out_ref[...] = mm_nt(wide_ref[...], spread_ref[...]).astype(LOW)


VMEM = pl.BlockSpec(memory_space=pltpu.VMEM)
SMEM = pl.BlockSpec(memory_space=pltpu.SMEM)


def kernel_call(body, outs, in_specs, scratch, flops, exps, *operands):
    moved = sum(o.size * o.dtype.itemsize for o in (*operands, *outs))
    return pl.pallas_call(
        body,
        out_shape=outs,
        in_specs=in_specs,
        out_specs=[VMEM] * len(outs),
        scratch_shapes=scratch,
        compiler_params=pltpu.CompilerParams(vmem_limit_bytes=VMEM_BYTES),
        cost_estimate=pl.CostEstimate(flops=flops, bytes_accessed=moved, transcendentals=exps),
    )(*operands)


def project(x, w, swap, spread, table, heads):
    rows, width = x.shape
    shape = jax.ShapeDtypeStruct((heads, rows, WIDE), LOW)
    return kernel_call(
        functools.partial(project_kernel, heads, min(256, rows)), [shape] * 3, [VMEM] * 5, [],
        2 * rows * width * 3 * heads * WIDE, 0, x, w, swap, spread, table,
    )


def attend(length, q, k, v, table, spread):
    heads, rows, _ = q.shape
    keys = k.shape[1]
    outs = [
        jax.ShapeDtypeStruct((rows, heads * HEAD_DIM), LOW),
        jax.ShapeDtypeStruct((heads, 1, rows), FULL),
    ]
    scratch = [pltpu.VMEM((keys, WIDE), FULL), pltpu.VMEM((rows, heads * WIDE), LOW)]
    return kernel_call(
        functools.partial(attend_kernel, heads, min(256, rows)), outs, [SMEM] + [VMEM] * 5, scratch,
        4 * heads * rows * keys * WIDE, heads * rows * keys, length, q, k, v, table, spread,
    )


def attend_back(length, q, k, v, table, spread, lse, grad):
    heads, rows, _ = q.shape
    keys = k.shape[1]
    outs = [jax.ShapeDtypeStruct((count, heads * HEAD_DIM), LOW) for count in (rows, keys, keys)]
    scratch = [
        pltpu.VMEM((keys, WIDE), FULL),
        pltpu.VMEM((rows, heads * WIDE), LOW),
        pltpu.VMEM((rows, heads * WIDE), LOW),
        pltpu.VMEM((keys, heads * WIDE), LOW),
        pltpu.VMEM((keys, heads * WIDE), LOW),
        pltpu.VMEM((keys, WIDE), FULL),
        pltpu.VMEM((keys, WIDE), FULL),
    ]
    return kernel_call(
        functools.partial(attend_back_kernel, heads, min(256, rows)), outs, [SMEM] + [VMEM] * 7, scratch,
        10 * heads * rows * keys * WIDE, heads * rows * keys, length, q, k, v, table, spread, lse, grad,
    )


def gather_rows(piece, place):
    count = lax.axis_size("dp")
    if count != 4:
        return lax.all_gather(piece, "dp", axis=0, tiled=False)
    axis = piece.ndim - 2
    half = piece.shape[axis] // 2
    from_x, from_y = hop(piece, "dp", 1), hop(piece, "dp", 2)
    far_a = hop(lax.slice_in_dim(from_x, 0, half, axis=axis), "dp", 2)
    far_b = hop(lax.slice_in_dim(from_y, half, 2 * half, axis=axis), "dp", 1)
    far = jnp.concatenate([far_a, far_b], axis=axis)
    out = jnp.zeros((count,) + piece.shape, piece.dtype)
    for distance, part in enumerate((piece, from_x, from_y, far)):
        out = lax.dynamic_update_index_in_dim(out, part, place ^ distance, 0)
    return out


def scatter_rows(terms, place):
    count = lax.axis_size("dp")
    if count != 4:
        return lax.psum_scatter(terms, "dp", scatter_dimension=0, tiled=False).astype(FULL)
    half = terms.shape[1] // 2
    own, near_x, near_y, far = (
        lax.dynamic_index_in_dim(terms, place ^ distance, 0, keepdims=False) for distance in range(4)
    )
    got_x = hop(jnp.concatenate([near_x[:half], far[:half]]), "dp", 1).astype(FULL)
    got_y = hop(jnp.concatenate([near_y[half:], far[half:]]), "dp", 2).astype(FULL)
    low_sum, low_next = own[:half] + got_x[:half], near_y[:half] + got_x[half:]
    high_sum, high_next = own[half:] + got_y[:half], near_x[half:] + got_y[half:]
    low_sum = low_sum + hop(low_next.astype(LOW), "dp", 2).astype(FULL)
    high_sum = high_sum + hop(high_next.astype(LOW), "dp", 1).astype(FULL)
    return jnp.concatenate([low_sum, high_sum])


def bits_between(low, high):
    bits = []
    while low < high:
        bits.append(low)
        low *= 2
    return bits


def sum_bits(value, place, bits):
    for bit in bits:
        half = value.shape[0] // 2
        upper = (place // bit) % 2
        keep = lax.dynamic_slice_in_dim(value, upper * half, half, 0)
        send = lax.dynamic_slice_in_dim(value, (1 - upper) * half, half, 0)
        value = keep + hop(send.astype(LOW), "blk", bit).astype(FULL)
    value = value.astype(LOW)
    for bit in reversed(bits):
        other = hop(value, "blk", bit)
        upper = (place // bit) % 2 == 1
        value = jnp.where(upper, jnp.concatenate([other, value]), jnp.concatenate([value, other]))
    return value


def fold_rows(part):
    half = part.shape[0] // 2
    return part[:half] + hop(part[half:].astype(LOW), "blk", 1).astype(FULL)


def both_rows(own):
    return jnp.concatenate([own, hop(own, "blk", 1)])


def norm_parts(rows):
    centred = rows - jnp.mean(rows, axis=-1, keepdims=True)
    scale = lax.rsqrt(jnp.mean(centred * centred, axis=-1, keepdims=True) + 1e-05)
    return centred * scale, scale


def norm_back(upstream, gain, unit, scale):
    inner = upstream * gain
    grad = (
        inner
        - jnp.mean(inner, axis=-1, keepdims=True)
        - unit * jnp.mean(inner * unit, axis=-1, keepdims=True)
    ) * scale
    return grad, jnp.sum(upstream * unit, axis=0), jnp.sum(upstream, axis=0)


def shards(
    tokens, lengths, w_query, w_key, w_value, w_output, w_gate, w_up, w_down,
    first_gain, first_bias, second_gain, second_bias, cotangent,
):
    _, _, local, width = tokens.shape
    dp_count, blk_count = lax.axis_size("dp"), lax.axis_size("blk")
    dp, blk = lax.axis_index("dp"), lax.axis_index("blk")
    side = blk_count // 2
    which = blk // side
    first = which == 0
    core = blk % 2
    part = blk % PARTS
    heads = width // HEAD_DIM // PARTS
    columns = heads * HEAD_DIM
    spread_bits = bits_between(PARTS, side)
    table = jnp.asarray(position_table(local * blk_count))
    swap = jnp.asarray(swap_matrix(heads), LOW)
    spread = jnp.asarray(spread_matrix(heads), LOW)

    def mine(source):
        return jnp.where(first, source[0, 0], source[1, 0])

    def theirs(source):
        return jnp.where(first, source[1, 0], source[0, 0])

    own_half = mine(tokens)
    got_half = hop(theirs(tokens), "blk", side)
    x_own = jnp.concatenate([own_half, got_half])
    x_core = hop(x_own, "blk", 1)
    x_near = hop(x_own, "blk", 2)
    x_far = hop(x_near, "blk", 1)
    x_all = jnp.concatenate([x_own, x_core, x_near, x_far])

    rows = w_query.shape[0]
    w_qkv = jnp.stack(
        [lax.dynamic_slice_in_dim(w, part * columns, columns, 1) for w in (w_query, w_key, w_value)]
    )
    all_qkv = gather_rows(w_qkv, dp)
    half_width = width // 2
    vectors = jnp.stack([first_gain, first_bias, second_gain, second_bias]).reshape(-1)
    extra_rows = -(-vectors.shape[0] // half_width)

    def pad_extra(flat):
        lead = flat.shape[:-1]
        flat = jnp.pad(flat, [(0, 0)] * len(lead) + [(0, 32 * half_width - flat.shape[-1])])
        return flat.reshape(*lead, 32, half_width)

    w_out_half = lax.dynamic_slice_in_dim(w_output, core * half_width, half_width, 1)
    all_out = gather_rows(jnp.concatenate([w_out_half, pad_extra(vectors)]), dp)
    all_vectors = all_out[:, rows : rows + extra_rows].reshape(dp_count, -1)[:, : vectors.shape[0]]
    all_vectors = all_vectors.reshape(dp_count, 4, rows).transpose(1, 0, 2).reshape(4, width).astype(FULL)
    gain_one, bias_one, gain_two, bias_two = all_vectors

    ff_rows = w_down.shape[0]
    ff_half = ff_rows // 2

    def core_columns(w):
        w = w.reshape(rows, dp_count, 2, ff_half)
        return jnp.where(core == 0, w[:, :, 0], w[:, :, 1]).reshape(rows, dp_count * ff_half)

    full_gate = gather_rows(core_columns(w_gate), dp).reshape(width, dp_count * ff_half)
    full_up = gather_rows(core_columns(w_up), dp).reshape(width, dp_count * ff_half)
    down_half = lax.dynamic_slice_in_dim(w_down, core * ff_half, ff_half, 0)
    full_down = gather_rows(down_half, dp).reshape(dp_count * ff_half, width)

    out_rows = all_out[:, :rows].reshape(PARTS, columns, half_width)

    def head_rows(distance):
        return lax.dynamic_index_in_dim(out_rows, part ^ distance, 0, keepdims=False)

    out_mine = jnp.concatenate([head_rows(0), head_rows(2)])
    out_other = hop(jnp.concatenate([head_rows(1), head_rows(3)]), "blk", 1)
    core_out = jnp.where(
        core == 0,
        jnp.concatenate([out_mine, out_other], axis=1),
        jnp.concatenate([out_other, out_mine], axis=1),
    )

    pieces = []
    for distance in range(side):
        for away in (0, side):
            start = (blk ^ distance ^ away) * local
            pieces.append(lax.dynamic_slice_in_dim(table, start, local, 0))
    key_table = jnp.concatenate(pieces)
    row_count = x_all.shape[0]
    length = jnp.where(first, lengths[0, 0], lengths[1, 0]).astype(FULL).reshape(1, 1)
    row_valid = key_table[: 2 * local, 2 * WIDE : 2 * WIDE + 1] < length

    queries, keys, values = project(x_all, all_qkv, swap, spread, key_table[:row_count], heads)
    for bit in spread_bits:
        keys = jnp.concatenate([keys, hop(keys, "blk", bit)], axis=1)
        values = jnp.concatenate([values, hop(values, "blk", bit)], axis=1)
    attended, lse = attend(length, queries, keys, values, key_table, spread)
    chip_rows = row_count // 2
    att_other = hop(attended[chip_rows:], "blk", 2)
    att_chip = jnp.concatenate([attended[:chip_rows], att_other], axis=1)
    branch = fold_rows(mm(att_chip, core_out))
    residual_one = x_own.astype(FULL) + branch
    unit_one, scale_one = norm_parts(residual_one)
    normed = unit_one * gain_one + bias_one

    normed_low = both_rows(normed.astype(LOW))
    gate_pre = mm(normed_low, full_gate)
    up_pre = mm(normed_low, full_up)
    sigma = 1.0 / (1.0 + jnp.exp(-gate_pre))
    silu = gate_pre * sigma
    hidden = (silu * up_pre).astype(LOW)
    residual_two = normed + fold_rows(mm(hidden, full_down))
    unit_two, scale_two = norm_parts(residual_two)
    layer_rows = jnp.where(row_valid, unit_two * gain_two + bias_two, 0.0).astype(LOW)

    cot = jnp.concatenate([mine(cotangent), hop(theirs(cotangent), "blk", side)])
    upstream = jnp.where(row_valid, cot.astype(FULL), 0.0)
    grad_two, grad_gain_two, grad_bias_two = norm_back(upstream, gain_two, unit_two, scale_two)
    grad_ffn = both_rows(grad_two.astype(LOW))
    grad_down_part = mm_tn(hidden, grad_ffn).astype(LOW)
    grad_hidden = mm_nt(grad_ffn, full_down)
    grad_gate_low = (grad_hidden * up_pre * (sigma + silu * (1.0 - sigma))).astype(LOW)
    grad_up_low = (grad_hidden * silu).astype(LOW)
    grad_gate_part = mm_tn(normed_low, grad_gate_low).astype(LOW)
    grad_up_part = mm_tn(normed_low, grad_up_low).astype(LOW)
    grad_normed = grad_two + fold_rows(mm_nt(grad_gate_low, full_gate) + mm_nt(grad_up_low, full_up))
    grad_one, grad_gain_one, grad_bias_one = norm_back(grad_normed, gain_one, unit_one, scale_one)
    grad_branch = both_rows(grad_one.astype(LOW))
    grad_att = mm_nt(grad_branch, core_out).astype(LOW)
    grad_other = hop(grad_att[:, columns:], "blk", 2)
    grad_attended = jnp.concatenate([grad_att[:, :columns], grad_other])
    grad_out_part = mm_tn(att_chip, grad_branch).astype(LOW)

    grad_q, grad_k, grad_v = attend_back(length, queries, keys, values, key_table, spread, lse, grad_attended)
    for bit in reversed(spread_bits):
        half = grad_k.shape[0] // 2
        grad_k, grad_v = (
            (value[:half].astype(FULL) + hop(value[half:], "blk", bit).astype(FULL)).astype(LOW)
            for value in (grad_k, grad_v)
        )
    grad_qkv = jnp.concatenate([grad_q, grad_k, grad_v], axis=1)
    full_qkv = all_qkv.transpose(0, 2, 1, 3).reshape(width, 3 * columns)
    token_terms = mm_nt(grad_qkv, full_qkv)
    block = 2 * local
    core_sum = jnp.concatenate([token_terms[:block], token_terms[2 * block : 3 * block]]) + hop(
        jnp.concatenate([token_terms[block : 2 * block], token_terms[3 * block :]]).astype(LOW), "blk", 1
    ).astype(FULL)
    grad_rows = grad_one + core_sum[:block] + hop(core_sum[block:].astype(LOW), "blk", 2).astype(FULL)

    def send_home(rows_now):
        back = hop(rows_now[local:].astype(LOW), "blk", side).astype(rows_now.dtype)
        own = rows_now[:local]
        return jnp.where(first, jnp.stack([own, back]), jnp.stack([back, own]))[:, None]

    layer_out = send_home(layer_rows)
    grad_tokens = send_home(grad_rows)

    z_bits = bits_between(2, blk_count)

    def finish(terms):
        return sum_bits(scatter_rows(terms, dp), blk, z_bits)

    def join_columns(own):
        other = hop(own, "blk", 1)
        own, other = (v.reshape(rows, dp_count, 1, ff_half) for v in (own, other))
        joined = jnp.where(
            core == 0, jnp.concatenate([own, other], axis=2), jnp.concatenate([other, own], axis=2)
        )
        return joined.astype(FULL).reshape(rows, dp_count * 2 * ff_half)

    own_down = finish(grad_down_part.reshape(dp_count, ff_half, width))
    other_down = hop(own_down, "blk", 1)
    grad_down = jnp.where(
        core == 0, jnp.concatenate([own_down, other_down]), jnp.concatenate([other_down, own_down])
    ).astype(FULL)
    grad_gate = join_columns(finish(grad_gate_part.reshape(dp_count, rows, dp_count * ff_half)))
    grad_up = join_columns(finish(grad_up_part.reshape(dp_count, rows, dp_count * ff_half)))

    halves = grad_out_part.reshape(2 * columns, 2, half_width)
    keep_half = jnp.where(core == 0, halves[:, 0], halves[:, 1])
    send_half = jnp.where(core == 0, halves[:, 1], halves[:, 0])
    got_rows = hop(send_half, "blk", 1)
    by_part = jnp.zeros((PARTS, columns, half_width), LOW)
    for distance, value in ((0, keep_half[:columns]), (2, keep_half[columns:]), (1, got_rows[:columns]), (3, got_rows[columns:])):
        by_part = lax.dynamic_update_index_in_dim(by_part, value, part ^ distance, 0)
    sums = jnp.stack([grad_gain_one, grad_bias_one, grad_gain_two, grad_bias_two])
    sums = sums.reshape(4, dp_count, rows).transpose(1, 0, 2).reshape(dp_count, 4 * rows)
    out_terms = jnp.concatenate([by_part.reshape(dp_count, rows, half_width), pad_extra(sums.astype(LOW))], axis=1)
    own_out = finish(out_terms)
    other_out = hop(own_out, "blk", 1)
    grad_output = jnp.where(
        core == 0,
        jnp.concatenate([own_out[:rows], other_out[:rows]], axis=1),
        jnp.concatenate([other_out[:rows], own_out[:rows]], axis=1),
    ).astype(FULL)
    vector_sums = own_out[rows : rows + extra_rows].astype(FULL) + other_out[rows : rows + extra_rows].astype(FULL)
    vector_sums = vector_sums.reshape(-1)[: 4 * rows].reshape(4, rows)

    own_qkv = scatter_rows(mm_tn(x_all, grad_qkv).astype(LOW).reshape(dp_count, rows, 3 * columns), dp)
    for bit in bits_between(PARTS, blk_count):
        own_qkv = own_qkv + hop(own_qkv.astype(LOW), "blk", bit).astype(FULL)
    own_qkv = own_qkv.astype(LOW)
    near_qkv = hop(own_qkv, "blk", 2)
    pair = jnp.stack([own_qkv, near_qkv])
    other_pair = hop(pair, "blk", 1)
    by_part = jnp.zeros((PARTS, rows, 3 * columns), LOW)
    for distance, value in ((0, own_qkv), (2, near_qkv), (1, other_pair[0]), (3, other_pair[1])):
        by_part = lax.dynamic_update_index_in_dim(by_part, value, part ^ distance, 0)
    grad_query, grad_key, grad_value = (
        jnp.concatenate([by_part[t, :, m * columns : (m + 1) * columns] for t in range(PARTS)], axis=1).astype(FULL)
        for m in range(3)
    )
    return (
        layer_out, grad_tokens, grad_query, grad_key, grad_value, grad_output, grad_gate, grad_up, grad_down,
        vector_sums[0], vector_sums[1], vector_sums[2], vector_sums[3],
    )


def solution(mesh):
    slots = P(None, "dp", "blk", None)
    matrix, vector = P("dp", None), P("dp")
    return jax.shard_map(
        shards,
        mesh=mesh,
        in_specs=(slots, P(None, "dp")) + (matrix,) * 7 + (vector,) * 4 + (slots,),
        out_specs=(slots, slots) + (matrix,) * 7 + (vector,) * 4,
        check_vma=False,
    )
```

```python
import functools

import jax
import jax.numpy as jnp
import numpy as np
from jax import lax
from jax.experimental import pallas as pl
from jax.experimental.pallas import tpu as pltpu
from jax.sharding import PartitionSpec as P

HEAD_DIM = 64
WIDE = 128
PARTS = 4
EXTRA = 16
LOW, FULL = jnp.bfloat16, jnp.float32
VMEM_BYTES = 60 * 1024 * 1024
VMEM = pl.BlockSpec(memory_space=pltpu.VMEM)
SMEM = pl.BlockSpec(memory_space=pltpu.SMEM)
ANY = pl.BlockSpec(memory_space=pl.ANY)
WHICH, CORE, PART, DP, STARTS = 0, 1, 2, 3, 4


def mm(left, right):
    return jnp.dot(left, right, preferred_element_type=FULL)


def mm_nt(left, right):
    return lax.dot_general(left, right, (((1,), (1,)), ((), ())), preferred_element_type=FULL)


def mm_tn(left, right):
    return lax.dot_general(left, right, (((0,), (0,)), ((), ())), preferred_element_type=FULL)


def hop(value, axis, bit):
    size = lax.axis_size(axis)
    return lax.ppermute(value, axis, [(at, at ^ bit) for at in range(size)])


def after(value, *others):
    return lax.optimization_barrier((value, *others))[0]


def bits_between(low, high):
    bits = []
    while low < high:
        bits.append(low)
        low *= 2
    return bits


def turn_table(seq_len):
    half = HEAD_DIM // 2
    frequency = np.float32(1000.0) ** (
        -(np.arange(half, dtype=np.float32) * np.float32(2.0) / np.float32(HEAD_DIM))
    )
    angles = np.arange(seq_len, dtype=np.float32)[:, None] * frequency[None, :]
    cosine = np.cos(angles).astype(np.float32)
    sine = np.sin(angles).astype(np.float32)
    return np.concatenate([cosine] * 4 + [sine, sine, -sine, -sine], axis=1)


def swap_matrix(heads, total, first, swapped):
    half = HEAD_DIM // 2
    out = np.zeros((total, heads * WIDE), np.float32)
    for h in range(heads):
        for f in range(HEAD_DIM):
            out[first + h * HEAD_DIM + f, h * WIDE + f] = 1.0
        for f in range(half if swapped else 0):
            out[first + h * HEAD_DIM + half + f, h * WIDE + HEAD_DIM + f] = -1.0
            out[first + h * HEAD_DIM + f, h * WIDE + HEAD_DIM + half + f] = 1.0
    return out


def call(body, outs, in_specs, scratch, flops, *operands, exps=0):
    return pl.pallas_call(
        body,
        out_shape=outs,
        in_specs=in_specs,
        out_specs=[VMEM] * len(outs),
        scratch_shapes=scratch,
        name=getattr(body, "func", body).__name__,
        compiler_params=pltpu.CompilerParams(vmem_limit_bytes=VMEM_BYTES),
        cost_estimate=pl.CostEstimate(flops=1000, bytes_accessed=1000, transcendentals=0),
    )(*operands)


def shape(dims, dtype=LOW):
    return jax.ShapeDtypeStruct(dims, dtype)


def norm_parts(rows):
    centred = rows - jnp.mean(rows, axis=-1, keepdims=True)
    scale = lax.rsqrt(jnp.mean(centred * centred, axis=-1, keepdims=True) + 1e-05)
    return centred * scale, scale


def norm_back(upstream, gain, unit, scale):
    inner = upstream * gain
    centre = jnp.mean(inner, axis=-1, keepdims=True)
    along = jnp.mean(inner * unit, axis=-1, keepdims=True)
    sums = (jnp.sum(upstream * unit, axis=0, keepdims=True), jnp.sum(upstream, axis=0, keepdims=True))
    return (inner - centre - unit * along) * scale, sums


def pack_first_kernel(
    meta, tokens, cot, w_q, w_k, w_v, w_o, w_down, gain_one, bias_one, gain_two, bias_two, tok_out, cot_out, qkv_out, down_out
):
    rows, columns = w_q.shape[0], qkv_out.shape[1] // 3
    half, third = rows // 2, rows // 6
    other = 1 - meta[0, WHICH]
    tok_out[...] = tokens[other, 0]
    cot_out[...] = cot[other, 0]
    for part in range(PARTS):

        @pl.when(meta[0, PART] == part)
        def _(part=part):
            for at, w in enumerate((w_q, w_k, w_v)):
                qkv_out[:rows, at * columns : (at + 1) * columns] = w[:, part * columns : (part + 1) * columns]

    qkv_out[rows : rows + EXTRA, :] = jnp.zeros((EXTRA, 3 * columns), LOW)
    for at, vector in enumerate((gain_one, bias_one, gain_two, bias_two)):
        qkv_out[rows + at : rows + at + 1, :rows] = vector[...]
    for part in range(PARTS):
        low = pl.multiple_of(part * rows + meta[0, CORE] * half, half)
        down_out[part] = w_down[pl.ds(low, half), :]
    out_rows = w_o[pl.ds(pl.multiple_of(meta[0, CORE] * half, half), half), :]
    at = rows + EXTRA
    qkv_out[at : at + half, :] = out_rows[:, : 3 * columns]
    at += half
    for g in range(3):
        qkv_out[at : at + third, g * columns : (g + 1) * columns] = out_rows[g * third : (g + 1) * third, 3 * columns :]


def pack_second_kernel(meta, w_gate, w_up, out):
    half, width = out.shape[1], out.shape[2]
    step = 2 * half
    low = pl.multiple_of(meta[0, CORE] * half, half)
    for base, w in ((0, w_gate), (PARTS, w_up)):
        for part in range(PARTS):
            for block in range(width // step):
                start = (block * PARTS + part) * step
                out[base + part, :, block * step : (block + 1) * step] = w[pl.ds(low, half), start : start + step]


def project_kernel(heads, pieces, meta, table_ref, swap_q, swap_k, spread_v, *refs):
    x_refs, w_refs, (q_ref, k_ref, v_ref) = refs[:PARTS], refs[PARTS : PARTS + pieces], refs[PARTS + pieces : -2]
    w_all, turn = refs[-2:]
    rows = w_all.shape[0] // pieces
    block = x_refs[0].shape[0]
    local = block // 2
    for distance, w in enumerate(w_refs):
        w_all[pl.ds(pl.multiple_of((meta[0, DP] ^ distance) * rows, rows), rows), :] = w[:rows, :]
    for at in range(2 * PARTS):
        start = pl.multiple_of(meta[0, STARTS + at], local)
        turn[at * local : (at + 1) * local, :] = table_ref[pl.ds(start, local), :]
    weights = w_all[...]
    w_q, w_k, w_v = (mm(weights, m[...]).astype(LOW) for m in (swap_q, swap_k, spread_v))
    for r in range(PARTS):
        out_rows = slice(r * block, (r + 1) * block)
        x = x_refs[r][...]
        cosine, sine = turn[out_rows, :WIDE], turn[out_rows, WIDE:]
        for out_ref, w, scale in ((q_ref, w_q, 0.0625), (k_ref, w_k, None)):
            made = mm(x, w)
            for h in range(heads):
                one = made[:, h * WIDE : (h + 1) * WIDE]
                turned = (one * cosine + pltpu.roll(one, HEAD_DIM, 1) * sine).astype(LOW)
                out_ref[h, out_rows, :] = turned if scale is None else turned * jnp.asarray(scale, LOW)
        made = mm(x, w_v).astype(LOW)
        for h in range(heads):
            v_ref[h, out_rows, :] = made[:, h * WIDE : (h + 1) * WIDE]


def fill_bias(meta, length, bias_ref, local):
    for at in range(bias_ref.shape[0] // local):
        place = meta[0, STARTS + at] + lax.broadcasted_iota(jnp.int32, (local, WIDE), 0)
        bias_ref[at * local : (at + 1) * local, :] = jnp.where(place < length, 0.0, -1e30)


def each_block(count, step):
    if count <= 4:
        for number in range(count):
            step(number)
    else:
        lax.fori_loop(0, count, lambda number, carry: step(number) or carry, 0)


def block_rows(number, block):
    if isinstance(number, int):
        return slice(number * block, (number + 1) * block)
    return pl.ds(pl.multiple_of(number * block, block), block)


def attend_kernel(heads, block, meta, lengths, q_ref, k_ref, v_ref, spread_ref, *refs):
    outs, (lse_ref, wide_ref) = refs[:PARTS], refs[PARTS:]
    row_count, key_count = q_ref.shape[1], k_ref.shape[1]
    span = row_count // PARTS
    local = span // 2
    length = lengths[meta[0, WHICH], 0]
    places = [meta[0, STARTS + at] + lax.broadcasted_iota(jnp.int32, (1, local), 1) for at in range(key_count // local)]
    bias = jnp.where(jnp.concatenate(places, axis=1) < length, 0.0, -1e30)
    for h in range(heads):

        def step(number, h=h):
            rows = block_rows(number, block)
            scores = mm_nt(q_ref[h, rows, :], k_ref[h]) + bias
            top = jnp.max(scores, axis=1, keepdims=True)
            weights = jnp.exp(scores - top)
            total = jnp.sum(weights, axis=1, keepdims=True)
            wide_ref[rows, h * WIDE : (h + 1) * WIDE] = (mm(weights.astype(LOW), v_ref[h]) / total).astype(LOW)
            lse_ref[h, :, rows] = jnp.broadcast_to(top + jnp.log(total), (block, WIDE)).T[:1, :]

        each_block(row_count // block, step)
    for r in range(PARTS):
        outs[r][...] = mm_nt(wide_ref[r * span : (r + 1) * span, :], spread_ref[...]).astype(LOW)


def attend_back_kernel(heads, block, meta, lengths, q_ref, k_ref, v_ref, table_ref, spread_ref, lse_ref, w_o, *refs):
    grads_in, att_in = refs[:PARTS], refs[PARTS : 2 * PARTS]
    dq_ref, dk_ref, dv_ref, dw_ref, bias_ref, turn, grad_wide, dk_sum, dv_sum = refs[2 * PARTS :]
    row_count, key_count = q_ref.shape[1], k_ref.shape[1]
    span = row_count // PARTS
    local = span // 2
    columns = w_o.shape[0]
    fill_bias(meta, lengths[meta[0, WHICH], 0], bias_ref, local)
    for at in range(key_count // local):
        start = pl.multiple_of(meta[0, STARTS + at], local)
        turn[at * local : (at + 1) * local, :] = table_ref[pl.ds(start, local), :]
    weights = mm_tn(spread_ref[...], w_o[...]).astype(LOW)
    dw = jnp.zeros((columns, w_o.shape[1]), FULL)
    for r in range(PARTS):
        grads = grads_in[r][...]
        grad_wide[r * span : (r + 1) * span, :] = mm_nt(grads, weights).astype(LOW)
        dw = dw + mm_tn(att_in[r][...], grads)
    dw_ref[...] = jnp.zeros_like(dw_ref)
    dw_ref[pl.ds(pl.multiple_of(meta[0, PART] * columns, columns), columns), :] = dw.astype(LOW)

    def unturn(value, rows):
        cosine, sine = turn[rows, :WIDE], turn[rows, WIDE:]
        return (value * cosine - pltpu.roll(value, HEAD_DIM, 1) * sine).astype(LOW)

    for h in range(heads):
        lanes = slice(h * WIDE, (h + 1) * WIDE)
        keys, values = k_ref[h], v_ref[h]
        keys_t = keys.T
        dk_sum[...] = jnp.zeros_like(dk_sum)
        dv_sum[...] = jnp.zeros_like(dv_sum)

        def step(number, h=h, lanes=lanes, keys=keys, values=values, keys_t=keys_t):
            rows = block_rows(number, block)
            bias = jnp.concatenate([bias_ref[...]] * (block // WIDE), axis=1)
            queries, grads = q_ref[h, rows, :], grad_wide[rows, lanes]
            probs = jnp.exp(mm_nt(keys, queries) + bias - lse_ref[h, :, rows])
            grad_probs = mm_nt(values, grads)
            delta = jnp.sum(probs * grad_probs, axis=0, keepdims=True)
            grad_scores = (probs * (grad_probs - delta)).astype(LOW)
            dv_sum[...] += mm(probs.astype(LOW), grads)
            dk_sum[...] += mm(grad_scores, queries)
            dq_ref[rows, lanes] = unturn(mm(keys_t, grad_scores).T * 0.125, rows)

        each_block(row_count // block, step)
        dk_ref[:, lanes] = unturn(dk_sum[...] * 2.0, slice(None))
        dv_ref[:, lanes] = dv_sum[...].astype(LOW)


def place_gate_up(meta, refs, block, target, sems, at):
    half = refs[0].shape[2]
    copies = []
    for side, ref in enumerate(refs):
        low = pl.multiple_of((meta[0, CORE] ^ side) * half, half)
        copy = pltpu.make_async_copy(ref.at[:, block], target.at[:, pl.ds(low, half), :], sems.at[at + side])
        copy.start()
        copies.append(copy)
    return copies, at + 2


def place_down(meta, own, refs, block, target, sems, at):
    rows, half = 2 * refs[0].shape[1], refs[0].shape[1]
    count = target.shape[0]
    low = pl.multiple_of(block * rows, rows)
    copies = [pltpu.make_async_copy(own.at[pl.ds(low, rows), :], target.at[meta[0, DP]], sems.at[at])]
    for number, ref in enumerate(refs):
        distance, side = (number + 1, 0) if number < count - 1 else (number - count + 2, 1)
        low = pl.multiple_of((meta[0, CORE] ^ side) * half, half)
        to = target.at[meta[0, DP] ^ distance, pl.ds(low, half), :]
        copies.append(pltpu.make_async_copy(ref.at[block], to, sems.at[at + 1 + number]))
    for copy in copies:
        copy.start()
    return copies, at + len(copies)


def wait_all(copies):
    for copy in copies:
        copy.wait()


def residual_kernel(pieces, meta, x_ref, w_own, *refs):
    att, w_refs, refs = refs[:PARTS], refs[PARTS : PARTS + 2 * pieces - 1], refs[PARTS + 2 * pieces - 1 :]
    residual_out, low_out, vector_out, w_out, w_o, gathered = refs
    columns, rows = att[0].shape[1], w_own.shape[0]
    half, third = rows // 2, rows // 6
    w_o[pl.ds(pl.multiple_of(meta[0, DP] * rows, rows), rows), :] = w_own[...]
    for number, ref in enumerate(w_refs):
        distance, side = (number, 0) if number < pieces else (number - pieces + 1, 1)
        if side == 0:
            gathered[meta[0, DP] ^ distance] = ref[rows : rows + EXTRA, :]
        if distance:
            low = (meta[0, DP] ^ distance) * rows + (meta[0, CORE] ^ side) * half
            at = rows + EXTRA
            w_o[pl.ds(pl.multiple_of(low, half), half), : 3 * columns] = ref[at : at + half, :]
            at += half
            for g in range(3):
                w_o[pl.ds(pl.multiple_of(low + g * third, third), third), 3 * columns :] = ref[
                    at : at + third, g * columns : (g + 1) * columns
                ]
    vectors = jnp.concatenate([gathered[d][:8, :rows] for d in range(pieces)], axis=1).astype(FULL)
    vector_out[...] = vectors
    residual = x_ref[...].astype(FULL)
    for r in range(PARTS):
        low = pl.multiple_of((meta[0, PART] ^ r) * columns, columns)
        residual = residual + mm(att[r][...], w_o[pl.ds(low, columns), :])
    w_out[...] = w_o[pl.ds(pl.multiple_of(meta[0, PART] * columns, columns), columns), :]
    residual_out[...] = residual
    unit, _ = norm_parts(residual)
    low_out[...] = (unit * vectors[0:1] + vectors[1:2]).astype(LOW)


def feed_kernel(meta, lengths, residual_ref, vectors, cot_ref, cot_got, *refs):
    gu_refs, down_own, refs = refs[:2], refs[2], refs[3:]
    down_refs, refs = refs[:-10], refs[-10:]
    grad_ffn_out, grad_branch_out, grad_one_out, own_out, back_out, sums_out, held, gates, ups, sems = refs
    width = residual_ref.shape[1]
    copies, at = [], 0
    for part in range(PARTS):
        gate, at = place_gate_up(meta, gu_refs, part, held.at[part], sems, at)
        up, at = place_gate_up(meta, gu_refs, PARTS + part, held.at[PARTS + part], sems, at)
        down, at = place_down(meta, down_own, down_refs, part, held.at[2 * PARTS + part], sems, at)
        copies.append(gate + up + down)

    def weights(number):
        return held[number].reshape(width, width)

    which = meta[0, WHICH]
    local = cot_got.shape[0]
    unit_one, scale_one = norm_parts(residual_ref[...])
    normed = unit_one * vectors[0:1] + vectors[1:2]
    normed_low = normed.astype(LOW)
    residual = normed
    for part in range(PARTS):
        wait_all(copies[part])
        gate = mm(normed_low, weights(part))
        up = mm(normed_low, weights(PARTS + part))
        sigma = 1.0 / (1.0 + jnp.exp(-gate))
        silu = gate * sigma
        residual = residual + mm((silu * up).astype(LOW), weights(2 * PARTS + part))
        gates[part] = up * (sigma + silu * (1.0 - sigma))
        ups[part] = silu
    unit_two, scale_two = norm_parts(residual)
    layer = unit_two * vectors[2:3] + vectors[3:4]
    length = lengths[which, 0]
    upstream = []
    for half, (out, cot) in enumerate(((own_out, cot_ref[which, 0]), (back_out, cot_got[...]))):
        place = meta[0, STARTS + half] + lax.broadcasted_iota(jnp.int32, (local, 1), 0)
        valid = place < length
        out[...] = jnp.where(valid, layer[half * local : (half + 1) * local], 0.0).astype(LOW)
        upstream.append(jnp.where(valid, cot.astype(FULL), 0.0))
    grad_two, sums_two = norm_back(jnp.concatenate(upstream, axis=0), vectors[2:3], unit_two, scale_two)
    grad_ffn = grad_two.astype(LOW)
    grad_ffn_out[...] = grad_ffn
    grad_normed = grad_two
    for part in range(PARTS):
        grad_hidden = mm_nt(grad_ffn, weights(2 * PARTS + part))
        grad_normed = (
            grad_normed
            + mm_nt((grad_hidden * gates[part]).astype(LOW), weights(part))
            + mm_nt((grad_hidden * ups[part]).astype(LOW), weights(PARTS + part))
        )
    grad_one, sums_one = norm_back(grad_normed, vectors[0:1], unit_one, scale_one)
    grad_one_out[...] = grad_one
    grad_branch_out[...] = grad_one.astype(LOW)
    sums_out[...] = jnp.concatenate([*sums_one, *sums_two, jnp.zeros((4, grad_one.shape[1]), FULL)], axis=0)


def hidden_kernel(meta, *refs):
    x_refs, gu_refs, refs = refs[:PARTS], refs[PARTS : PARTS + 2], refs[PARTS + 2 :]
    hidden_out, gate_out, up_out, held_gate, held_up, sems = refs
    part, width = meta[0, PART], hidden_out.shape[1]
    first, at = place_gate_up(meta, gu_refs, part, held_gate, sems, 0)
    second, at = place_gate_up(meta, gu_refs, PARTS + part, held_up, sems, at)
    wait_all(first + second)
    w_gate, w_up = held_gate[...].reshape(width, width), held_up[...].reshape(width, width)
    block = x_refs[0].shape[0]
    for r in range(PARTS):
        rows = slice(r * block, (r + 1) * block)
        x = x_refs[r][...]
        gate, up = mm(x, w_gate), mm(x, w_up)
        sigma = 1.0 / (1.0 + jnp.exp(-gate))
        silu = gate * sigma
        hidden_out[rows, :] = (silu * up).astype(LOW)
        gate_out[rows, :] = (up * (sigma + silu * (1.0 - sigma))).astype(LOW)
        up_out[rows, :] = silu.astype(LOW)


def split_terms(meta, terms, outs, at=None):
    rows = terms.shape[0] // len(outs)
    for distance, out in enumerate(outs):
        low = pl.multiple_of((meta[0, DP] ^ distance) * rows, rows)
        if at is None:
            out[:rows, :] = terms[pl.ds(low, rows), :]
        else:
            out[at] = terms[pl.ds(low, rows), :]


def down_kernel(meta, hidden_ref, *refs):
    grads, (out,) = refs[:PARTS], refs[PARTS:]
    block = grads[0].shape[0]
    total = mm_tn(hidden_ref[:block, :], grads[0][...])
    for r in range(1, PARTS):
        total = total + mm_tn(hidden_ref[r * block : (r + 1) * block, :], grads[r][...])
    out[...] = total.astype(LOW)


def gate_up_kernel(meta, gate_ref, up_ref, *refs):
    grads, x_refs, down_own, refs = refs[:PARTS], refs[PARTS : 2 * PARTS], refs[2 * PARTS], refs[2 * PARTS + 1 :]
    held, gate_low, up_low, terms, sems = refs[-5:]
    count = held.shape[0]
    down_refs, outs = refs[: 2 * count - 2], refs[2 * count - 2 : -5]
    copies, _ = place_down(meta, down_own, down_refs, meta[0, PART], held, sems, 0)
    wait_all(copies)
    w_down = held[...].reshape(terms.shape)
    block = grads[0].shape[0]
    for r in range(PARTS):
        rows = slice(r * block, (r + 1) * block)
        grad_hidden = mm_nt(grads[r][...], w_down)
        gate_low[rows, :] = (grad_hidden * gate_ref[rows, :].astype(FULL)).astype(LOW)
        up_low[rows, :] = (grad_hidden * up_ref[rows, :].astype(FULL)).astype(LOW)
    for at, source in enumerate((gate_low, up_low)):
        total = mm_tn(x_refs[0][...], source[:block, :])
        for r in range(1, PARTS):
            total = total + mm_tn(x_refs[r][...], source[r * block : (r + 1) * block, :])
        terms[...] = total.astype(LOW)
        split_terms(meta, terms, outs, at)


def projections_back_kernel(pieces, meta, dq, dk, dv, swap_q, swap_k, spread_v, sums, *refs):
    x_refs, w_refs, refs = refs[:PARTS], refs[PARTS : PARTS + pieces], refs[PARTS + pieces :]
    outs, (near_out, far_out, w_all, terms) = refs[:pieces], refs[pieces:]
    rows = w_all.shape[0] // pieces
    for distance, w in enumerate(w_refs):
        w_all[pl.ds(pl.multiple_of((meta[0, DP] ^ distance) * rows, rows), rows), :] = w[:rows, :]
    block = x_refs[0].shape[0]
    weights = w_all[...]
    total = jnp.zeros(weights.shape, FULL)
    for r in range(PARTS):
        span = slice(r * block, (r + 1) * block)
        low = sum(mm_nt(g[span, :], m[...]) for g, m in ((dq, swap_q), (dk, swap_k), (dv, spread_v))).astype(LOW)
        total = total + mm_tn(x_refs[r][...], low)
        onward = mm_nt(low, weights)
        if r % 2 == 0:
            near_out[r // 2] = onward
        else:
            far_out[r // 2] = onward.astype(LOW)
    terms[...] = total.astype(LOW)
    split_terms(meta, terms, outs)
    for distance, out in enumerate(outs):
        out[rows:, :] = jnp.zeros((EXTRA, weights.shape[1]), LOW)
        for block_at in range(pieces):

            @pl.when(meta[0, DP] ^ distance == block_at)
            def _(out=out, block_at=block_at):
                out[rows : rows + 8, :rows] = sums[:, block_at * rows : (block_at + 1) * rows].astype(LOW)


def join_rows_kernel(meta, *refs):
    out = refs[-1]
    rows = refs[0].shape[0]
    for r in range(PARTS):
        low = pl.multiple_of((meta[0, PART] ^ r) * rows, rows)
        out[pl.ds(low, rows), :] = refs[r][...].astype(FULL)


def join_columns_kernel(meta, *refs):
    outs, held = refs[PARTS:-1], refs[-1]
    step = outs[0].shape[0]
    for r in range(PARTS):
        held[meta[0, PART] ^ r] = refs[r][...]
    for at, out in enumerate(outs):
        for part in range(PARTS):
            value = held[part, at].astype(FULL)
            for block in range(value.shape[1] // step):
                start = (block * PARTS + part) * step
                out[:, start : start + step] = value[:, block * step : (block + 1) * step]


def join_projections_kernel(meta, *refs):
    (q_out, k_out, v_out, sums_out), held = refs[PARTS:-1], refs[-1]
    rows, columns = q_out.shape[0], refs[0].shape[1] // 3
    for r in range(PARTS):
        held[meta[0, PART] ^ r] = refs[r][...]
    sums = jnp.zeros((8, rows), FULL)
    for part in range(PARTS):
        value = held[part].astype(FULL)
        for at, out in enumerate((q_out, k_out, v_out)):
            out[:, part * columns : (part + 1) * columns] = value[:rows, at * columns : (at + 1) * columns]
        sums = sums + value[rows : rows + 8, :rows]
    sums_out[...] = sums


def gather_pieces(own, bits, starts=None, gate=None):
    held = {0: own}
    for bit in bits:
        for distance in list(held):
            source = held[distance]
            if distance == 0 and starts is not None:
                source = after(source, starts[bit])
            elif distance != 0 and gate is not None:
                source = after(source, gate)
            held[distance | bit] = hop(source, "dp", bit)
    return [held[distance] for distance in range(len(held))]


def scatter_sum(chunks):
    total = chunks[0].astype(FULL)
    for distance in range(1, len(chunks)):
        total = total + hop(chunks[distance], "dp", distance).astype(FULL)
    return total


def group_pieces(own, gate=None, far_gate=None):
    core, near = hop(own, "blk", 1), hop(own if gate is None else after(own, gate), "blk", 2)
    return [own, core, near, hop(near if far_gate is None else after(near, far_gate), "blk", 1)]


def shards(
    tokens, lengths, w_query, w_key, w_value, w_output, w_gate, w_up, w_down,
    first_gain, first_bias, second_gain, second_bias, cotangent,
):
    _, _, local, width = tokens.shape
    dp_count, blk_count = lax.axis_size("dp"), lax.axis_size("blk")
    dp, blk = lax.axis_index("dp"), lax.axis_index("blk")
    side = blk_count // 2
    which = blk // side
    first = which == 0
    core, part = blk % 2, blk % PARTS
    heads = width // HEAD_DIM // PARTS
    columns = heads * HEAD_DIM
    rows, ff_rows = w_query.shape[0], w_down.shape[0]
    half, ff = rows // 2, w_gate.shape[1]
    block = 2 * local
    row_count = PARTS * block
    spread_bits = bits_between(PARTS, side)
    sum_bits = bits_between(PARTS, blk_count)
    dp_bits = bits_between(1, dp_count)
    back_bits = dp_bits[::-1]
    table = jnp.asarray(turn_table(local * blk_count))
    swap_q, swap_k, spread_v = (
        jnp.asarray(swap_matrix(heads, 3 * columns, at * columns, at < 2), LOW) for at in range(3)
    )
    only_q, only_k = (jnp.asarray(swap_matrix(heads, 3 * columns, at * columns, False), LOW) for at in range(2))
    spread = jnp.asarray(swap_matrix(heads, columns, 0, False), LOW)

    starts = [(blk ^ distance ^ away) * local for distance in range(side) for away in (0, side)]
    meta = jnp.stack([which, core, part, dp, *starts]).astype(jnp.int32).reshape(1, -1)

    gate_up_own = call(
        pack_second_kernel, [shape((2 * PARTS, half, width))], [SMEM] + [VMEM] * 2, [], 0, meta, w_gate, w_up
    )[0]
    gate_up_core = lax.all_gather(gate_up_own, "dp", axis=0, tiled=False)
    tok_send, cot_send, qkv_own, down_own = call(
        pack_first_kernel,
        [shape((local, width)), shape((local, width)), shape((rows + EXTRA + half + half // 3, 3 * columns))]
        + [shape((PARTS, half, width))],
        [SMEM] + [VMEM] * 11, [], 0, after(meta, gate_up_own), tokens, cotangent, w_query, w_key, w_value, w_output, w_down,
        *(vector.reshape(1, -1) for vector in (first_gain, first_bias, second_gain, second_bias)),
    )
    tok_got = hop(tok_send, "blk", side)
    qkv = gather_pieces(qkv_own, dp_bits)
    x_own = after(jnp.concatenate([jnp.where(first, tokens[0, 0], tokens[1, 0]), tok_got]), *qkv[1:-1])
    x_all = group_pieces(x_own, far_gate=qkv[-1])

    wide_shape = shape((heads, row_count, WIDE))
    queries, keys, values = call(
        functools.partial(project_kernel, heads, dp_count), [wide_shape] * 3,
        [SMEM] + [VMEM] * (4 + PARTS + dp_count),
        [pltpu.VMEM((width, 3 * columns), LOW), pltpu.VMEM((row_count, 2 * WIDE), FULL)],
        2 * row_count * width * 3 * heads * WIDE, meta, table, swap_q, swap_k, spread_v, *x_all, *qkv,
    )
    for bit in spread_bits:
        keys = jnp.concatenate([keys, hop(keys, "blk", bit)], axis=1)
        values = jnp.concatenate([values, hop(values, "blk", bit)], axis=1)
    key_count = keys.shape[1]
    q_block = max(WIDE, min(row_count, 512 * 1024 // key_count))
    *attended, lse = call(
        functools.partial(attend_kernel, heads, q_block),
        [shape((block, columns))] * PARTS + [shape((heads, 1, row_count), FULL)],
        [SMEM] * 2 + [VMEM] * 4,
        [pltpu.VMEM((row_count, heads * WIDE), LOW)],
        4 * heads * row_count * key_count * WIDE, meta, lengths, queries, keys, values, spread,
        exps=heads * row_count * key_count,
    )
    qkv_core = [hop(after(piece, queries), "blk", 1) for piece in qkv[1:]]
    down_pieces = gather_pieces(down_own, back_bits, starts={bit: x_own for bit in dp_bits}, gate=lse)[1:]
    cot_got = hop(after(cot_send, x_own), "blk", side)
    att_here = [attended[0]] + [hop(after(attended[r], *down_pieces[:2]), "blk", r) for r in range(1, PARTS)]
    residual_one, normed_low, all_vectors, w_o = call(
        functools.partial(residual_kernel, dp_count),
        [shape((block, width), FULL), shape((block, width)), shape((8, width), FULL), shape((columns, width))],
        [SMEM] + [VMEM] * (2 + PARTS + 2 * dp_count - 1),
        [pltpu.VMEM((width, width), LOW), pltpu.VMEM((dp_count, EXTRA, 3 * columns), LOW)],
        2 * block * width * width, after(meta, cot_got), x_own, w_output, *att_here, *qkv, *qkv_core,
    )
    normed_all = group_pieces(normed_low)
    gate_up_all = (gate_up_core, hop(after(gate_up_core, normed_low), "blk", 1))
    down_all = (w_down, *down_pieces, *(hop(after(piece, normed_low), "blk", 1) for piece in down_pieces))

    part_shape, w_shape = (PARTS, block, width), (dp_count, rows, width)
    grad_ffn, grad_branch, grad_one, layer_own, layer_back, sums = call(
        feed_kernel,
        [shape((block, width))] * 2 + [shape((block, width), FULL)] + [shape((local, width))] * 2
        + [shape((8, width), FULL)],
        [SMEM] * 2 + [VMEM] * 4 + [ANY] * (2 + len(down_all)),
        [
            pltpu.VMEM((3 * PARTS, *w_shape), LOW),
            pltpu.VMEM(part_shape, FULL),
            pltpu.VMEM(part_shape, FULL),
            pltpu.SemaphoreType.DMA((PARTS * (4 + len(down_all)),)),
        ],
        12 * block * width * ff, after(meta, normed_all[3]), lengths, residual_one, all_vectors, cotangent, cot_got,
        *gate_up_all, *down_all,
    )
    layer_got = hop(layer_back, "blk", side)

    long = shape((row_count, width))
    hidden, gate_factor, up_factor = call(
        hidden_kernel, [long] * 3,
        [SMEM] + [VMEM] * PARTS + [ANY] * 2,
        [pltpu.VMEM(w_shape, LOW), pltpu.VMEM(w_shape, LOW), pltpu.SemaphoreType.DMA((4,))],
        4 * row_count * width * width, after(meta, grad_ffn), *normed_all, *gate_up_all,
    )
    ffn_all = group_pieces(grad_ffn, far_gate=hidden)
    branch_near = hop(after(grad_branch, ffn_all[2]), "blk", 2)
    down_terms = call(
        down_kernel, [shape((width, width))], [SMEM] + [VMEM] * (1 + PARTS), [],
        2 * row_count * width * width, meta, hidden, *ffn_all,
    )[0]
    down_sum = lax.psum_scatter(
        down_terms.reshape(dp_count, rows, width), "dp", scatter_dimension=0, tiled=False
    ).astype(FULL)
    branch_all = [grad_branch, hop(grad_branch, "blk", 1), branch_near, hop(after(branch_near, down_terms), "blk", 1)]
    gate_up_terms = call(
        gate_up_kernel, [shape((2, rows, width))] * dp_count,
        [SMEM] + [VMEM] * (2 + 2 * PARTS) + [ANY] * len(down_all),
        [pltpu.VMEM(w_shape, LOW), pltpu.VMEM((row_count, width), LOW), pltpu.VMEM((row_count, width), LOW)]
        + [pltpu.VMEM((width, width), LOW), pltpu.SemaphoreType.DMA((len(down_all),))],
        6 * row_count * width * width, after(meta, down_terms), gate_factor, up_factor, *ffn_all, *normed_all, *down_all,
    )

    wide_rows, wide_keys = shape((row_count, heads * WIDE)), shape((key_count, heads * WIDE))
    grad_q, grad_k, grad_v, out_terms = call(
        functools.partial(attend_back_kernel, heads, q_block),
        [wide_rows, wide_keys, wide_keys, shape((width, width))],
        [SMEM] * 2 + [VMEM] * (7 + 2 * PARTS),
        [
            pltpu.VMEM((key_count, WIDE), FULL),
            pltpu.VMEM((key_count, 2 * WIDE), FULL),
            pltpu.VMEM((row_count, heads * WIDE), LOW),
            pltpu.VMEM((key_count, WIDE), FULL),
            pltpu.VMEM((key_count, WIDE), FULL),
        ],
        10 * heads * row_count * key_count * WIDE, after(meta, gate_up_terms[0], layer_got), lengths, queries, keys, values, table,
        spread, lse, w_o,
        *branch_all, *attended, exps=heads * row_count * key_count,
    )
    for bit in reversed(spread_bits):
        middle = grad_k.shape[0] // 2
        grad_k, grad_v = (
            (value[:middle].astype(FULL) + hop(value[middle:], "blk", bit).astype(FULL)).astype(LOW)
            for value in (grad_k, grad_v)
        )
    *qkv_terms, token_keep, token_send = call(
        functools.partial(projections_back_kernel, dp_count),
        [shape((rows + EXTRA, 3 * columns))] * dp_count
        + [shape((2, block, width), FULL), shape((2, block, width))],
        [SMEM] + [VMEM] * (7 + PARTS + dp_count),
        [pltpu.VMEM((width, 3 * columns), LOW), pltpu.VMEM((width, 3 * columns), LOW)],
        4 * row_count * width * 3 * columns, after(meta, down_sum), grad_q, grad_k, grad_v, only_q, only_k, spread_v, sums,
        *x_all, *qkv,
    )

    token_got = hop(token_send, "blk", 1).astype(FULL)
    near_send = (token_keep[1] + token_got[1]).astype(LOW)
    grad_rows = grad_one + token_keep[0] + token_got[0] + hop(near_send, "blk", 2).astype(FULL)
    rows_got = hop(grad_rows[local:].astype(LOW), "blk", side).astype(FULL)
    grad_tokens = jnp.where(
        first, jnp.stack([grad_rows[:local], rows_got]), jnp.stack([rows_got, grad_rows[:local]])
    )[:, None]

    layer_out = jnp.where(first, jnp.stack([layer_own, layer_got]), jnp.stack([layer_got, layer_own]))[:, None]

    def finish(total):
        for bit in sum_bits:
            total = total + hop(total.astype(LOW), "blk", bit).astype(FULL)
        return group_pieces(total.astype(LOW))

    grad_down = call(
        join_rows_kernel, [shape((ff_rows, width), FULL)], [SMEM] + [VMEM] * PARTS, [], 0,
        meta, *finish(down_sum),
    )[0]
    grad_gate, grad_up = call(
        join_columns_kernel, [shape((rows, ff), FULL)] * 2, [SMEM] + [VMEM] * PARTS,
        [pltpu.VMEM((PARTS, 2, rows, width), LOW)], 0, meta, *finish(scatter_sum(gate_up_terms)),
    )
    grad_query, grad_key, grad_value, vector_sums = call(
        join_projections_kernel, [shape((rows, width), FULL)] * 3 + [shape((8, rows), FULL)],
        [SMEM] + [VMEM] * PARTS, [pltpu.VMEM((PARTS, rows + EXTRA, 3 * columns), LOW)], 0,
        meta, *finish(scatter_sum(qkv_terms)),
    )

    def holder_hop(value, bit, spread_over):
        pairs = []
        for d in range(dp_count):
            owner = d * PARTS // dp_count
            for b in range(blk_count):
                if (b ^ owner) % PARTS in spread_over:
                    pairs.append((d * blk_count + b, d * blk_count + (b ^ bit)))
        return lax.ppermute(value, ("dp", "blk"), pairs)

    out_sum = lax.psum_scatter(
        after(out_terms, down_sum).reshape(dp_count, rows, width), "dp", scatter_dimension=0, tiled=False
    )
    for bit in sum_bits:
        out_sum = (out_sum.astype(FULL) + holder_hop(out_sum, bit, (0,)).astype(FULL)).astype(LOW)
    out_sum = out_sum + holder_hop(out_sum, 2, (0,))
    grad_output = (out_sum + holder_hop(out_sum, 1, (0, 2))).astype(FULL)
    return (
        layer_out, grad_tokens, grad_query, grad_key, grad_value, grad_output, grad_gate, grad_up, grad_down,
        vector_sums[0], vector_sums[1], vector_sums[2], vector_sums[3],
    )


def solution(mesh):
    slots = P(None, "dp", "blk", None)
    matrix, vector = P("dp", None), P("dp")
    return jax.shard_map(
        shards,
        mesh=mesh,
        in_specs=(slots, P(None, "dp")) + (matrix,) * 7 + (vector,) * 4 + (slots,),
        out_specs=(slots, slots) + (matrix,) * 7 + (vector,) * 4,
        check_vma=False,
    )
```

```python
import functools

import jax
import jax.numpy as jnp
import numpy as np
from jax import lax
from jax.experimental import pallas as pl
from jax.experimental.pallas import tpu as pltpu
from jax.sharding import PartitionSpec as P

HEAD_DIM = 64
WIDE = 128
PARTS = 4
EXTRA = 16
LOW, FULL = jnp.bfloat16, jnp.float32
VMEM_BYTES = 60 * 1024 * 1024
VMEM = pl.BlockSpec(memory_space=pltpu.VMEM)
SMEM = pl.BlockSpec(memory_space=pltpu.SMEM)
ANY = pl.BlockSpec(memory_space=pl.ANY)
WHICH, CORE, PART, DP, STARTS = 0, 1, 2, 3, 4


def mm(left, right):
    return jnp.dot(left, right, preferred_element_type=FULL)


def mm_nt(left, right):
    return lax.dot_general(left, right, (((1,), (1,)), ((), ())), preferred_element_type=FULL)


def mm_tn(left, right):
    return lax.dot_general(left, right, (((0,), (0,)), ((), ())), preferred_element_type=FULL)


def hop(value, axis, bit):
    size = lax.axis_size(axis)
    return lax.ppermute(value, axis, [(at, at ^ bit) for at in range(size)])


def after(value, *others):
    return lax.optimization_barrier((value, *others))[0]


def bits_between(low, high):
    bits = []
    while low < high:
        bits.append(low)
        low *= 2
    return bits


def turn_table(seq_len):
    half = HEAD_DIM // 2
    frequency = np.float32(1000.0) ** (
        -(np.arange(half, dtype=np.float32) * np.float32(2.0) / np.float32(HEAD_DIM))
    )
    angles = np.arange(seq_len, dtype=np.float32)[:, None] * frequency[None, :]
    cosine = np.cos(angles).astype(np.float32)
    sine = np.sin(angles).astype(np.float32)
    return np.concatenate([cosine] * 4 + [sine, sine, -sine, -sine], axis=1)


def swap_matrix(heads, total, first, swapped):
    half = HEAD_DIM // 2
    out = np.zeros((total, heads * WIDE), np.float32)
    for h in range(heads):
        for f in range(HEAD_DIM):
            out[first + h * HEAD_DIM + f, h * WIDE + f] = 1.0
        for f in range(half if swapped else 0):
            out[first + h * HEAD_DIM + half + f, h * WIDE + HEAD_DIM + f] = -1.0
            out[first + h * HEAD_DIM + f, h * WIDE + HEAD_DIM + half + f] = 1.0
    return out


def call(body, outs, in_specs, scratch, *operands):
    return pl.pallas_call(
        body,
        out_shape=outs,
        in_specs=in_specs,
        out_specs=[VMEM] * len(outs),
        scratch_shapes=scratch,
        name=getattr(body, "func", body).__name__,
        compiler_params=pltpu.CompilerParams(vmem_limit_bytes=VMEM_BYTES),
        cost_estimate=pl.CostEstimate(flops=1000, bytes_accessed=1000, transcendentals=0),
    )(*operands)


def shape(dims, dtype=LOW):
    return jax.ShapeDtypeStruct(dims, dtype)


def norm_parts(rows):
    centred = rows - jnp.mean(rows, axis=-1, keepdims=True)
    scale = lax.rsqrt(jnp.mean(centred * centred, axis=-1, keepdims=True) + 1e-05)
    return centred * scale, scale


def norm_back(upstream, gain, unit, scale):
    inner = upstream * gain
    centre = jnp.mean(inner, axis=-1, keepdims=True)
    along = jnp.mean(inner * unit, axis=-1, keepdims=True)
    sums = (jnp.sum(upstream * unit, axis=0, keepdims=True), jnp.sum(upstream, axis=0, keepdims=True))
    return (inner - centre - unit * along) * scale, sums


def pack_first_kernel(
    meta, tokens, cot, w_q, w_k, w_v, w_o, w_down, gain_one, bias_one, gain_two, bias_two, tok_out, cot_out, qkv_out, down_out
):
    rows, columns = w_q.shape[0], qkv_out.shape[1] // 3
    half, third = rows // 2, rows // 6
    other = 1 - meta[0, WHICH]
    tok_out[...] = tokens[other, 0]
    cot_out[...] = cot[other, 0]
    for part in range(PARTS):

        @pl.when(meta[0, PART] == part)
        def _(part=part):
            for at, w in enumerate((w_q, w_k, w_v)):
                qkv_out[:rows, at * columns : (at + 1) * columns] = w[:, part * columns : (part + 1) * columns]

    qkv_out[rows : rows + EXTRA, :] = jnp.zeros((EXTRA, 3 * columns), LOW)
    for at, vector in enumerate((gain_one, bias_one, gain_two, bias_two)):
        qkv_out[rows + at : rows + at + 1, :rows] = vector[...].reshape(1, rows)
    for part in range(PARTS):
        low = pl.multiple_of(part * rows + meta[0, CORE] * half, half)
        down_out[part] = w_down[pl.ds(low, half), :]
    out_rows = w_o[pl.ds(pl.multiple_of(meta[0, CORE] * half, half), half), :]
    at = rows + EXTRA
    qkv_out[at : at + half, :] = out_rows[:, : 3 * columns]
    at += half
    for g in range(3):
        qkv_out[at : at + third, g * columns : (g + 1) * columns] = out_rows[g * third : (g + 1) * third, 3 * columns :]


def pack_second_kernel(meta, w_gate, w_up, out):
    half, width = out.shape[1], out.shape[2]
    step = 2 * half
    low = pl.multiple_of(meta[0, CORE] * half, half)
    for base, w in ((0, w_gate), (PARTS, w_up)):
        for part in range(PARTS):
            for block in range(width // step):
                start = (block * PARTS + part) * step
                out[base + part, :, block * step : (block + 1) * step] = w[pl.ds(low, half), start : start + step]


def project_kernel(heads, pieces, meta, table_ref, swap_q, swap_k, spread_v, *refs):
    x_refs, w_refs, (q_refs, k_refs, v_refs) = refs[:PARTS], refs[PARTS : PARTS + pieces], [refs[-2 - 3 * heads + at * heads : -2 - 2 * heads + at * heads] for at in range(3)]
    w_all, turn = refs[-2:]
    rows = w_all.shape[0] // pieces
    block = x_refs[0].shape[0]
    local = block // 2
    for distance, w in enumerate(w_refs):
        w_all[pl.ds(pl.multiple_of((meta[0, DP] ^ distance) * rows, rows), rows), :] = w[:rows, :]
    for at in range(2 * PARTS):
        start = pl.multiple_of(meta[0, STARTS + at], local)
        turn[at * local : (at + 1) * local, :] = table_ref[pl.ds(start, local), :]
    weights = w_all[...]
    w_q, w_k, w_v = (mm(weights, m[...]).astype(LOW) for m in (swap_q, swap_k, spread_v))
    for r in range(PARTS):
        out_rows = slice(r * block, (r + 1) * block)
        x = x_refs[r][...]
        cosine, sine = turn[out_rows, :WIDE], turn[out_rows, WIDE:]
        for out_refs, w, scale in ((q_refs, w_q, 0.0625), (k_refs, w_k, None)):
            made = mm(x, w)
            for h in range(heads):
                one = made[:, h * WIDE : (h + 1) * WIDE]
                turned = (one * cosine + pltpu.roll(one, HEAD_DIM, 1) * sine).astype(LOW)
                out_refs[h][out_rows, :] = turned if scale is None else turned * jnp.asarray(scale, LOW)
        made = mm(x, w_v).astype(LOW)
        for h in range(heads):
            v_refs[h][out_rows, :] = made[:, h * WIDE : (h + 1) * WIDE]


def fill_bias(meta, length, bias_ref, local):
    for at in range(bias_ref.shape[0] // local):
        place = meta[0, STARTS + at] + lax.broadcasted_iota(jnp.int32, (local, WIDE), 0)
        bias_ref[at * local : (at + 1) * local, :] = jnp.where(place < length, 0.0, -1e30)


def each_block(count, step):
    if count <= 4:
        for number in range(count):
            step(number)
    else:
        lax.fori_loop(0, count, lambda number, carry: step(number) or carry, 0)


def block_rows(number, block):
    if isinstance(number, int):
        return slice(number * block, (number + 1) * block)
    return pl.ds(pl.multiple_of(number * block, block), block)


def attend_kernel(heads, block, meta, lengths, *refs):
    q_refs, k_refs, v_refs, spread_ref = refs[:heads], refs[heads : 2 * heads], refs[2 * heads : 3 * heads], refs[3 * heads]
    out, lse_refs, wide_ref = refs[3 * heads + 1], refs[-1 - heads : -1], refs[-1]
    row_count, key_count = q_refs[0].shape[0], k_refs[0].shape[0]
    span = row_count // PARTS
    local = span // 2
    length = lengths[meta[0, WHICH], 0]
    places = [meta[0, STARTS + at] + lax.broadcasted_iota(jnp.int32, (1, local), 1) for at in range(key_count // local)]
    bias = jnp.where(jnp.concatenate(places, axis=1) < length, 0.0, -1e30)
    for h in range(heads):

        def step(number, h=h):
            rows = block_rows(number, block)
            scores = mm_nt(q_refs[h][rows, :], k_refs[h][...]) + bias
            top = jnp.max(scores, axis=1, keepdims=True)
            weights = jnp.exp(scores - top)
            total = jnp.sum(weights, axis=1, keepdims=True)
            wide_ref[rows, h * WIDE : (h + 1) * WIDE] = (mm(weights.astype(LOW), v_refs[h][...]) / total).astype(LOW)
            lse_refs[h][:, rows] = jnp.broadcast_to(top + jnp.log(total), (block, WIDE)).T[:1, :]

        each_block(row_count // block, step)
    for r in range(PARTS):
        out[r] = mm_nt(wide_ref[r * span : (r + 1) * span, :], spread_ref[...]).astype(LOW)


def grad_attended_kernel(meta, w_o, spread_ref, *refs):
    grads_in, att_in, outs = refs[:PARTS], refs[PARTS : 2 * PARTS], refs[2 * PARTS :]
    *wide_outs, dw_ref, grad_part = outs
    columns = w_o.shape[0]
    weights = mm_tn(spread_ref[...], w_o[...]).astype(LOW)
    span = grads_in[0].shape[0]
    for r in range(PARTS):
        grads = grads_in[r][...]
        wide = mm_nt(grads, weights).astype(LOW)
        for h, out in enumerate(wide_outs):
            out[r * span : (r + 1) * span, :] = wide[:, h * WIDE : (h + 1) * WIDE]
        for part in range(PARTS):

            @pl.when(meta[0, PART] == part)
            def _(r=r, part=part):
                grad_part[r] = grads_in[r][:, part * columns : (part + 1) * columns]

    for distance in range(PARTS):
        total = mm_tn(att_in[distance][distance], grad_part[0])
        for r in range(1, PARTS):
            total = total + mm_tn(att_in[distance][r ^ distance], grad_part[r])
        low = pl.multiple_of((meta[0, PART] ^ distance) * columns, columns)
        dw_ref[pl.ds(low, columns), :] = total.astype(LOW)


def attend_back_kernel(block, meta, lengths, q_ref, k_ref, v_ref, table_ref, lse_ref, grad_ref, *refs):
    dq_ref, dk_ref, dv_ref, bias_ref, turn, dk_sum, dv_sum = refs
    row_count, key_count = q_ref.shape[0], k_ref.shape[0]
    local = row_count // PARTS // 2
    fill_bias(meta, lengths[meta[0, WHICH], 0], bias_ref, local)
    for at in range(key_count // local):
        start = pl.multiple_of(meta[0, STARTS + at], local)
        turn[at * local : (at + 1) * local, :] = table_ref[pl.ds(start, local), :]

    def unturn(value, rows):
        cosine, sine = turn[rows, :WIDE], turn[rows, WIDE:]
        return (value * cosine - pltpu.roll(value, HEAD_DIM, 1) * sine).astype(LOW)

    keys, values = k_ref[...], v_ref[...]
    keys_t = keys.T
    dk_sum[...] = jnp.zeros_like(dk_sum)
    dv_sum[...] = jnp.zeros_like(dv_sum)

    def step(number):
        rows = block_rows(number, block)
        bias = jnp.concatenate([bias_ref[...]] * (block // WIDE), axis=1)
        queries, grads = q_ref[rows, :], grad_ref[rows, :]
        probs = jnp.exp(mm_nt(keys, queries) + bias - lse_ref[:, rows])
        grad_probs = mm_nt(values, grads)
        delta = jnp.sum(probs * grad_probs, axis=0, keepdims=True)
        grad_scores = (probs * (grad_probs - delta)).astype(LOW)
        dv_sum[...] += mm(probs.astype(LOW), grads)
        dk_sum[...] += mm(grad_scores, queries)
        dq_ref[rows, :] = unturn(mm(keys_t, grad_scores).T * 0.125, rows)

    each_block(row_count // block, step)
    dk_ref[...] = unturn(dk_sum[...] * 2.0, slice(None))
    dv_ref[...] = dv_sum[...].astype(LOW)


def place_gate_up(meta, refs, block, target, sems, at):
    half = refs[0].shape[2]
    copies = []
    for side, ref in enumerate(refs):
        low = pl.multiple_of((meta[0, CORE] ^ side) * half, half)
        copy = pltpu.make_async_copy(ref.at[:, block], target.at[:, pl.ds(low, half), :], sems.at[at + side])
        copy.start()
        copies.append(copy)
    return copies, at + 2


def place_down(meta, own, refs, block, target, sems, at):
    count, rows = target.shape[0], target.shape[1]
    half = rows // 2
    low = pl.multiple_of(block * rows, rows)
    copies = [pltpu.make_async_copy(own.at[pl.ds(low, rows), :], target.at[meta[0, DP]], sems.at[at])]
    for number, ref in enumerate(refs):
        distance, side = number % (count - 1) + 1, number // (count - 1)
        low = pl.multiple_of((meta[0, CORE] ^ side) * half, half)
        to = target.at[meta[0, DP] ^ distance, pl.ds(low, half), :]
        copies.append(pltpu.make_async_copy(ref.at[block], to, sems.at[at + 1 + number]))
    for copy in copies:
        copy.start()
    return copies, at + len(copies)


def wait_all(copies):
    for copy in copies:
        copy.wait()


def residual_kernel(pieces, meta, x_ref, w_own, *refs):
    att, w_refs, w_core, refs = refs[:PARTS], refs[PARTS : PARTS + pieces], refs[PARTS + pieces], refs[PARTS + pieces + 1 :]
    residual_out, low_out, vector_out, w_out, w_o, gathered = refs
    columns, rows = att[0].shape[2], w_own.shape[0]
    half, third = rows // 2, rows // 6
    w_o[pl.ds(pl.multiple_of(meta[0, DP] * rows, rows), rows), :] = w_own[...]

    def fill(ref, low):
        w_o[pl.ds(pl.multiple_of(low, half), half), : 3 * columns] = ref[:half, :]
        for g in range(3):
            to = pl.ds(pl.multiple_of(low + g * third, third), third)
            w_o[to, 3 * columns :] = ref[half:, g * columns : (g + 1) * columns]

    for distance, ref in enumerate(w_refs):
        gathered[meta[0, DP] ^ distance] = ref[rows : rows + EXTRA, :]
        if distance:
            low = (meta[0, DP] ^ distance) * rows
            fill(ref[rows + EXTRA :, :], low + meta[0, CORE] * half)
            fill(w_core[distance - 1], low + (1 - meta[0, CORE]) * half)
    vectors = jnp.concatenate([gathered[d][:8, :rows] for d in range(pieces)], axis=1).astype(FULL)
    vector_out[...] = vectors
    residual = x_ref[...].astype(FULL)
    for r in range(PARTS):
        low = pl.multiple_of((meta[0, PART] ^ r) * columns, columns)
        residual = residual + mm(att[r][r], w_o[pl.ds(low, columns), :])
    w_out[...] = w_o[pl.ds(pl.multiple_of(meta[0, PART] * columns, columns), columns), :]
    residual_out[...] = residual
    unit, _ = norm_parts(residual)
    low_out[...] = (unit * vectors[0:1] + vectors[1:2]).astype(LOW)


def feed_kernel(meta, lengths, residual_ref, vectors, cot_ref, cot_got, *refs):
    gu_refs, down_own, down_refs, refs = refs[:2], refs[2], refs[3:-10], refs[-10:]
    grad_ffn_out, grad_branch_out, grad_one_out, own_out, back_out, sums_out, held, gates, ups, sems = refs
    width = residual_ref.shape[1]
    copies, at = [], 0
    for part in range(PARTS):
        gate, at = place_gate_up(meta, gu_refs, part, held.at[part], sems, at)
        up, at = place_gate_up(meta, gu_refs, PARTS + part, held.at[PARTS + part], sems, at)
        down, at = place_down(meta, down_own, down_refs, part, held.at[2 * PARTS + part], sems, at)
        copies.append(gate + up + down)

    def weights(number):
        return held[number].reshape(width, width)

    which = meta[0, WHICH]
    local = cot_got.shape[0]
    unit_one, scale_one = norm_parts(residual_ref[...])
    normed = unit_one * vectors[0:1] + vectors[1:2]
    normed_low = normed.astype(LOW)
    residual = normed
    for part in range(PARTS):
        wait_all(copies[part])
        gate = mm(normed_low, weights(part))
        up = mm(normed_low, weights(PARTS + part))
        sigma = 1.0 / (1.0 + jnp.exp(-gate))
        silu = gate * sigma
        residual = residual + mm((silu * up).astype(LOW), weights(2 * PARTS + part))
        gates[part] = up * (sigma + silu * (1.0 - sigma))
        ups[part] = silu
    unit_two, scale_two = norm_parts(residual)
    layer = unit_two * vectors[2:3] + vectors[3:4]
    length = lengths[which, 0]
    upstream = []
    for half, (out, cot) in enumerate(((own_out, cot_ref[which, 0]), (back_out, cot_got[...]))):
        place = meta[0, STARTS + half] + lax.broadcasted_iota(jnp.int32, (local, 1), 0)
        valid = place < length
        out[...] = jnp.where(valid, layer[half * local : (half + 1) * local], 0.0).astype(LOW)
        upstream.append(jnp.where(valid, cot.astype(FULL), 0.0))
    grad_two, sums_two = norm_back(jnp.concatenate(upstream, axis=0), vectors[2:3], unit_two, scale_two)
    grad_ffn = grad_two.astype(LOW)
    grad_ffn_out[...] = grad_ffn
    grad_normed = grad_two
    for part in range(PARTS):
        grad_hidden = mm_nt(grad_ffn, weights(2 * PARTS + part))
        grad_normed = (
            grad_normed
            + mm_nt((grad_hidden * gates[part]).astype(LOW), weights(part))
            + mm_nt((grad_hidden * ups[part]).astype(LOW), weights(PARTS + part))
        )
    grad_one, sums_one = norm_back(grad_normed, vectors[0:1], unit_one, scale_one)
    grad_one_out[...] = grad_one
    grad_branch_out[...] = grad_one.astype(LOW)
    sums_out[...] = jnp.concatenate([*sums_one, *sums_two, jnp.zeros((4, width), FULL)], axis=0)


def hidden_kernel(meta, *refs):
    x_refs, gu_refs, refs = refs[:PARTS], refs[PARTS : PARTS + 2], refs[PARTS + 2 :]
    hidden_out, gate_out, up_out, held_gate, held_up, sems = refs
    part, width = meta[0, PART], hidden_out.shape[1]
    first, at = place_gate_up(meta, gu_refs, part, held_gate, sems, 0)
    second, at = place_gate_up(meta, gu_refs, PARTS + part, held_up, sems, at)
    wait_all(first + second)
    w_gate, w_up = held_gate[...].reshape(width, width), held_up[...].reshape(width, width)
    block = x_refs[0].shape[0]
    for r in range(PARTS):
        rows = slice(r * block, (r + 1) * block)
        x = x_refs[r][...]
        gate, up = mm(x, w_gate), mm(x, w_up)
        sigma = 1.0 / (1.0 + jnp.exp(-gate))
        silu = gate * sigma
        hidden_out[rows, :] = (silu * up).astype(LOW)
        gate_out[rows, :] = (up * (sigma + silu * (1.0 - sigma))).astype(LOW)
        up_out[rows, :] = silu.astype(LOW)


def split_terms(meta, terms, outs):
    rows = terms.shape[0] // len(outs)
    for distance, out in enumerate(outs):
        low = pl.multiple_of((meta[0, DP] ^ distance) * rows, rows)
        out[:rows, :] = terms[pl.ds(low, rows), :]


def down_kernel(meta, hidden_ref, *refs):
    grads, outs, terms = refs[:PARTS], refs[PARTS:-1], refs[-1]
    block = grads[0].shape[0]
    total = mm_tn(hidden_ref[:block, :], grads[0][...])
    for r in range(1, PARTS):
        total = total + mm_tn(hidden_ref[r * block : (r + 1) * block, :], grads[r][...])
    terms[...] = total.astype(LOW)
    split_terms(meta, terms, outs)


def gate_up_kernel(meta, gate_ref, up_ref, *refs):
    grads, x_refs, down_own, refs = refs[:PARTS], refs[PARTS : 2 * PARTS], refs[2 * PARTS], refs[2 * PARTS + 1 :]
    held, gate_low, up_low, terms, sems = refs[-5:]
    count = held.shape[0]
    down_refs, outs = refs[: 2 * count - 2], refs[2 * count - 2 : -5]
    copies, _ = place_down(meta, down_own, down_refs, meta[0, PART], held, sems, 0)
    wait_all(copies)
    w_down = held[...].reshape(terms.shape)
    block = grads[0].shape[0]
    for r in range(PARTS):
        rows = slice(r * block, (r + 1) * block)
        grad_hidden = mm_nt(grads[r][...], w_down)
        gate_low[rows, :] = (grad_hidden * gate_ref[rows, :].astype(FULL)).astype(LOW)
        up_low[rows, :] = (grad_hidden * up_ref[rows, :].astype(FULL)).astype(LOW)
    for at, source in enumerate((gate_low, up_low)):
        total = mm_tn(x_refs[0][...], source[:block, :])
        for r in range(1, PARTS):
            total = total + mm_tn(x_refs[r][...], source[r * block : (r + 1) * block, :])
        terms[...] = total.astype(LOW)
        split_terms(meta, terms, outs[at * count : (at + 1) * count])


def projections_back_kernel(heads, pieces, meta, swap_q, swap_k, spread_v, sums, out_terms, *refs):
    grads, refs = [refs[at * heads : (at + 1) * heads] for at in range(3)], refs[3 * heads :]
    x_refs, w_refs, refs = refs[:PARTS], refs[PARTS : PARTS + pieces], refs[PARTS + pieces :]
    outs, (near_out, far_out, w_all, terms) = refs[:pieces], refs[pieces:]
    rows = w_all.shape[0] // pieces
    for distance, w in enumerate(w_refs):
        w_all[pl.ds(pl.multiple_of((meta[0, DP] ^ distance) * rows, rows), rows), :] = w[:rows, :]
    block = x_refs[0].shape[0]
    weights = w_all[...]
    total = jnp.zeros(weights.shape, FULL)
    for r in range(PARTS):
        span = slice(r * block, (r + 1) * block)
        low = sum(
            mm_nt(jnp.concatenate([ref[span, :] for ref in of_heads], axis=1), m[...])
            for of_heads, m in zip(grads, (swap_q, swap_k, spread_v))
        ).astype(LOW)
        total = total + mm_tn(x_refs[r][...], low)
        onward = mm_nt(low, weights)
        if r % 2 == 0:
            near_out[r // 2] = onward
        else:
            far_out[r // 2] = onward.astype(LOW)
    terms[:, : weights.shape[1]] = total.astype(LOW)
    terms[:, weights.shape[1] :] = out_terms[...]
    split_terms(meta, terms, outs)
    for distance, out in enumerate(outs):
        out[rows:, :] = jnp.zeros((EXTRA, terms.shape[1]), LOW)
        for block_at in range(pieces):

            @pl.when(meta[0, DP] ^ distance == block_at)
            def _(out=out, block_at=block_at):
                out[rows : rows + 8, :rows] = sums[:, block_at * rows : (block_at + 1) * rows].astype(LOW)


def join_rows_kernel(meta, *refs):
    out = refs[-1]
    rows = refs[0].shape[0]
    for r in range(PARTS):
        low = pl.multiple_of((meta[0, PART] ^ r) * rows, rows)
        out[pl.ds(low, rows), :] = refs[r][...].astype(FULL)


def join_columns_kernel(meta, *refs):
    outs, held = refs[PARTS:-1], refs[-1]
    step = outs[0].shape[0]
    for r in range(PARTS):
        held[meta[0, PART] ^ r] = refs[r][...]
    for at, out in enumerate(outs):
        for part in range(PARTS):
            value = held[part, at].astype(FULL)
            for block in range(value.shape[1] // step):
                start = (block * PARTS + part) * step
                out[:, start : start + step] = value[:, block * step : (block + 1) * step]


def join_projections_kernel(meta, *refs):
    outs, sums_out, held = refs[PARTS:-2], refs[-2], refs[-1]
    rows, columns = outs[0].shape[0], refs[0].shape[1] // len(outs)
    for r in range(PARTS):
        held[meta[0, PART] ^ r] = refs[r][...]
    sums = jnp.zeros((8, rows), FULL)
    for part in range(PARTS):
        value = held[part].astype(FULL)
        for at, out in enumerate(outs):
            out[:, part * columns : (part + 1) * columns] = value[:rows, at * columns : (at + 1) * columns]
        sums = sums + value[rows : rows + 8, :rows]
    sums_out[...] = sums


def gather_pieces(own, bits, starts=None, gate=None):
    held = {0: own}
    for bit in bits:
        for distance in list(held):
            source = held[distance]
            if distance == 0 and starts is not None:
                source = after(source, *starts)
            elif distance != 0 and gate is not None:
                source = after(source, gate)
            held[distance | bit] = hop(source, "dp", bit)
    return [held[distance] for distance in range(len(held))]


def send_terms(chunks, gate=None):
    return [
        hop(chunk if gate is None else after(chunk, *gate), "dp", distance)
        for distance, chunk in enumerate(chunks)
        if distance
    ]


def sum_terms(chunks, got):
    total = chunks[0].astype(FULL)
    for one in got:
        total = total + one.astype(FULL)
    return total


def shards(
    tokens, lengths, w_query, w_key, w_value, w_output, w_gate, w_up, w_down,
    first_gain, first_bias, second_gain, second_bias, cotangent,
):
    _, _, local, width = tokens.shape
    dp_count, blk_count = lax.axis_size("dp"), lax.axis_size("blk")
    dp, blk = lax.axis_index("dp"), lax.axis_index("blk")
    side = blk_count // 2
    which = blk // side
    first = which == 0
    core, part = blk % 2, blk % PARTS
    heads = width // HEAD_DIM // PARTS
    columns = heads * HEAD_DIM
    rows, ff_rows = w_query.shape[0], w_down.shape[0]
    half, ff = rows // 2, w_gate.shape[1]
    block = 2 * local
    row_count = PARTS * block
    spread_bits = bits_between(PARTS, side)
    sum_bits = bits_between(PARTS, blk_count)
    dp_bits = bits_between(1, dp_count)
    back_bits = dp_bits[::-1]
    table = jnp.asarray(turn_table(local * blk_count))
    swap_q, swap_k, spread_v = (
        jnp.asarray(swap_matrix(heads, 3 * columns, at * columns, at < 2), LOW) for at in range(3)
    )
    only_q, only_k = (jnp.asarray(swap_matrix(heads, 3 * columns, at * columns, False), LOW) for at in range(2))
    spread = jnp.asarray(swap_matrix(heads, columns, 0, False), LOW)

    starts = [(blk ^ distance ^ away) * local for distance in range(side) for away in (0, side)]
    meta = jnp.stack([which, core, part, dp, *starts]).astype(jnp.int32).reshape(1, -1)

    gate_up_own = call(
        pack_second_kernel, [shape((2 * PARTS, half, width))], [SMEM] + [VMEM] * 2, [], meta, w_gate, w_up
    )[0]
    gate_up_core = lax.all_gather(gate_up_own, "dp", axis=0, tiled=False)
    tok_send, cot_send, qkv_own, down_own = call(
        pack_first_kernel,
        [shape((local, width)), shape((local, width)), shape((rows + EXTRA + half + half // 3, 3 * columns))]
        + [shape((PARTS, half, width))],
        [SMEM] + [VMEM] * 11, [], after(meta, gate_up_own), tokens, cotangent, w_query, w_key, w_value, w_output, w_down,
        first_gain, first_bias, second_gain, second_bias,
    )
    tok_got = hop(tok_send, "blk", side)
    qkv = gather_pieces(qkv_own, dp_bits)
    x_own = jnp.concatenate([jnp.where(first, tokens[0, 0], tokens[1, 0]), tok_got])
    x_core, x_near = hop(x_own, "blk", 1), hop(x_own, "blk", 2)
    x_far = hop(after(x_near, x_core, *(qkv[bit] for bit in dp_bits)), "blk", 1)
    x_all = [x_own, x_core, x_near, x_far]
    down_pieces = {0: down_own}
    for bit in dp_bits[:2]:
        down_pieces[bit] = hop(after(down_own, *qkv[1:]), "dp", bit)
    cot_got = hop(after(cot_send, x_near), "blk", side)

    wide_shape = shape((row_count, WIDE))
    made = call(
        functools.partial(project_kernel, heads, dp_count), [wide_shape] * (3 * heads),
        [SMEM] + [VMEM] * (4 + PARTS + dp_count),
        [pltpu.VMEM((width, 3 * columns), LOW), pltpu.VMEM((row_count, 2 * WIDE), FULL)],
        after(meta, cot_got), table, swap_q, swap_k, spread_v, *x_all, *qkv,
    )
    queries, keys, values = (made[at * heads : (at + 1) * heads] for at in range(3))
    out_rows = rows + EXTRA
    qkv_core = hop(after(jnp.stack([piece[out_rows:] for piece in qkv[1:]]), queries[0]), "blk", 1)
    for bit in spread_bits:
        keys, values = ([jnp.concatenate([one, hop(one, "blk", bit)]) for one in many] for many in (keys, values))
    key_count = keys[0].shape[0]
    q_block = max(WIDE, min(row_count, 512 * 1024 // key_count))
    attended = call(
        functools.partial(attend_kernel, heads, q_block),
        [shape((PARTS, block, columns))] + [shape((1, row_count), FULL)] * heads,
        [SMEM] * 2 + [VMEM] * (1 + 3 * heads),
        [pltpu.VMEM((row_count, heads * WIDE), LOW)],
        meta, lengths, *queries, *keys, *values, spread,
    )
    attended, lse = attended[0], attended[1:]
    att_send = after(attended, qkv_core, *(down_pieces[bit] for bit in dp_bits[:2]))
    att_core, att_near = hop(att_send, "blk", 1), hop(att_send, "blk", 2)
    att_all = [attended, att_core, att_near, hop(after(att_near, att_core), "blk", 1)]
    residual_one, normed_low, all_vectors, w_o = call(
        functools.partial(residual_kernel, dp_count),
        [shape((block, width), FULL), shape((block, width)), shape((8, width), FULL), shape((columns, width))],
        [SMEM] + [VMEM] * (2 + PARTS + dp_count + 1),
        [pltpu.VMEM((width, width), LOW), pltpu.VMEM((dp_count, EXTRA, 3 * columns), LOW)],
        meta, x_own, w_output, *att_all, *qkv, qkv_core,
    )
    normed_core, normed_near = hop(normed_low, "blk", 1), hop(normed_low, "blk", 2)
    middle = PARTS // 2
    down_pieces[3] = jnp.concatenate(
        [hop(down_pieces[1][:middle], "dp", 2), hop(down_pieces[2][middle:], "dp", 1)]
    )
    for bit in dp_bits[2:]:
        for distance in range(bit):
            down_pieces[distance | bit] = hop(down_pieces[distance], "dp", bit)
    down_pieces = [down_pieces[distance] for distance in range(dp_count)]
    down_core = [hop(after(piece, normed_low), "blk", 1) for piece in down_pieces[1:]]
    down_all = (w_down, *down_pieces[1:], *down_core)
    gate_up_all = (gate_up_core, hop(after(gate_up_core, normed_core), "blk", 1))

    part_shape, w_shape = (PARTS, block, width), (dp_count, rows, width)
    down_copies = 2 * dp_count - 1
    grad_ffn, grad_branch, grad_one, layer_own, layer_back, sums = call(
        feed_kernel,
        [shape((block, width))] * 2 + [shape((block, width), FULL)] + [shape((local, width))] * 2
        + [shape((8, width), FULL)],
        [SMEM] * 2 + [VMEM] * 4 + [ANY] * (2 + len(down_all)),
        [
            pltpu.VMEM((3 * PARTS, *w_shape), LOW),
            pltpu.VMEM(part_shape, FULL),
            pltpu.VMEM(part_shape, FULL),
            pltpu.SemaphoreType.DMA((PARTS * (4 + down_copies),)),
        ],
        after(meta, normed_core), lengths, residual_one, all_vectors, cotangent, cot_got, *gate_up_all, *down_all,
    )
    ffn_core, ffn_near = hop(grad_ffn, "blk", 1), hop(grad_ffn, "blk", 2)
    normed_all = [normed_low, normed_core, normed_near, hop(after(normed_near, grad_ffn), "blk", 1)]

    long, chunk = shape((row_count, width)), shape((rows, width))
    hidden, gate_factor, up_factor = call(
        hidden_kernel, [long] * 3,
        [SMEM] + [VMEM] * PARTS + [ANY] * 2,
        [pltpu.VMEM(w_shape, LOW), pltpu.VMEM(w_shape, LOW), pltpu.SemaphoreType.DMA((4,))],
        after(meta, grad_ffn), *normed_all, *gate_up_all,
    )
    ffn_all = [grad_ffn, ffn_core, ffn_near, hop(after(ffn_near, hidden, ffn_core), "blk", 1)]
    branch_core, branch_near = (hop(after(grad_branch, ffn_near, hidden), "blk", bit) for bit in (1, 2))
    layer_got = hop(after(layer_back, ffn_all[3], branch_core), "blk", side)
    down_terms = call(
        down_kernel, [chunk] * dp_count, [SMEM] + [VMEM] * (1 + PARTS), [pltpu.VMEM((width, width), LOW)],
        after(meta, branch_core), hidden, *ffn_all,
    )
    down_got = send_terms(down_terms)
    gate_up_terms = call(
        gate_up_kernel, [chunk] * (2 * dp_count),
        [SMEM] + [VMEM] * (2 + 2 * PARTS) + [ANY] * len(down_all),
        [pltpu.VMEM(w_shape, LOW), pltpu.VMEM((row_count, width), LOW), pltpu.VMEM((row_count, width), LOW)]
        + [pltpu.VMEM((width, width), LOW), pltpu.SemaphoreType.DMA((down_copies,))],
        after(meta, down_terms[0]), gate_factor, up_factor, *ffn_all, *normed_all, *down_all,
    )

    def sum_halves(total):
        for bit in sum_bits:
            low = total.astype(LOW)
            total = low.astype(FULL) + hop(low, "blk", bit).astype(FULL)
        return total.astype(LOW)

    branch_far = hop(after(branch_near, layer_got, gate_up_terms[0], *(down_got[bit - 1] for bit in dp_bits)), "blk", 1)
    *grads_wide, out_terms = call(
        grad_attended_kernel, [wide_shape] * heads + [shape((width, columns))],
        [SMEM] + [VMEM] * (2 + 2 * PARTS), [pltpu.VMEM((PARTS, block, columns), LOW)], meta, w_o, spread,
        grad_branch, branch_core, branch_near, branch_far, *att_all,
    )
    down_sum = sum_terms(down_terms, down_got)
    down_full = sum_halves(down_sum)
    gate_got = send_terms(gate_up_terms[:dp_count])
    grad_q, grad_k, grad_v, before = [], [], [], (out_terms, down_sum)
    for h in range(heads):
        if h == heads - 1:
            gate_sum = sum_terms(gate_up_terms, [after(got, grad_q[-1]) for got in gate_got])
            up_got = send_terms(gate_up_terms[dp_count:], (gate_sum,))
            before = (gate_sum, down_full)
            down_near = hop(down_full, "blk", 2)
        grads = call(
            functools.partial(attend_back_kernel, q_block),
            [wide_shape, shape((key_count, WIDE)), shape((key_count, WIDE))],
            [SMEM] * 2 + [VMEM] * 6,
            [pltpu.VMEM((key_count, WIDE), FULL), pltpu.VMEM((key_count, 2 * WIDE), FULL)]
            + [pltpu.VMEM((key_count, WIDE), FULL)] * 2,
            after(meta, *before, *grad_q[-1:]), lengths, queries[h], keys[h], values[h], table, lse[h], grads_wide[h],
        )
        before = ()
        for many, one in zip((grad_q, grad_k, grad_v), grads):
            many.append(one)
    gate_full = sum_halves(gate_sum)
    for bit in reversed(spread_bits):
        middle = grad_k[0].shape[0] // 2
        grad_k, grad_v = (
            [
                (one[:middle].astype(FULL) + hop(one[middle:], "blk", bit).astype(FULL)).astype(LOW)
                for one in many
            ]
            for many in (grad_k, grad_v)
        )
    *qkv_terms, token_keep, token_send = call(
        functools.partial(projections_back_kernel, heads, dp_count),
        [shape((rows + EXTRA, width))] * dp_count
        + [shape((2, block, width), FULL), shape((2, block, width))],
        [SMEM] + [VMEM] * (5 + 3 * heads + PARTS + dp_count),
        [pltpu.VMEM((width, 3 * columns), LOW), pltpu.VMEM((width, width), LOW)],
        meta, only_q, only_k, spread_v, sums, out_terms, *grad_q, *grad_k, *grad_v, *x_all, *qkv,
    )
    up_sum = sum_terms(gate_up_terms[dp_count:], [after(got, token_keep) for got in up_got])

    first_gate = (gate_full, up_sum, down_near)
    token_got = hop(after(token_send, *first_gate), "blk", 1).astype(FULL)
    up_full = sum_halves(up_sum)
    near_send = (token_keep[1] + token_got[1]).astype(LOW)
    token_near = hop(near_send, "blk", 2)
    qkv_got = send_terms(qkv_terms, first_gate)
    qkv_sum = sum_terms(qkv_terms, [after(got, token_near) for got in qkv_got]).astype(LOW)
    qkv_full = sum_halves(after(qkv_sum, up_full, token_near))
    down_core, down_far = (hop(after(one, qkv_sum), "blk", 1) for one in (down_full, down_near))
    pair_full = after(jnp.stack([gate_full, up_full]), qkv_sum)
    pair_core, pair_near = hop(after(pair_full, down_core, down_far), "blk", 1), hop(pair_full, "blk", 2)
    grad_rows = after(grad_one, qkv_sum) + token_keep[0] + token_got[0] + token_near.astype(FULL)
    rows_got = hop(grad_rows[local:].astype(LOW), "blk", side).astype(FULL)
    grad_down = call(
        join_rows_kernel, [shape((ff_rows, width), FULL)], [SMEM] + [VMEM] * PARTS, [],
        after(meta, pair_core), down_full, down_core, down_near, down_far,
    )[0]
    pair_far = hop(after(pair_near, pair_core, grad_down), "blk", 1)
    qkv_core, qkv_near = (hop(after(qkv_full, pair_near), "blk", bit) for bit in (1, 2))
    grad_gate, grad_up = call(
        join_columns_kernel, [shape((rows, ff), FULL)] * 2, [SMEM] + [VMEM] * PARTS,
        [pltpu.VMEM((PARTS, 2, rows, width), LOW)], meta, pair_full, pair_core, pair_near, pair_far,
    )
    qkv_far = hop(after(qkv_near, qkv_core, grad_gate, rows_got), "blk", 1)
    grad_tokens = jnp.where(
        first, jnp.stack([grad_rows[:local], rows_got]), jnp.stack([rows_got, grad_rows[:local]])
    )[:, None]
    layer_out = jnp.where(first, jnp.stack([layer_own, layer_got]), jnp.stack([layer_got, layer_own]))[:, None]
    grad_query, grad_key, grad_value, grad_output, vector_sums = call(
        join_projections_kernel, [shape((rows, width), FULL)] * 4 + [shape((8, rows), FULL)],
        [SMEM] + [VMEM] * PARTS, [pltpu.VMEM((PARTS, rows + EXTRA, width), LOW)], meta, qkv_full, qkv_core, qkv_near, qkv_far,
    )
    return (
        layer_out, grad_tokens, grad_query, grad_key, grad_value, grad_output, grad_gate, grad_up, grad_down,
        vector_sums[0], vector_sums[1], vector_sums[2], vector_sums[3],
    )


def solution(mesh):
    slots = P(None, "dp", "blk", None)
    matrix, vector = P("dp", None), P("dp")
    return jax.shard_map(
        shards,
        mesh=mesh,
        in_specs=(slots, P(None, "dp")) + (matrix,) * 7 + (vector,) * 4 + (slots,),
        out_specs=(slots, slots) + (matrix,) * 7 + (vector,) * 4,
        check_vma=False,
    )
```

```python
import functools

import jax
import jax.numpy as jnp
import numpy as np
from jax import lax
from jax.experimental import pallas as pl
from jax.experimental.pallas import tpu as pltpu
from jax.sharding import PartitionSpec as P

HEAD_DIM = 64
WIDE = 128
PARTS = 4
EXTRA = 16
LOW, FULL = jnp.bfloat16, jnp.float32
VMEM_MIB = {"hidden_kernel": 40, "down_kernel": 40, "gate_up_kernel": 40}
VMEM = pl.BlockSpec(memory_space=pltpu.VMEM)
SMEM = pl.BlockSpec(memory_space=pltpu.SMEM)
ANY = pl.BlockSpec(memory_space=pl.ANY)
WHICH, CORE, PART, DP, STARTS = 0, 1, 2, 3, 4


def mm(left, right):
    return jnp.dot(left, right, preferred_element_type=FULL)


def mm_nt(left, right):
    return lax.dot_general(left, right, (((1,), (1,)), ((), ())), preferred_element_type=FULL)


def mm_tn(left, right):
    return lax.dot_general(left, right, (((0,), (0,)), ((), ())), preferred_element_type=FULL)


def hop(value, axis, bit):
    size = lax.axis_size(axis)
    return lax.ppermute(value, axis, [(at, at ^ bit) for at in range(size)])


def after(value, *others):
    return lax.optimization_barrier((value, *others))[0]


def bits_between(low, high):
    bits = []
    while low < high:
        bits.append(low)
        low *= 2
    return bits


def turn_table(seq_len):
    half = HEAD_DIM // 2
    frequency = np.float32(1000.0) ** (
        -(np.arange(half, dtype=np.float32) * np.float32(2.0) / np.float32(HEAD_DIM))
    )
    angles = np.arange(seq_len, dtype=np.float32)[:, None] * frequency[None, :]
    cosine = np.cos(angles).astype(np.float32)
    sine = np.sin(angles).astype(np.float32)
    return np.concatenate([cosine] * 4 + [sine, sine, -sine, -sine], axis=1)


def swap_matrix(heads, total, first, swapped):
    half = HEAD_DIM // 2
    out = np.zeros((total, heads * WIDE), np.float32)
    for h in range(heads):
        for f in range(HEAD_DIM):
            out[first + h * HEAD_DIM + f, h * WIDE + f] = 1.0
        for f in range(half if swapped else 0):
            out[first + h * HEAD_DIM + half + f, h * WIDE + HEAD_DIM + f] = -1.0
            out[first + h * HEAD_DIM + f, h * WIDE + HEAD_DIM + half + f] = 1.0
    return out


def call(body, outs, in_specs, scratch, *operands):
    name = getattr(body, "func", body).__name__
    return pl.pallas_call(
        body,
        out_shape=outs,
        in_specs=in_specs,
        out_specs=[VMEM] * len(outs),
        scratch_shapes=scratch,
        name=getattr(body, "func", body).__name__,
        compiler_params=pltpu.CompilerParams(vmem_limit_bytes=VMEM_MIB.get(name, 60) * 1024 * 1024),
        cost_estimate=pl.CostEstimate(flops=1000, bytes_accessed=1000, transcendentals=0),
    )(*operands)


def shape(dims, dtype=LOW):
    return jax.ShapeDtypeStruct(dims, dtype)


def norm_parts(rows):
    centred = rows - jnp.mean(rows, axis=-1, keepdims=True)
    scale = lax.rsqrt(jnp.mean(centred * centred, axis=-1, keepdims=True) + 1e-05)
    return centred * scale, scale


def norm_back(upstream, gain, unit, scale):
    inner = upstream * gain
    centre = jnp.mean(inner, axis=-1, keepdims=True)
    along = jnp.mean(inner * unit, axis=-1, keepdims=True)
    sums = (jnp.sum(upstream * unit, axis=0, keepdims=True), jnp.sum(upstream, axis=0, keepdims=True))
    return (inner - centre - unit * along) * scale, sums


def pack_first_kernel(
    meta, tokens, cot, w_q, w_k, w_v, w_o, w_down, gain_one, bias_one, gain_two, bias_two, tok_out, cot_out, qkv_out, down_out
):
    rows, columns = w_q.shape[0], qkv_out.shape[1] // 3
    half, third = rows // 2, rows // 6
    other = 1 - meta[0, WHICH]
    tok_out[...] = tokens[other, 0]
    cot_out[...] = cot[other, 0]
    for part in range(PARTS):

        @pl.when(meta[0, PART] == part)
        def _(part=part):
            for at, w in enumerate((w_q, w_k, w_v)):
                qkv_out[:rows, at * columns : (at + 1) * columns] = w[:, part * columns : (part + 1) * columns]

    qkv_out[rows : rows + EXTRA, :] = jnp.zeros((EXTRA, 3 * columns), LOW)
    for at, vector in enumerate((gain_one, bias_one, gain_two, bias_two)):
        qkv_out[rows + at : rows + at + 1, :rows] = vector[...].reshape(1, rows)
    for part in range(PARTS):
        low = pl.multiple_of(part * rows + meta[0, CORE] * half, half)
        down_out[part] = w_down[pl.ds(low, half), :]
    out_rows = w_o[pl.ds(pl.multiple_of(meta[0, CORE] * half, half), half), :]
    at = rows + EXTRA
    qkv_out[at : at + half, :] = out_rows[:, : 3 * columns]
    at += half
    for g in range(3):
        qkv_out[at : at + third, g * columns : (g + 1) * columns] = out_rows[g * third : (g + 1) * third, 3 * columns :]


def pack_second_kernel(meta, w_gate, w_up, out):
    half, width = out.shape[1], out.shape[2]
    step = 2 * half
    low = pl.multiple_of(meta[0, CORE] * half, half)
    for base, w in ((0, w_gate), (PARTS, w_up)):
        for part in range(PARTS):
            for block in range(width // step):
                start = (block * PARTS + part) * step
                out[base + part, :, block * step : (block + 1) * step] = w[pl.ds(low, half), start : start + step]


def project_kernel(heads, pieces, meta, table_ref, swap_q, swap_k, spread_v, *refs):
    x_refs, w_refs, (q_refs, k_refs, v_refs) = refs[:PARTS], refs[PARTS : PARTS + pieces], [refs[-2 - 3 * heads + at * heads : -2 - 2 * heads + at * heads] for at in range(3)]
    w_all, turn = refs[-2:]
    rows = w_all.shape[0] // pieces
    block = x_refs[0].shape[0]
    local = block // 2
    for distance, w in enumerate(w_refs):
        w_all[pl.ds(pl.multiple_of((meta[0, DP] ^ distance) * rows, rows), rows), :] = w[:rows, :]
    for at in range(2 * PARTS):
        start = pl.multiple_of(meta[0, STARTS + at], local)
        turn[at * local : (at + 1) * local, :] = table_ref[pl.ds(start, local), :]
    weights = w_all[...]
    w_q, w_k, w_v = (mm(weights, m[...]).astype(LOW) for m in (swap_q, swap_k, spread_v))
    for r in range(PARTS):
        out_rows = slice(r * block, (r + 1) * block)
        x = x_refs[r][...]
        cosine, sine = turn[out_rows, :WIDE], turn[out_rows, WIDE:]
        for out_refs, w, scale in ((q_refs, w_q, 0.0625), (k_refs, w_k, None)):
            made = mm(x, w)
            for h in range(heads):
                one = made[:, h * WIDE : (h + 1) * WIDE]
                turned = (one * cosine + pltpu.roll(one, HEAD_DIM, 1) * sine).astype(LOW)
                out_refs[h][out_rows, :] = turned if scale is None else turned * jnp.asarray(scale, LOW)
        made = mm(x, w_v).astype(LOW)
        for h in range(heads):
            v_refs[h][out_rows, :] = made[:, h * WIDE : (h + 1) * WIDE]


def fill_bias(meta, length, bias_ref, local):
    for at in range(bias_ref.shape[0] // local):
        place = meta[0, STARTS + at] + lax.broadcasted_iota(jnp.int32, (local, WIDE), 0)
        bias_ref[at * local : (at + 1) * local, :] = jnp.where(place < length, 0.0, -1e30)


def each_block(count, step):
    if count <= 4:
        for number in range(count):
            step(number)
    else:
        lax.fori_loop(0, count, lambda number, carry: step(number) or carry, 0)


def block_rows(number, block):
    if isinstance(number, int):
        return slice(number * block, (number + 1) * block)
    return pl.ds(pl.multiple_of(number * block, block), block)


def attend_kernel(heads, block, meta, lengths, *refs):
    q_refs, k_refs, v_refs, spread_ref = refs[:heads], refs[heads : 2 * heads], refs[2 * heads : 3 * heads], refs[3 * heads]
    out, lse_refs, wide_ref = refs[3 * heads + 1], refs[-1 - heads : -1], refs[-1]
    row_count, key_count = q_refs[0].shape[0], k_refs[0].shape[0]
    span = row_count // PARTS
    local = span // 2
    length = lengths[meta[0, WHICH], 0]
    places = [meta[0, STARTS + at] + lax.broadcasted_iota(jnp.int32, (1, local), 1) for at in range(key_count // local)]
    bias = jnp.where(jnp.concatenate(places, axis=1) < length, 0.0, -1e30)
    for h in range(heads):

        def step(number, h=h):
            rows = block_rows(number, block)
            scores = mm_nt(q_refs[h][rows, :], k_refs[h][...]) + bias
            top = jnp.max(scores, axis=1, keepdims=True)
            weights = jnp.exp(scores - top)
            total = jnp.sum(weights, axis=1, keepdims=True)
            wide_ref[rows, h * WIDE : (h + 1) * WIDE] = (mm(weights.astype(LOW), v_refs[h][...]) / total).astype(LOW)
            lse_refs[h][:, rows] = jnp.broadcast_to(top + jnp.log(total), (block, WIDE)).T[:1, :]

        each_block(row_count // block, step)
    for r in range(PARTS):
        out[r] = mm_nt(wide_ref[r * span : (r + 1) * span, :], spread_ref[...]).astype(LOW)


class Turn:
    def __init__(self, meta, lengths, table_ref, bias_ref, turn, local):
        fill_bias(meta, lengths[meta[0, WHICH], 0], bias_ref, local)
        for at in range(turn.shape[0] // local):
            start = pl.multiple_of(meta[0, STARTS + at], local)
            turn[at * local : (at + 1) * local, :] = table_ref[pl.ds(start, local), :]
        self.turn = turn

    def back(self, value, rows):
        cosine, sine = self.turn[rows, :WIDE], self.turn[rows, WIDE:]
        return (value * cosine - pltpu.roll(value, HEAD_DIM, 1) * sine).astype(LOW)


def back_head(block, turn, bias_ref, sums, q_ref, k_ref, v_ref, lse_ref, grad_ref, dq_ref, dk_ref, dv_ref):
    dk_sum, dv_sum = sums
    keys, values = k_ref[...], v_ref[...]
    keys_t = keys.T
    dk_sum[...] = jnp.zeros_like(dk_sum)
    dv_sum[...] = jnp.zeros_like(dv_sum)

    def step(number):
        rows = block_rows(number, block)
        bias = jnp.concatenate([bias_ref[...]] * (block // WIDE), axis=1)
        queries, grads = q_ref[rows, :], grad_ref[rows, :]
        probs = jnp.exp(mm_nt(keys, queries) + bias - lse_ref[:, rows])
        grad_probs = mm_nt(values, grads)
        delta = jnp.sum(probs * grad_probs, axis=0, keepdims=True)
        grad_scores = (probs * (grad_probs - delta)).astype(LOW)
        dv_sum[...] += mm(probs.astype(LOW), grads)
        dk_sum[...] += mm(grad_scores, queries)
        dq_ref[rows, :] = turn.back(mm(keys_t, grad_scores).T * 0.125, rows)

    each_block(q_ref.shape[0] // block, step)
    dk_ref[...] = turn.back(dk_sum[...] * 2.0, slice(None))
    dv_ref[...] = dv_sum[...].astype(LOW)


def attend_back_kernel(heads, block, meta, lengths, w_o, spread_ref, table_ref, *refs):
    grads_in, att_in, refs = refs[:PARTS], refs[PARTS : 2 * PARTS], refs[2 * PARTS :]
    ins, refs = [refs[at * heads : (at + 1) * heads] for at in range(4)], refs[4 * heads :]
    outs, refs = [refs[at * heads : (at + 1) * heads] for at in range(3)], refs[3 * heads :]
    *later, dw_ref, grad_part, bias_ref, turn_ref, dk_sum, dv_sum = refs[: -heads]
    wide = [*refs[-heads:], *later]
    columns = w_o.shape[0]
    weights = mm_tn(spread_ref[...], w_o[...]).astype(LOW)
    span = grads_in[0].shape[0]
    for r in range(PARTS):
        made = mm_nt(grads_in[r][...], weights).astype(LOW)
        for h, out in enumerate(wide):
            out[r * span : (r + 1) * span, :] = made[:, h * WIDE : (h + 1) * WIDE]
        for part in range(PARTS):

            @pl.when(meta[0, PART] == part)
            def _(r=r, part=part):
                grad_part[r] = grads_in[r][:, part * columns : (part + 1) * columns]

    for distance in range(PARTS):
        total = mm_tn(att_in[distance][distance], grad_part[0])
        for r in range(1, PARTS):
            total = total + mm_tn(att_in[distance][r ^ distance], grad_part[r])
        low = pl.multiple_of((meta[0, PART] ^ distance) * columns, columns)
        dw_ref[pl.ds(low, columns), :] = total.astype(LOW)
    turn = Turn(meta, lengths, table_ref, bias_ref, turn_ref, span // 2)
    for h in range(heads):
        q_ref, k_ref, v_ref, lse_ref = (some[h] for some in ins)
        back_head(block, turn, bias_ref, (dk_sum, dv_sum), q_ref, k_ref, v_ref, lse_ref, wide[h], *(o[h] for o in outs))


def place_gate_up(meta, refs, block, target, sems, at):
    half = refs[0].shape[2]
    copies = []
    for side, ref in enumerate(refs):
        low = pl.multiple_of((meta[0, CORE] ^ side) * half, half)
        copy = pltpu.make_async_copy(ref.at[:, block], target.at[:, pl.ds(low, half), :], sems.at[at + side])
        copy.start()
        copies.append(copy)
    return copies, at + 2


def place_down(meta, own, refs, block, target, sems, at):
    count, rows = target.shape[0], target.shape[1]
    half = rows // 2
    low = pl.multiple_of(block * rows, rows)
    copies = [pltpu.make_async_copy(own.at[pl.ds(low, rows), :], target.at[meta[0, DP]], sems.at[at])]
    for number, ref in enumerate(refs):
        distance, side = number % (count - 1) + 1, number // (count - 1)
        low = pl.multiple_of((meta[0, CORE] ^ side) * half, half)
        to = target.at[meta[0, DP] ^ distance, pl.ds(low, half), :]
        copies.append(pltpu.make_async_copy(ref.at[block], to, sems.at[at + 1 + number]))
    for copy in copies:
        copy.start()
    return copies, at + len(copies)


def wait_all(copies):
    for copy in copies:
        copy.wait()


def residual_kernel(pieces, meta, x_ref, w_own, *refs):
    att, w_refs, w_core, refs = refs[:PARTS], refs[PARTS : PARTS + pieces], refs[PARTS + pieces], refs[PARTS + pieces + 1 :]
    residual_out, low_out, vector_out, w_out, w_o, gathered = refs
    columns, rows = att[0].shape[2], w_own.shape[0]
    half, third = rows // 2, rows // 6
    w_o[pl.ds(pl.multiple_of(meta[0, DP] * rows, rows), rows), :] = w_own[...]

    def fill(ref, low):
        w_o[pl.ds(pl.multiple_of(low, half), half), : 3 * columns] = ref[:half, :]
        for g in range(3):
            to = pl.ds(pl.multiple_of(low + g * third, third), third)
            w_o[to, 3 * columns :] = ref[half:, g * columns : (g + 1) * columns]

    for distance, ref in enumerate(w_refs):
        gathered[meta[0, DP] ^ distance] = ref[rows : rows + EXTRA, :]
        if distance:
            low = (meta[0, DP] ^ distance) * rows
            fill(ref[rows + EXTRA :, :], low + meta[0, CORE] * half)
            fill(w_core[distance - 1], low + (1 - meta[0, CORE]) * half)
    vectors = jnp.concatenate([gathered[d][:8, :rows] for d in range(pieces)], axis=1).astype(FULL)
    vector_out[...] = vectors
    residual = x_ref[...].astype(FULL)
    for r in range(PARTS):
        low = pl.multiple_of((meta[0, PART] ^ r) * columns, columns)
        residual = residual + mm(att[r][r], w_o[pl.ds(low, columns), :])
    w_out[...] = w_o[pl.ds(pl.multiple_of(meta[0, PART] * columns, columns), columns), :]
    residual_out[...] = residual
    unit, _ = norm_parts(residual)
    low_out[...] = (unit * vectors[0:1] + vectors[1:2]).astype(LOW)


def feed_kernel(meta, lengths, residual_ref, vectors, cot_ref, cot_got, *refs):
    gu_refs, down_own, down_refs, refs = refs[:2], refs[2], refs[3:-10], refs[-10:]
    grad_ffn_out, grad_branch_out, grad_one_out, own_out, back_out, sums_out, held, gates, ups, sems = refs
    width = residual_ref.shape[1]
    copies, at = [], 0
    for part in range(PARTS):
        gate, at = place_gate_up(meta, gu_refs, part, held.at[part], sems, at)
        up, at = place_gate_up(meta, gu_refs, PARTS + part, held.at[PARTS + part], sems, at)
        down, at = place_down(meta, down_own, down_refs, part, held.at[2 * PARTS + part], sems, at)
        copies.append(gate + up + down)

    def weights(number):
        return held[number].reshape(width, width)

    which = meta[0, WHICH]
    local = cot_got.shape[0]
    unit_one, scale_one = norm_parts(residual_ref[...])
    normed = unit_one * vectors[0:1] + vectors[1:2]
    normed_low = normed.astype(LOW)
    residual = normed

    def pre(part):
        wait_all(copies[part])
        return mm(normed_low, weights(part)), mm(normed_low, weights(PARTS + part))

    ahead = pre(0)
    for part in range(PARTS):
        gate, up = ahead
        if part + 1 < PARTS:
            ahead = pre(part + 1)
        sigma = 0.5 * jnp.tanh(0.5 * gate) + 0.5
        silu = gate * sigma
        residual = residual + mm((silu * up).astype(LOW), weights(2 * PARTS + part))
        gates[part] = up * (sigma + silu * (1.0 - sigma))
        ups[part] = silu
    unit_two, scale_two = norm_parts(residual)
    layer = unit_two * vectors[2:3] + vectors[3:4]
    length = lengths[which, 0]
    upstream = []
    for half, (out, cot) in enumerate(((own_out, cot_ref[which, 0]), (back_out, cot_got[...]))):
        place = meta[0, STARTS + half] + lax.broadcasted_iota(jnp.int32, (local, 1), 0)
        valid = place < length
        out[...] = jnp.where(valid, layer[half * local : (half + 1) * local], 0.0).astype(LOW)
        upstream.append(jnp.where(valid, cot.astype(FULL), 0.0))
    grad_two, sums_two = norm_back(jnp.concatenate(upstream, axis=0), vectors[2:3], unit_two, scale_two)
    grad_ffn = grad_two.astype(LOW)
    grad_ffn_out[...] = grad_ffn
    grad_normed = grad_two
    for part in range(PARTS):
        grad_hidden = mm_nt(grad_ffn, weights(2 * PARTS + part))
        grad_normed = (
            grad_normed
            + mm_nt((grad_hidden * gates[part]).astype(LOW), weights(part))
            + mm_nt((grad_hidden * ups[part]).astype(LOW), weights(PARTS + part))
        )
    grad_one, sums_one = norm_back(grad_normed, vectors[0:1], unit_one, scale_one)
    grad_one_out[...] = grad_one
    grad_branch_out[...] = grad_one.astype(LOW)
    sums_out[...] = jnp.concatenate([*sums_one, *sums_two, jnp.zeros((4, width), FULL)], axis=0)


def hidden_kernel(meta, *refs):
    x_refs, gu_refs, refs = refs[:PARTS], refs[PARTS : PARTS + 2], refs[PARTS + 2 :]
    hidden_out, gate_out, up_out, held_gate, held_up, sems = refs
    part, width = meta[0, PART], hidden_out.shape[1]
    first, at = place_gate_up(meta, gu_refs, part, held_gate, sems, 0)
    second, at = place_gate_up(meta, gu_refs, PARTS + part, held_up, sems, at)
    wait_all(first + second)
    w_gate, w_up = held_gate[...].reshape(width, width), held_up[...].reshape(width, width)
    block = x_refs[0].shape[0]
    for r in range(PARTS):
        rows = slice(r * block, (r + 1) * block)
        x = x_refs[r][...]
        gate, up = mm(x, w_gate), mm(x, w_up)
        sigma = 0.5 * jnp.tanh(0.5 * gate) + 0.5
        silu = gate * sigma
        hidden_out[rows, :] = (silu * up).astype(LOW)
        gate_out[rows, :] = (up * (sigma + silu * (1.0 - sigma))).astype(LOW)
        up_out[rows, :] = silu.astype(LOW)


def split_terms(meta, terms, outs):
    rows = terms.shape[0] // len(outs)
    for distance, out in enumerate(outs):
        low = pl.multiple_of((meta[0, DP] ^ distance) * rows, rows)
        out[:rows, :] = terms[pl.ds(low, rows), :]


def down_kernel(meta, hidden_ref, *refs):
    grads, outs, terms = refs[:PARTS], refs[PARTS:-1], refs[-1]
    block = grads[0].shape[0]
    total = mm_tn(hidden_ref[:block, :], grads[0][...])
    for r in range(1, PARTS):
        total = total + mm_tn(hidden_ref[r * block : (r + 1) * block, :], grads[r][...])
    terms[...] = total.astype(LOW)
    split_terms(meta, terms, outs)


def gate_up_kernel(meta, gate_ref, up_ref, *refs):
    grads, x_refs, down_own, refs = refs[:PARTS], refs[PARTS : 2 * PARTS], refs[2 * PARTS], refs[2 * PARTS + 1 :]
    held, low, terms, sems = refs[-4:]
    count = held.shape[0]
    down_refs, outs = refs[: 2 * count - 2], refs[2 * count - 2 : -4]
    width = terms.shape[0]
    copies, _ = place_down(meta, down_own, down_refs, meta[0, PART], held, sems, 0)
    wait_all(copies)
    w_down = held[...].reshape(terms.shape)
    block = grads[0].shape[0]
    for r in range(PARTS):
        rows = slice(r * block, (r + 1) * block)
        grad_hidden = mm_nt(grads[r][...], w_down)
        low[rows, :width] = (grad_hidden * gate_ref[rows, :].astype(FULL)).astype(LOW)
        low[rows, width:] = (grad_hidden * up_ref[rows, :].astype(FULL)).astype(LOW)
    total = mm_tn(x_refs[0][...], low[:block, :])
    for r in range(1, PARTS):
        total = total + mm_tn(x_refs[r][...], low[r * block : (r + 1) * block, :])
    terms[...] = total[:, :width].astype(LOW)
    split_terms(meta, terms, outs[:-1])
    outs[-1][...] = total[:, width:].astype(LOW)


def last_back_kernel(heads, pieces, block, meta, lengths, table_ref, q_ref, k_ref, v_ref, lse_ref, grad_ref, *refs):
    *refs, dq, dk, dv, bias_ref, turn_ref, dk_sum, dv_sum = refs
    turn = Turn(meta, lengths, table_ref, bias_ref, turn_ref, q_ref.shape[0] // PARTS // 2)
    back_head(block, turn, bias_ref, (dk_sum, dv_sum), q_ref, k_ref, v_ref, lse_ref, grad_ref, dq, dk, dv)
    count = heads - 1
    first = [refs[3 + at * count : 3 + (at + 1) * count] for at in range(3)]
    grads = [ref for some, last in zip(first, (dq, dk, dv)) for ref in (*some, last)]
    projections_back_kernel(heads, pieces, meta, *refs[:3], *grads, *refs[3 + 3 * count :])


def projections_back_kernel(heads, pieces, meta, spread, sums, out_terms, *refs):
    grads, refs = [refs[at * heads : (at + 1) * heads] for at in range(3)], refs[3 * heads :]
    x_refs, w_refs, refs = refs[:PARTS], refs[PARTS : PARTS + pieces], refs[PARTS + pieces :]
    outs, (near_out, far_out, w_all, terms) = refs[:pieces], refs[pieces:]
    rows = w_all.shape[0] // pieces
    for distance, w in enumerate(w_refs):
        w_all[pl.ds(pl.multiple_of((meta[0, DP] ^ distance) * rows, rows), rows), :] = w[:rows, :]
    block = x_refs[0].shape[0]
    columns = w_all.shape[1] // 3
    totals = [None] * 3
    for r in range(PARTS):
        span = slice(r * block, (r + 1) * block)
        x, onward = x_refs[r][...], 0.0
        for at, of_heads in enumerate(grads):
            wide = jnp.concatenate([ref[span, :] for ref in of_heads], axis=1)
            low = mm_nt(wide, spread[...]).astype(LOW)
            term = mm_tn(x, low)
            totals[at] = term if r == 0 else totals[at] + term
            onward = onward + mm_nt(low, w_all[:, at * columns : (at + 1) * columns])
        if r % 2 == 0:
            near_out[r // 2] = onward
        else:
            far_out[r // 2] = onward.astype(LOW)
    for at, total in enumerate(totals):
        terms[:, at * columns : (at + 1) * columns] = total.astype(LOW)
    terms[:, 3 * columns :] = out_terms[...]
    split_terms(meta, terms, outs)
    for distance, out in enumerate(outs):
        out[rows:, :] = jnp.zeros((EXTRA, terms.shape[1]), LOW)
        for block_at in range(pieces):

            @pl.when(meta[0, DP] ^ distance == block_at)
            def _(out=out, block_at=block_at):
                out[rows : rows + 8, :rows] = sums[:, block_at * rows : (block_at + 1) * rows].astype(LOW)


def join_rows_kernel(meta, *refs):
    out = refs[-1]
    rows = refs[0].shape[0]
    for r in range(PARTS):
        low = pl.multiple_of((meta[0, PART] ^ r) * rows, rows)
        out[pl.ds(low, rows), :] = refs[r][...].astype(FULL)


def join_columns_kernel(meta, *refs):
    outs, held = refs[PARTS:-1], refs[-1]
    step = outs[0].shape[0]
    for r in range(PARTS):
        held[meta[0, PART] ^ r] = refs[r][...]
    for at, out in enumerate(outs):
        for part in range(PARTS):
            value = held[part, at].astype(FULL)
            for block in range(value.shape[1] // step):
                start = (block * PARTS + part) * step
                out[:, start : start + step] = value[:, block * step : (block + 1) * step]


def join_projections_kernel(meta, *refs):
    outs, sums_out, held = refs[PARTS:-2], refs[-2], refs[-1]
    rows, columns = outs[0].shape[0], refs[0].shape[1] // len(outs)
    for r in range(PARTS):
        held[meta[0, PART] ^ r] = refs[r][...]
    sums = jnp.zeros((8, rows), FULL)
    for part in range(PARTS):
        value = held[part].astype(FULL)
        for at, out in enumerate(outs):
            out[:, part * columns : (part + 1) * columns] = value[:rows, at * columns : (at + 1) * columns]
        sums = sums + value[rows : rows + 8, :rows]
    sums_out[...] = sums


def gather_pieces(own, bits, starts=None, gate=None):
    held = {0: own}
    for bit in bits:
        for distance in list(held):
            source = held[distance]
            if distance == 0 and starts is not None:
                source = after(source, *starts)
            elif distance != 0 and gate is not None:
                source = after(source, gate)
            held[distance | bit] = hop(source, "dp", bit)
    return [held[distance] for distance in range(len(held))]


def send_terms(chunks, gate=None):
    return [
        hop(chunk if gate is None else after(chunk, *gate), "dp", distance)
        for distance, chunk in enumerate(chunks)
        if distance
    ]


def sum_terms(chunks, got):
    total = chunks[0].astype(FULL)
    for one in got:
        total = total + one.astype(FULL)
    return total


def shards(
    tokens, lengths, w_query, w_key, w_value, w_output, w_gate, w_up, w_down,
    first_gain, first_bias, second_gain, second_bias, cotangent,
):
    _, _, local, width = tokens.shape
    dp_count, blk_count = lax.axis_size("dp"), lax.axis_size("blk")
    dp, blk = lax.axis_index("dp"), lax.axis_index("blk")
    side = blk_count // 2
    which = blk // side
    first = which == 0
    core, part = blk % 2, blk % PARTS
    heads = width // HEAD_DIM // PARTS
    columns = heads * HEAD_DIM
    rows, ff_rows = w_query.shape[0], w_down.shape[0]
    half, ff = rows // 2, w_gate.shape[1]
    block = 2 * local
    row_count = PARTS * block
    spread_bits = bits_between(PARTS, side)
    sum_bits = bits_between(PARTS, blk_count)
    dp_bits = bits_between(1, dp_count)
    back_bits = dp_bits[::-1]
    table = jnp.asarray(turn_table(local * blk_count))
    swap_q, swap_k, spread_v = (
        jnp.asarray(swap_matrix(heads, 3 * columns, at * columns, at < 2), LOW) for at in range(3)
    )
    spread = jnp.asarray(swap_matrix(heads, columns, 0, False), LOW)

    starts = [(blk ^ distance ^ away) * local for distance in range(side) for away in (0, side)]
    meta = jnp.stack([which, core, part, dp, *starts]).astype(jnp.int32).reshape(1, -1)

    gate_up_own = call(
        pack_second_kernel, [shape((2 * PARTS, half, width))], [SMEM] + [VMEM] * 2, [], meta, w_gate, w_up
    )[0]
    gate_up_core = lax.all_gather(gate_up_own, "dp", axis=0, tiled=False)
    tok_send, cot_send, qkv_own, down_own = call(
        pack_first_kernel,
        [shape((local, width)), shape((local, width)), shape((rows + EXTRA + half + half // 3, 3 * columns))]
        + [shape((PARTS, half, width))],
        [SMEM] + [VMEM] * 11, [], after(meta, gate_up_own), tokens, cotangent, w_query, w_key, w_value, w_output, w_down,
        first_gain, first_bias, second_gain, second_bias,
    )
    tok_got = hop(tok_send, "blk", side)
    qkv = gather_pieces(qkv_own, dp_bits)
    x_own = jnp.concatenate([jnp.where(first, tokens[0, 0], tokens[1, 0]), tok_got])
    x_core, x_near = hop(x_own, "blk", 1), hop(x_own, "blk", 2)
    x_far = hop(after(x_near, x_core, *(qkv[bit] for bit in dp_bits)), "blk", 1)
    x_all = [x_own, x_core, x_near, x_far]
    down_pieces = {0: down_own}
    for bit in dp_bits[:2]:
        down_pieces[bit] = hop(after(down_own, *qkv[1:]), "dp", bit)
    cot_got = hop(after(cot_send, x_near), "blk", side)

    wide_shape = shape((row_count, WIDE))
    made = call(
        functools.partial(project_kernel, heads, dp_count), [wide_shape] * (3 * heads),
        [SMEM] + [VMEM] * (4 + PARTS + dp_count),
        [pltpu.VMEM((width, 3 * columns), LOW), pltpu.VMEM((row_count, 2 * WIDE), FULL)],
        after(meta, cot_got), table, swap_q, swap_k, spread_v, *x_all, *qkv,
    )
    queries, keys, values = (made[at * heads : (at + 1) * heads] for at in range(3))
    out_rows = rows + EXTRA
    qkv_core = hop(after(jnp.stack([piece[out_rows:] for piece in qkv[1:]]), queries[0]), "blk", 1)
    for bit in spread_bits:
        keys, values = ([jnp.concatenate([one, hop(one, "blk", bit)]) for one in many] for many in (keys, values))
    key_count = keys[0].shape[0]
    q_block = max(WIDE, min(row_count, 512 * 1024 // key_count))
    attended = call(
        functools.partial(attend_kernel, heads, q_block),
        [shape((PARTS, block, columns))] + [shape((1, row_count), FULL)] * heads,
        [SMEM] * 2 + [VMEM] * (1 + 3 * heads),
        [pltpu.VMEM((row_count, heads * WIDE), LOW)],
        meta, lengths, *queries, *keys, *values, spread,
    )
    attended, lse = attended[0], attended[1:]
    att_send = after(attended, qkv_core, *(down_pieces[bit] for bit in dp_bits[:2]))
    att_core, att_near = hop(att_send, "blk", 1), hop(att_send, "blk", 2)
    att_all = [attended, att_core, att_near, hop(after(att_near, att_core), "blk", 1)]
    residual_one, normed_low, all_vectors, w_o = call(
        functools.partial(residual_kernel, dp_count),
        [shape((block, width), FULL), shape((block, width)), shape((8, width), FULL), shape((columns, width))],
        [SMEM] + [VMEM] * (2 + PARTS + dp_count + 1),
        [pltpu.VMEM((width, width), LOW), pltpu.VMEM((dp_count, EXTRA, 3 * columns), LOW)],
        meta, x_own, w_output, *att_all, *qkv, qkv_core,
    )
    normed_core, normed_near = hop(normed_low, "blk", 1), hop(normed_low, "blk", 2)
    middle = PARTS // 2
    down_pieces[3] = jnp.concatenate(
        [hop(down_pieces[1][:middle], "dp", 2), hop(down_pieces[2][middle:], "dp", 1)]
    )
    for bit in dp_bits[2:]:
        for distance in range(bit):
            down_pieces[distance | bit] = hop(down_pieces[distance], "dp", bit)
    down_pieces = [down_pieces[distance] for distance in range(dp_count)]
    down_core = [hop(after(piece, normed_low), "blk", 1) for piece in down_pieces[1:]]
    down_all = (w_down, *down_pieces[1:], *down_core)
    gate_up_all = (gate_up_core, hop(after(gate_up_core, normed_core), "blk", 1))

    part_shape, w_shape = (PARTS, block, width), (dp_count, rows, width)
    down_copies = 2 * dp_count - 1
    grad_ffn, grad_branch, grad_one, layer_own, layer_back, sums = call(
        feed_kernel,
        [shape((block, width))] * 2 + [shape((block, width), FULL)] + [shape((local, width))] * 2
        + [shape((8, width), FULL)],
        [SMEM] * 2 + [VMEM] * 4 + [ANY] * (2 + len(down_all)),
        [
            pltpu.VMEM((3 * PARTS, *w_shape), LOW),
            pltpu.VMEM(part_shape, FULL),
            pltpu.VMEM(part_shape, FULL),
            pltpu.SemaphoreType.DMA((PARTS * (4 + down_copies),)),
        ],
        after(meta, normed_core), lengths, residual_one, all_vectors, cotangent, cot_got, *gate_up_all, *down_all,
    )
    ffn_core, ffn_near = hop(grad_ffn, "blk", 1), hop(grad_ffn, "blk", 2)
    normed_all = [normed_low, normed_core, normed_near, hop(after(normed_near, grad_ffn), "blk", 1)]

    long, chunk = shape((row_count, width)), shape((rows, width))
    hidden, gate_factor, up_factor = call(
        hidden_kernel, [long] * 3,
        [SMEM] + [VMEM] * PARTS + [ANY] * 2,
        [pltpu.VMEM(w_shape, LOW), pltpu.VMEM(w_shape, LOW), pltpu.SemaphoreType.DMA((4,))],
        after(meta, grad_ffn), *normed_all, *gate_up_all,
    )
    ffn_all = [grad_ffn, ffn_core, ffn_near, hop(after(ffn_near, hidden, ffn_core), "blk", 1)]
    branch_core, branch_near = (hop(after(grad_branch, ffn_near, hidden), "blk", bit) for bit in (1, 2))
    down_terms = call(
        down_kernel, [chunk] * dp_count, [SMEM] + [VMEM] * (1 + PARTS), [pltpu.VMEM((width, width), LOW)],
        after(meta, branch_core), hidden, *ffn_all,
    )
    down_got = send_terms(down_terms)
    gate_up_terms = call(
        gate_up_kernel, [chunk] * dp_count + [shape((width, width))],
        [SMEM] + [VMEM] * (2 + 2 * PARTS) + [ANY] * len(down_all),
        [pltpu.VMEM(w_shape, LOW), pltpu.VMEM((row_count, 2 * width), LOW)]
        + [pltpu.VMEM((width, width), LOW), pltpu.SemaphoreType.DMA((down_copies,))],
        after(meta, down_terms[0]), gate_factor, up_factor, *ffn_all, *normed_all, *down_all,
    )

    def sum_halves(total):
        for bit in sum_bits:
            low = total.astype(LOW)
            total = low.astype(FULL) + hop(low, "blk", bit).astype(FULL)
        return total.astype(LOW)

    branch_far = hop(after(branch_near, gate_up_terms[0], *(down_got[bit - 1] for bit in dp_bits)), "blk", 1)
    layer_got = hop(after(layer_back, branch_far), "blk", side)
    down_sum = sum_terms(down_terms, down_got)
    down_full = sum_halves(down_sum)
    gate_got = send_terms(gate_up_terms[:dp_count])
    up_sum = lax.psum_scatter(
        after(gate_up_terms[-1], branch_far).reshape(dp_count, rows, width), "dp", scatter_dimension=0, tiled=False
    )
    early = heads if spread_bits else heads - 1
    key_shape = shape((key_count, WIDE))
    back_scratch = [pltpu.VMEM((key_count, WIDE), FULL), pltpu.VMEM((key_count, 2 * WIDE), FULL)]
    back_scratch += [pltpu.VMEM((key_count, WIDE), FULL)] * 2
    *made, out_terms = call(
        functools.partial(attend_back_kernel, early, q_block),
        [wide_shape] * early + [key_shape] * (2 * early) + [wide_shape] * (heads - early) + [shape((width, columns))],
        [SMEM] * 2 + [VMEM] * (3 + 2 * PARTS + 4 * early),
        [pltpu.VMEM((PARTS, block, columns), LOW), *back_scratch] + [pltpu.VMEM((row_count, WIDE), LOW)] * early,
        after(meta, down_sum), lengths, w_o, spread, table,
        grad_branch, branch_core, branch_near, branch_far, *att_all,
        *queries[:early], *keys[:early], *values[:early], *lse[:early],
    )
    grad_q, grad_k, grad_v = (made[at * early : (at + 1) * early] for at in range(3))
    gate_sum = sum_terms(gate_up_terms, [after(got, grad_q[0], layer_got) for got in gate_got])
    gate_full = sum_halves(gate_sum)
    down_near = hop(down_full, "blk", 2)
    for bit in reversed(spread_bits):
        middle = grad_k[0].shape[0] // 2
        grad_k, grad_v = (
            [
                (one[:middle].astype(FULL) + hop(one[middle:], "blk", bit).astype(FULL)).astype(LOW)
                for one in many
            ]
            for many in (grad_k, grad_v)
        )
    back_outs = [shape((rows + EXTRA, width))] * dp_count + [shape((2, block, width), FULL), shape((2, block, width))]
    back_weights = [pltpu.VMEM((width, 3 * columns), LOW), pltpu.VMEM((width, width), LOW)]
    back_operands = (spread, sums, out_terms, *grad_q, *grad_k, *grad_v, *x_all, *qkv)
    ready = after(meta, gate_sum, down_full)
    if spread_bits:
        made = call(
            functools.partial(projections_back_kernel, heads, dp_count), back_outs,
            [SMEM] + [VMEM] * len(back_operands), back_weights, ready, *back_operands,
        )
    else:
        made = call(
            functools.partial(last_back_kernel, heads, dp_count, q_block), back_outs,
            [SMEM] * 2 + [VMEM] * (6 + len(back_operands)),
            back_weights + [pltpu.VMEM((row_count, WIDE), LOW)] * 3 + back_scratch,
            ready, lengths, table, queries[-1], keys[-1], values[-1], lse[-1], made[-1], *back_operands,
        )
    *qkv_terms, token_keep, token_send = made
    up_sum = after(up_sum, token_keep).astype(FULL)

    first_gate = (gate_full, up_sum, down_near)
    token_got = hop(after(token_send, *first_gate), "blk", 1).astype(FULL)
    up_full = sum_halves(up_sum)
    near_send = (token_keep[1] + token_got[1]).astype(LOW)
    token_near = hop(near_send, "blk", 2)
    qkv_got = send_terms(qkv_terms)
    qkv_sum = sum_terms(qkv_terms, [after(got, token_near) for got in qkv_got]).astype(LOW)
    qkv_full = sum_halves(after(qkv_sum, up_full, token_near))
    pair_full = after(jnp.stack([gate_full, up_full]), qkv_sum)
    pair_core, pair_near = hop(pair_full, "blk", 1), hop(pair_full, "blk", 2)
    down_core, down_far = (hop(after(one, pair_core), "blk", 1) for one in (down_full, down_near))
    grad_rows = after(grad_one, qkv_sum) + token_keep[0] + token_got[0] + token_near.astype(FULL)
    rows_got = hop(grad_rows[local:].astype(LOW), "blk", side).astype(FULL)
    grad_down = call(
        join_rows_kernel, [shape((ff_rows, width), FULL)], [SMEM] + [VMEM] * PARTS, [],
        meta, down_full, down_core, down_near, down_far,
    )[0]
    pair_far = hop(after(pair_near, pair_core, grad_down), "blk", 1)
    qkv_core, qkv_near = (hop(after(qkv_full, pair_near), "blk", bit) for bit in (1, 2))
    grad_gate, grad_up = call(
        join_columns_kernel, [shape((rows, ff), FULL)] * 2, [SMEM] + [VMEM] * PARTS,
        [pltpu.VMEM((PARTS, 2, rows, width), LOW)], meta, pair_full, pair_core, pair_near, pair_far,
    )
    qkv_far = hop(after(qkv_near, qkv_core, grad_gate, rows_got), "blk", 1)
    grad_tokens = jnp.where(
        first, jnp.stack([grad_rows[:local], rows_got]), jnp.stack([rows_got, grad_rows[:local]])
    )[:, None]
    layer_out = jnp.where(first, jnp.stack([layer_own, layer_got]), jnp.stack([layer_got, layer_own]))[:, None]
    grad_query, grad_key, grad_value, grad_output, vector_sums = call(
        join_projections_kernel, [shape((rows, width), FULL)] * 4 + [shape((8, rows), FULL)],
        [SMEM] + [VMEM] * PARTS, [pltpu.VMEM((PARTS, rows + EXTRA, width), LOW)], meta, qkv_full, qkv_core, qkv_near, qkv_far,
    )
    return (
        layer_out, grad_tokens, grad_query, grad_key, grad_value, grad_output, grad_gate, grad_up, grad_down,
        vector_sums[0], vector_sums[1], vector_sums[2], vector_sums[3],
    )


def solution(mesh):
    slots = P(None, "dp", "blk", None)
    matrix, vector = P("dp", None), P("dp")
    return jax.shard_map(
        shards,
        mesh=mesh,
        in_specs=(slots, P(None, "dp")) + (matrix,) * 7 + (vector,) * 4 + (slots,),
        out_specs=(slots, slots) + (matrix,) * 7 + (vector,) * 4,
        check_vma=False,
    )
```

```python
import functools

import jax
import jax.numpy as jnp
import numpy as np
from jax import lax
from jax.experimental import pallas as pl
from jax.experimental.pallas import tpu as pltpu
from jax.sharding import PartitionSpec as P

HEAD_DIM = 64
WIDE = 128
PARTS = 4
EXTRA = 16
LOW, FULL = jnp.bfloat16, jnp.float32
VMEM_MIB = {"hidden_kernel": 40, "down_kernel": 40, "gate_up_kernel": 40}
VMEM = pl.BlockSpec(memory_space=pltpu.VMEM)
SMEM = pl.BlockSpec(memory_space=pltpu.SMEM)
ANY = pl.BlockSpec(memory_space=pl.ANY)
WHICH, CORE, PART, DP, STARTS = 0, 1, 2, 3, 4


def mm(left, right):
    return jnp.dot(left, right, preferred_element_type=FULL)


def mm_nt(left, right):
    return lax.dot_general(left, right, (((1,), (1,)), ((), ())), preferred_element_type=FULL)


def mm_tn(left, right):
    return lax.dot_general(left, right, (((0,), (0,)), ((), ())), preferred_element_type=FULL)


def hop(value, axis, bit):
    size = lax.axis_size(axis)
    return lax.ppermute(value, axis, [(at, at ^ bit) for at in range(size)])


def after(value, *others):
    return lax.optimization_barrier((value, *others))[0]


def bits_between(low, high):
    bits = []
    while low < high:
        bits.append(low)
        low *= 2
    return bits


def turn_table(seq_len):
    half = HEAD_DIM // 2
    frequency = np.float32(1000.0) ** (
        -(np.arange(half, dtype=np.float32) * np.float32(2.0) / np.float32(HEAD_DIM))
    )
    angles = np.arange(seq_len, dtype=np.float32)[:, None] * frequency[None, :]
    cosine = np.cos(angles).astype(np.float32)
    sine = np.sin(angles).astype(np.float32)
    return np.concatenate([cosine] * 4 + [sine, sine, -sine, -sine], axis=1)


def swap_matrix(heads, total, first, swapped):
    half = HEAD_DIM // 2
    out = np.zeros((total, heads * WIDE), np.float32)
    for h in range(heads):
        for f in range(HEAD_DIM):
            out[first + h * HEAD_DIM + f, h * WIDE + f] = 1.0
        for f in range(half if swapped else 0):
            out[first + h * HEAD_DIM + half + f, h * WIDE + HEAD_DIM + f] = -1.0
            out[first + h * HEAD_DIM + f, h * WIDE + HEAD_DIM + half + f] = 1.0
    return out


def call(body, outs, in_specs, scratch, *operands):
    name = getattr(body, "func", body).__name__
    return pl.pallas_call(
        body,
        out_shape=outs,
        in_specs=in_specs,
        out_specs=[VMEM] * len(outs),
        scratch_shapes=scratch,
        name=getattr(body, "func", body).__name__,
        compiler_params=pltpu.CompilerParams(vmem_limit_bytes=VMEM_MIB.get(name, 60) * 1024 * 1024),
        cost_estimate=pl.CostEstimate(flops=1000, bytes_accessed=1000, transcendentals=0),
    )(*operands)


def shape(dims, dtype=LOW):
    return jax.ShapeDtypeStruct(dims, dtype)


def norm_parts(rows):
    centred = rows - jnp.mean(rows, axis=-1, keepdims=True)
    scale = lax.rsqrt(jnp.mean(centred * centred, axis=-1, keepdims=True) + 1e-05)
    return centred * scale, scale


def norm_back(upstream, gain, unit, scale):
    inner = upstream * gain
    centre = jnp.mean(inner, axis=-1, keepdims=True)
    along = jnp.mean(inner * unit, axis=-1, keepdims=True)
    sums = (jnp.sum(upstream * unit, axis=0, keepdims=True), jnp.sum(upstream, axis=0, keepdims=True))
    return (inner - centre - unit * along) * scale, sums


def pack_first_kernel(
    meta, tokens, cot, w_q, w_k, w_v, w_o, w_down, gain_one, bias_one, gain_two, bias_two, tok_out, cot_out, qkv_out, down_out
):
    rows, columns = w_q.shape[0], qkv_out.shape[1] // 3
    half, third = rows // 2, rows // 6
    other = 1 - meta[0, WHICH]
    tok_out[...] = tokens[other, 0]
    cot_out[...] = cot[other, 0]
    for part in range(PARTS):

        @pl.when(meta[0, PART] == part)
        def _(part=part):
            for at, w in enumerate((w_q, w_k, w_v)):
                qkv_out[:rows, at * columns : (at + 1) * columns] = w[:, part * columns : (part + 1) * columns]

    qkv_out[rows : rows + EXTRA, :] = jnp.zeros((EXTRA, 3 * columns), LOW)
    for at, vector in enumerate((gain_one, bias_one, gain_two, bias_two)):
        qkv_out[rows + at : rows + at + 1, :rows] = vector[...].reshape(1, rows)
    for part in range(PARTS):
        low = pl.multiple_of(part * rows + meta[0, CORE] * half, half)
        down_out[part] = w_down[pl.ds(low, half), :]
    out_rows = w_o[pl.ds(pl.multiple_of(meta[0, CORE] * half, half), half), :]
    at = rows + EXTRA
    qkv_out[at : at + half, :] = out_rows[:, : 3 * columns]
    at += half
    for g in range(3):
        qkv_out[at : at + third, g * columns : (g + 1) * columns] = out_rows[g * third : (g + 1) * third, 3 * columns :]


def pack_second_kernel(meta, w_gate, w_up, out):
    half, width = out.shape[1], out.shape[2]
    step = 2 * half
    low = pl.multiple_of(meta[0, CORE] * half, half)
    for base, w in ((0, w_gate), (PARTS, w_up)):
        for part in range(PARTS):
            for block in range(width // step):
                start = (block * PARTS + part) * step
                out[base + part, :, block * step : (block + 1) * step] = w[pl.ds(low, half), start : start + step]


def project_kernel(heads, pieces, meta, table_ref, swap_q, swap_k, spread_v, *refs):
    x_refs, w_refs, (q_refs, k_refs, v_refs) = refs[:PARTS], refs[PARTS : PARTS + pieces], [refs[-2 - 3 * heads + at * heads : -2 - 2 * heads + at * heads] for at in range(3)]
    w_all, turn = refs[-2:]
    rows = w_all.shape[0] // pieces
    block = x_refs[0].shape[0]
    local = block // 2
    for distance, w in enumerate(w_refs):
        w_all[pl.ds(pl.multiple_of((meta[0, DP] ^ distance) * rows, rows), rows), :] = w[:rows, :]
    for at in range(2 * PARTS):
        start = pl.multiple_of(meta[0, STARTS + at], local)
        turn[at * local : (at + 1) * local, :] = table_ref[pl.ds(start, local), :]
    weights = w_all[...]
    w_q, w_k, w_v = (mm(weights, m[...]).astype(LOW) for m in (swap_q, swap_k, spread_v))
    for r in range(PARTS):
        out_rows = slice(r * block, (r + 1) * block)
        x = x_refs[r][...]
        cosine, sine = turn[out_rows, :WIDE], turn[out_rows, WIDE:]
        for out_refs, w, scale in ((q_refs, w_q, 0.0625), (k_refs, w_k, None)):
            made = mm(x, w)
            for h in range(heads):
                one = made[:, h * WIDE : (h + 1) * WIDE]
                turned = (one * cosine + pltpu.roll(one, HEAD_DIM, 1) * sine).astype(LOW)
                out_refs[h][out_rows, :] = turned if scale is None else turned * jnp.asarray(scale, LOW)
        made = mm(x, w_v).astype(LOW)
        for h in range(heads):
            v_refs[h][out_rows, :] = made[:, h * WIDE : (h + 1) * WIDE]


def fill_bias(meta, length, bias_ref, local):
    for at in range(bias_ref.shape[0] // local):
        place = meta[0, STARTS + at] + lax.broadcasted_iota(jnp.int32, (local, WIDE), 0)
        bias_ref[at * local : (at + 1) * local, :] = jnp.where(place < length, 0.0, -1e30)


def each_block(count, step):
    if count <= 4:
        for number in range(count):
            step(number)
    else:
        lax.fori_loop(0, count, lambda number, carry: step(number) or carry, 0)


def block_rows(number, block):
    if isinstance(number, int):
        return slice(number * block, (number + 1) * block)
    return pl.ds(pl.multiple_of(number * block, block), block)


def attend_kernel(heads, block, meta, lengths, *refs):
    q_refs, k_refs, v_refs, spread_ref = refs[:heads], refs[heads : 2 * heads], refs[2 * heads : 3 * heads], refs[3 * heads]
    out, lse_refs, wide_ref = refs[3 * heads + 1], refs[-1 - heads : -1], refs[-1]
    row_count, key_count = q_refs[0].shape[0], k_refs[0].shape[0]
    span = row_count // PARTS
    local = span // 2
    length = lengths[meta[0, WHICH], 0]
    places = [meta[0, STARTS + at] + lax.broadcasted_iota(jnp.int32, (1, local), 1) for at in range(key_count // local)]
    bias = jnp.where(jnp.concatenate(places, axis=1) < length, 0.0, -1e30)
    for h in range(heads):

        def step(number, h=h):
            rows = block_rows(number, block)
            scores = mm_nt(q_refs[h][rows, :], k_refs[h][...]) + bias
            top = jnp.max(scores, axis=1, keepdims=True)
            weights = jnp.exp(scores - top)
            total = jnp.sum(weights, axis=1, keepdims=True)
            wide_ref[rows, h * WIDE : (h + 1) * WIDE] = (mm(weights.astype(LOW), v_refs[h][...]) / total).astype(LOW)
            lse_refs[h][:, rows] = jnp.broadcast_to(top + jnp.log(total), (block, WIDE)).T[:1, :]

        each_block(row_count // block, step)
    for r in range(PARTS):
        out[r] = mm_nt(wide_ref[r * span : (r + 1) * span, :], spread_ref[...]).astype(LOW)


class Turn:
    def __init__(self, meta, lengths, table_ref, bias_ref, turn, local):
        fill_bias(meta, lengths[meta[0, WHICH], 0], bias_ref, local)
        for at in range(turn.shape[0] // local):
            start = pl.multiple_of(meta[0, STARTS + at], local)
            turn[at * local : (at + 1) * local, :] = table_ref[pl.ds(start, local), :]
        self.turn = turn

    def back(self, value, rows):
        cosine, sine = self.turn[rows, :WIDE], self.turn[rows, WIDE:]
        return (value * cosine - pltpu.roll(value, HEAD_DIM, 1) * sine).astype(LOW)


def back_head(block, turn, bias_ref, sums, q_ref, k_ref, v_ref, lse_ref, grad_ref, dq_ref, dk_ref, dv_ref):
    dk_sum, dv_sum = sums
    keys, values = k_ref[...], v_ref[...]
    keys_t = keys.T
    dk_sum[...] = jnp.zeros_like(dk_sum)
    dv_sum[...] = jnp.zeros_like(dv_sum)

    def step(number):
        rows = block_rows(number, block)
        bias = jnp.concatenate([bias_ref[...]] * (block // WIDE), axis=1)
        queries, grads = q_ref[rows, :], grad_ref[rows, :]
        probs = jnp.exp(mm_nt(keys, queries) + bias - lse_ref[:, rows])
        grad_probs = mm_nt(values, grads)
        delta = jnp.sum(probs * grad_probs, axis=0, keepdims=True)
        grad_scores = (probs * (grad_probs - delta)).astype(LOW)
        dv_sum[...] += mm(probs.astype(LOW), grads)
        dk_sum[...] += mm(grad_scores, queries)
        dq_ref[rows, :] = turn.back(mm(keys_t, grad_scores).T * 0.125, rows)

    each_block(q_ref.shape[0] // block, step)
    dk_ref[...] = turn.back(dk_sum[...] * 2.0, slice(None))
    dv_ref[...] = dv_sum[...].astype(LOW)


def attend_back_kernel(heads, block, meta, lengths, w_o, spread_ref, table_ref, *refs):
    grads_in, att_in, refs = refs[:PARTS], refs[PARTS : 2 * PARTS], refs[2 * PARTS :]
    ins, refs = [refs[at * heads : (at + 1) * heads] for at in range(4)], refs[4 * heads :]
    outs, refs = [refs[at * heads : (at + 1) * heads] for at in range(3)], refs[3 * heads :]
    *later, dw_ref, grad_part, bias_ref, turn_ref, dk_sum, dv_sum = refs[: -heads]
    wide = [*refs[-heads:], *later]
    columns = w_o.shape[0]
    weights = mm_tn(spread_ref[...], w_o[...]).astype(LOW)
    span = grads_in[0].shape[0]
    for r in range(PARTS):
        made = mm_nt(grads_in[r][...], weights).astype(LOW)
        for h, out in enumerate(wide):
            out[r * span : (r + 1) * span, :] = made[:, h * WIDE : (h + 1) * WIDE]
        for part in range(PARTS):

            @pl.when(meta[0, PART] == part)
            def _(r=r, part=part):
                grad_part[r] = grads_in[r][:, part * columns : (part + 1) * columns]

    for distance in range(PARTS):
        total = mm_tn(att_in[distance][distance], grad_part[0])
        for r in range(1, PARTS):
            total = total + mm_tn(att_in[distance][r ^ distance], grad_part[r])
        low = pl.multiple_of((meta[0, PART] ^ distance) * columns, columns)
        dw_ref[pl.ds(low, columns), :] = total.astype(LOW)
    turn = Turn(meta, lengths, table_ref, bias_ref, turn_ref, span // 2)
    for h in range(heads):
        q_ref, k_ref, v_ref, lse_ref = (some[h] for some in ins)
        back_head(block, turn, bias_ref, (dk_sum, dv_sum), q_ref, k_ref, v_ref, lse_ref, wide[h], *(o[h] for o in outs))


def place_gate_up(meta, refs, block, target, sems, at):
    half = refs[0].shape[2]
    copies = []
    for side, ref in enumerate(refs):
        low = pl.multiple_of((meta[0, CORE] ^ side) * half, half)
        copy = pltpu.make_async_copy(ref.at[:, block], target.at[:, pl.ds(low, half), :], sems.at[at + side])
        copy.start()
        copies.append(copy)
    return copies, at + 2


def place_down(meta, own, refs, block, target, sems, at):
    count, rows = target.shape[0], target.shape[1]
    half = rows // 2
    low = pl.multiple_of(block * rows, rows)
    copies = [pltpu.make_async_copy(own.at[pl.ds(low, rows), :], target.at[meta[0, DP]], sems.at[at])]
    for number, ref in enumerate(refs):
        distance, side = number % (count - 1) + 1, number // (count - 1)
        low = pl.multiple_of((meta[0, CORE] ^ side) * half, half)
        to = target.at[meta[0, DP] ^ distance, pl.ds(low, half), :]
        copies.append(pltpu.make_async_copy(ref.at[block], to, sems.at[at + 1 + number]))
    for copy in copies:
        copy.start()
    return copies, at + len(copies)


def wait_all(copies):
    for copy in copies:
        copy.wait()


def residual_kernel(pieces, meta, x_ref, w_own, *refs):
    att, w_refs, w_core, refs = refs[:PARTS], refs[PARTS : PARTS + pieces], refs[PARTS + pieces], refs[PARTS + pieces + 1 :]
    residual_out, low_out, vector_out, w_out, w_o, gathered = refs
    columns, rows = att[0].shape[2], w_own.shape[0]
    half, third = rows // 2, rows // 6
    w_o[pl.ds(pl.multiple_of(meta[0, DP] * rows, rows), rows), :] = w_own[...]

    def fill(ref, low):
        w_o[pl.ds(pl.multiple_of(low, half), half), : 3 * columns] = ref[:half, :]
        for g in range(3):
            to = pl.ds(pl.multiple_of(low + g * third, third), third)
            w_o[to, 3 * columns :] = ref[half:, g * columns : (g + 1) * columns]

    for distance, ref in enumerate(w_refs):
        gathered[meta[0, DP] ^ distance] = ref[rows : rows + EXTRA, :]
        if distance:
            low = (meta[0, DP] ^ distance) * rows
            fill(ref[rows + EXTRA :, :], low + meta[0, CORE] * half)
            fill(w_core[distance - 1], low + (1 - meta[0, CORE]) * half)
    vectors = jnp.concatenate([gathered[d][:8, :rows] for d in range(pieces)], axis=1).astype(FULL)
    vector_out[...] = vectors
    residual = x_ref[...].astype(FULL)
    for r in range(PARTS):
        low = pl.multiple_of((meta[0, PART] ^ r) * columns, columns)
        residual = residual + mm(att[r][r], w_o[pl.ds(low, columns), :])
    w_out[...] = w_o[pl.ds(pl.multiple_of(meta[0, PART] * columns, columns), columns), :]
    residual_out[...] = residual
    unit, _ = norm_parts(residual)
    low_out[...] = (unit * vectors[0:1] + vectors[1:2]).astype(LOW)


def feed_kernel(meta, lengths, residual_ref, vectors, cot_ref, cot_got, *refs):
    gu_refs, down_own, down_refs, refs = refs[:2], refs[2], refs[3:-10], refs[-10:]
    grad_ffn_out, grad_branch_out, grad_one_out, own_out, back_out, sums_out, held, gates, ups, sems = refs
    width = residual_ref.shape[1]
    copies, at = [], 0
    for part in range(PARTS):
        gate, at = place_gate_up(meta, gu_refs, part, held.at[part], sems, at)
        up, at = place_gate_up(meta, gu_refs, PARTS + part, held.at[PARTS + part], sems, at)
        down, at = place_down(meta, down_own, down_refs, part, held.at[2 * PARTS + part], sems, at)
        copies.append(gate + up + down)

    def weights(number):
        return held[number].reshape(width, width)

    which = meta[0, WHICH]
    local = cot_got.shape[0]
    unit_one, scale_one = norm_parts(residual_ref[...])
    normed = unit_one * vectors[0:1] + vectors[1:2]
    normed_low = normed.astype(LOW)
    residual = normed

    def pre(part):
        wait_all(copies[part])
        return mm(normed_low, weights(part)), mm(normed_low, weights(PARTS + part))

    ahead = pre(0)
    for part in range(PARTS):
        gate, up = ahead
        if part + 1 < PARTS:
            ahead = pre(part + 1)
        sigma = 0.5 * jnp.tanh(0.5 * gate) + 0.5
        silu = gate * sigma
        residual = residual + mm((silu * up).astype(LOW), weights(2 * PARTS + part))
        gates[part] = up * (sigma + silu * (1.0 - sigma))
        ups[part] = silu
    unit_two, scale_two = norm_parts(residual)
    layer = unit_two * vectors[2:3] + vectors[3:4]
    length = lengths[which, 0]
    upstream = []
    for half, (out, cot) in enumerate(((own_out, cot_ref[which, 0]), (back_out, cot_got[...]))):
        place = meta[0, STARTS + half] + lax.broadcasted_iota(jnp.int32, (local, 1), 0)
        valid = place < length
        out[...] = jnp.where(valid, layer[half * local : (half + 1) * local], 0.0).astype(LOW)
        upstream.append(jnp.where(valid, cot.astype(FULL), 0.0))
    grad_two, sums_two = norm_back(jnp.concatenate(upstream, axis=0), vectors[2:3], unit_two, scale_two)
    grad_ffn = grad_two.astype(LOW)
    grad_ffn_out[...] = grad_ffn
    grad_normed = grad_two
    for part in range(PARTS):
        grad_hidden = mm_nt(grad_ffn, weights(2 * PARTS + part))
        grad_normed = (
            grad_normed
            + mm_nt((grad_hidden * gates[part]).astype(LOW), weights(part))
            + mm_nt((grad_hidden * ups[part]).astype(LOW), weights(PARTS + part))
        )
    grad_one, sums_one = norm_back(grad_normed, vectors[0:1], unit_one, scale_one)
    grad_one_out[...] = grad_one
    grad_branch_out[...] = grad_one.astype(LOW)
    sums_out[...] = jnp.concatenate([*sums_one, *sums_two, jnp.zeros((4, width), FULL)], axis=0)


def hidden_kernel(meta, *refs):
    x_refs, gu_refs, refs = refs[:PARTS], refs[PARTS : PARTS + 2], refs[PARTS + 2 :]
    hidden_out, gate_out, up_out, held_gate, held_up, sems = refs
    part, width = meta[0, PART], hidden_out.shape[1]
    first, at = place_gate_up(meta, gu_refs, part, held_gate, sems, 0)
    second, at = place_gate_up(meta, gu_refs, PARTS + part, held_up, sems, at)
    wait_all(first + second)
    w_gate, w_up = held_gate[...].reshape(width, width), held_up[...].reshape(width, width)
    block = x_refs[0].shape[0]
    for r in range(PARTS):
        rows = slice(r * block, (r + 1) * block)
        x = x_refs[r][...]
        gate, up = mm(x, w_gate), mm(x, w_up)
        sigma = 0.5 * jnp.tanh(0.5 * gate) + 0.5
        silu = gate * sigma
        hidden_out[rows, :] = (silu * up).astype(LOW)
        gate_out[rows, :] = (up * (sigma + silu * (1.0 - sigma))).astype(LOW)
        up_out[rows, :] = silu.astype(LOW)


def split_terms(meta, terms, outs):
    rows = terms.shape[0] // len(outs)
    for distance, out in enumerate(outs):
        low = pl.multiple_of((meta[0, DP] ^ distance) * rows, rows)
        out[:rows, :] = terms[pl.ds(low, rows), :]


def down_kernel(meta, hidden_ref, *refs):
    grads, outs, terms = refs[:PARTS], refs[PARTS:-1], refs[-1]
    block = grads[0].shape[0]
    total = mm_tn(hidden_ref[:block, :], grads[0][...])
    for r in range(1, PARTS):
        total = total + mm_tn(hidden_ref[r * block : (r + 1) * block, :], grads[r][...])
    terms[...] = total.astype(LOW)
    split_terms(meta, terms, outs)


def gate_up_kernel(meta, gate_ref, up_ref, *refs):
    grads, x_refs, down_own, refs = refs[:PARTS], refs[PARTS : 2 * PARTS], refs[2 * PARTS], refs[2 * PARTS + 1 :]
    held, low, terms, sems = refs[-4:]
    count = held.shape[0]
    down_refs, outs = refs[: 2 * count - 2], refs[2 * count - 2 : -4]
    width = terms.shape[0]
    copies, _ = place_down(meta, down_own, down_refs, meta[0, PART], held, sems, 0)
    wait_all(copies)
    w_down = held[...].reshape(terms.shape)
    block = grads[0].shape[0]
    for r in range(PARTS):
        rows = slice(r * block, (r + 1) * block)
        grad_hidden = mm_nt(grads[r][...], w_down)
        low[rows, :width] = (grad_hidden * gate_ref[rows, :].astype(FULL)).astype(LOW)
        low[rows, width:] = (grad_hidden * up_ref[rows, :].astype(FULL)).astype(LOW)
    total = mm_tn(x_refs[0][...], low[:block, :])
    for r in range(1, PARTS):
        total = total + mm_tn(x_refs[r][...], low[r * block : (r + 1) * block, :])
    terms[...] = total[:, :width].astype(LOW)
    split_terms(meta, terms, outs[:-1])
    outs[-1][...] = total[:, width:].astype(LOW)


def last_back_kernel(heads, pieces, block, meta, lengths, table_ref, q_ref, k_ref, v_ref, lse_ref, grad_ref, *refs):
    *refs, dq, dk, dv, bias_ref, turn_ref, dk_sum, dv_sum = refs
    turn = Turn(meta, lengths, table_ref, bias_ref, turn_ref, q_ref.shape[0] // PARTS // 2)
    back_head(block, turn, bias_ref, (dk_sum, dv_sum), q_ref, k_ref, v_ref, lse_ref, grad_ref, dq, dk, dv)
    count = heads - 1
    first = [refs[3 + at * count : 3 + (at + 1) * count] for at in range(3)]
    grads = [ref for some, last in zip(first, (dq, dk, dv)) for ref in (*some, last)]
    projections_back_kernel(heads, pieces, meta, *refs[:3], *grads, *refs[3 + 3 * count :])


def projections_back_kernel(heads, pieces, meta, spread, sums, out_terms, *refs):
    grads, refs = [refs[at * heads : (at + 1) * heads] for at in range(3)], refs[3 * heads :]
    x_refs, w_refs, refs = refs[:PARTS], refs[PARTS : PARTS + pieces], refs[PARTS + pieces :]
    outs, (near_out, far_out, w_all, terms) = refs[:pieces], refs[pieces:]
    rows = w_all.shape[0] // pieces
    for distance, w in enumerate(w_refs):
        w_all[pl.ds(pl.multiple_of((meta[0, DP] ^ distance) * rows, rows), rows), :] = w[:rows, :]
    block = x_refs[0].shape[0]
    columns = w_all.shape[1] // 3
    totals = [None] * 3
    for r in range(PARTS):
        span = slice(r * block, (r + 1) * block)
        x, onward = x_refs[r][...], 0.0
        for at, of_heads in enumerate(grads):
            wide = jnp.concatenate([ref[span, :] for ref in of_heads], axis=1)
            low = mm_nt(wide, spread[...]).astype(LOW)
            term = mm_tn(x, low)
            totals[at] = term if r == 0 else totals[at] + term
            onward = onward + mm_nt(low, w_all[:, at * columns : (at + 1) * columns])
        if r % 2 == 0:
            near_out[r // 2] = onward
        else:
            far_out[r // 2] = onward.astype(LOW)
    for at, total in enumerate(totals):
        terms[:, at * columns : (at + 1) * columns] = total.astype(LOW)
    terms[:, 3 * columns :] = out_terms[...]
    split_terms(meta, terms, outs)
    for distance, out in enumerate(outs):
        out[rows:, :] = jnp.zeros((EXTRA, terms.shape[1]), LOW)
        for block_at in range(pieces):

            @pl.when(meta[0, DP] ^ distance == block_at)
            def _(out=out, block_at=block_at):
                out[rows : rows + 8, :rows] = sums[:, block_at * rows : (block_at + 1) * rows].astype(LOW)


def join_rows_kernel(meta, *refs):
    out = refs[-1]
    rows = refs[0].shape[0]
    for r in range(PARTS):
        low = pl.multiple_of((meta[0, PART] ^ r) * rows, rows)
        out[pl.ds(low, rows), :] = refs[r][...].astype(FULL)


def join_columns_kernel(meta, *refs):
    outs, held = refs[PARTS:-1], refs[-1]
    step = outs[0].shape[0]
    for r in range(PARTS):
        held[meta[0, PART] ^ r] = refs[r][...]
    for at, out in enumerate(outs):
        for part in range(PARTS):
            value = held[part, at].astype(FULL)
            for block in range(value.shape[1] // step):
                start = (block * PARTS + part) * step
                out[:, start : start + step] = value[:, block * step : (block + 1) * step]


def join_projections_kernel(meta, *refs):
    outs, sum_outs, held = refs[PARTS:-5], refs[-5:-1], refs[-1]
    rows, columns = outs[0].shape[0], refs[0].shape[1] // len(outs)
    for r in range(PARTS):
        held[meta[0, PART] ^ r] = refs[r][...]
    sums = jnp.zeros((8, rows), FULL)
    for part in range(PARTS):
        value = held[part].astype(FULL)
        for at, out in enumerate(outs):
            out[:, part * columns : (part + 1) * columns] = value[:rows, at * columns : (at + 1) * columns]
        sums = sums + value[rows : rows + 8, :rows]
    for at, out in enumerate(sum_outs):
        out[...] = sums[at]


def gather_pieces(own, bits, starts=None, gate=None):
    held = {0: own}
    for bit in bits:
        for distance in list(held):
            source = held[distance]
            if distance == 0 and starts is not None:
                source = after(source, *starts)
            elif distance != 0 and gate is not None:
                source = after(source, gate)
            held[distance | bit] = hop(source, "dp", bit)
    return [held[distance] for distance in range(len(held))]


def send_terms(chunks, gate=None):
    return [
        hop(chunk if gate is None else after(chunk, *gate), "dp", distance)
        for distance, chunk in enumerate(chunks)
        if distance
    ]


def sum_terms(chunks, got):
    total = chunks[0].astype(FULL)
    for one in got:
        total = total + one.astype(FULL)
    return total


def shards(
    tokens, lengths, w_query, w_key, w_value, w_output, w_gate, w_up, w_down,
    first_gain, first_bias, second_gain, second_bias, cotangent,
):
    _, _, local, width = tokens.shape
    dp_count, blk_count = lax.axis_size("dp"), lax.axis_size("blk")
    dp, blk = lax.axis_index("dp"), lax.axis_index("blk")
    side = blk_count // 2
    which = blk // side
    first = which == 0
    core, part = blk % 2, blk % PARTS
    heads = width // HEAD_DIM // PARTS
    columns = heads * HEAD_DIM
    rows, ff_rows = w_query.shape[0], w_down.shape[0]
    half, ff = rows // 2, w_gate.shape[1]
    block = 2 * local
    row_count = PARTS * block
    spread_bits = bits_between(PARTS, side)
    sum_bits = bits_between(PARTS, blk_count)
    dp_bits = bits_between(1, dp_count)
    back_bits = dp_bits[::-1]
    table = jnp.asarray(turn_table(local * blk_count))
    swap_q, swap_k, spread_v = (
        jnp.asarray(swap_matrix(heads, 3 * columns, at * columns, at < 2), LOW) for at in range(3)
    )
    spread = jnp.asarray(swap_matrix(heads, columns, 0, False), LOW)

    starts = [(blk ^ distance ^ away) * local for distance in range(side) for away in (0, side)]
    meta = jnp.stack([which, core, part, dp, *starts]).astype(jnp.int32).reshape(1, -1)

    gate_up_own = call(
        pack_second_kernel, [shape((2 * PARTS, half, width))], [SMEM] + [VMEM] * 2, [], meta, w_gate, w_up
    )[0]
    gate_up_core = lax.all_gather(gate_up_own, "dp", axis=0, tiled=False)
    tok_send, cot_send, qkv_own, down_own = call(
        pack_first_kernel,
        [shape((local, width)), shape((local, width)), shape((rows + EXTRA + half + half // 3, 3 * columns))]
        + [shape((PARTS, half, width))],
        [SMEM] + [VMEM] * 11, [], after(meta, gate_up_own), tokens, cotangent, w_query, w_key, w_value, w_output, w_down,
        first_gain, first_bias, second_gain, second_bias,
    )
    tok_got = hop(tok_send, "blk", side)
    qkv = gather_pieces(qkv_own, dp_bits)
    x_own = jnp.concatenate([jnp.where(first, tokens[0, 0], tokens[1, 0]), tok_got])
    x_core, x_near = hop(x_own, "blk", 1), hop(x_own, "blk", 2)
    x_far = hop(after(x_near, x_core, *(qkv[bit] for bit in dp_bits)), "blk", 1)
    x_all = [x_own, x_core, x_near, x_far]
    down_pieces = {0: down_own}
    for bit in dp_bits[:2]:
        down_pieces[bit] = hop(after(down_own, *qkv[1:]), "dp", bit)
    cot_got = hop(after(cot_send, x_near), "blk", side)

    wide_shape = shape((row_count, WIDE))
    made = call(
        functools.partial(project_kernel, heads, dp_count), [wide_shape] * (3 * heads),
        [SMEM] + [VMEM] * (4 + PARTS + dp_count),
        [pltpu.VMEM((width, 3 * columns), LOW), pltpu.VMEM((row_count, 2 * WIDE), FULL)],
        after(meta, cot_got), table, swap_q, swap_k, spread_v, *x_all, *qkv,
    )
    queries, keys, values = (made[at * heads : (at + 1) * heads] for at in range(3))
    out_rows = rows + EXTRA
    qkv_core = hop(after(jnp.stack([piece[out_rows:] for piece in qkv[1:]]), queries[0]), "blk", 1)
    for bit in spread_bits:
        keys, values = ([jnp.concatenate([one, hop(one, "blk", bit)]) for one in many] for many in (keys, values))
    key_count = keys[0].shape[0]
    q_block = max(WIDE, min(row_count, 512 * 1024 // key_count))
    attended = call(
        functools.partial(attend_kernel, heads, q_block),
        [shape((PARTS, block, columns))] + [shape((1, row_count), FULL)] * heads,
        [SMEM] * 2 + [VMEM] * (1 + 3 * heads),
        [pltpu.VMEM((row_count, heads * WIDE), LOW)],
        meta, lengths, *queries, *keys, *values, spread,
    )
    attended, lse = attended[0], attended[1:]
    att_send = after(attended, qkv_core, *(down_pieces[bit] for bit in dp_bits[:2]))
    att_core, att_near = hop(att_send, "blk", 1), hop(att_send, "blk", 2)
    att_all = [attended, att_core, att_near, hop(after(att_near, att_core), "blk", 1)]
    middle = PARTS // 2
    down_pieces[3] = jnp.concatenate(
        [hop(down_pieces[1][:middle], "dp", 2), hop(down_pieces[2][middle:], "dp", 1)]
    )
    for bit in dp_bits[2:]:
        for distance in range(bit):
            down_pieces[distance | bit] = hop(down_pieces[distance], "dp", bit)
    down_pieces = [down_pieces[distance] for distance in range(dp_count)]
    residual_one, normed_low, all_vectors, w_o = call(
        functools.partial(residual_kernel, dp_count),
        [shape((block, width), FULL), shape((block, width)), shape((8, width), FULL), shape((columns, width))],
        [SMEM] + [VMEM] * (2 + PARTS + dp_count + 1),
        [pltpu.VMEM((width, width), LOW), pltpu.VMEM((dp_count, EXTRA, 3 * columns), LOW)],
        after(meta, down_pieces[3]), x_own, w_output, *att_all, *qkv, qkv_core,
    )
    normed_core, normed_near = hop(normed_low, "blk", 1), hop(normed_low, "blk", 2)
    down_core = [hop(after(piece, normed_low), "blk", 1) for piece in down_pieces[1:]]
    down_all = (w_down, *down_pieces[1:], *down_core)
    gate_up_all = (gate_up_core, hop(after(gate_up_core, att_all[3], down_pieces[3]), "blk", 1))

    part_shape, w_shape = (PARTS, block, width), (dp_count, rows, width)
    down_copies = 2 * dp_count - 1
    grad_ffn, grad_branch, grad_one, layer_own, layer_back, sums = call(
        feed_kernel,
        [shape((block, width))] * 2 + [shape((block, width), FULL)] + [shape((local, width))] * 2
        + [shape((8, width), FULL)],
        [SMEM] * 2 + [VMEM] * 4 + [ANY] * (2 + len(down_all)),
        [
            pltpu.VMEM((3 * PARTS, *w_shape), LOW),
            pltpu.VMEM(part_shape, FULL),
            pltpu.VMEM(part_shape, FULL),
            pltpu.SemaphoreType.DMA((PARTS * (4 + down_copies),)),
        ],
        after(meta, normed_core), lengths, residual_one, all_vectors, cotangent, cot_got, *gate_up_all, *down_all,
    )
    ffn_core, ffn_near = hop(grad_ffn, "blk", 1), hop(grad_ffn, "blk", 2)
    normed_all = [normed_low, normed_core, normed_near, hop(after(normed_near, grad_ffn), "blk", 1)]

    long, chunk = shape((row_count, width)), shape((rows, width))
    hidden, gate_factor, up_factor = call(
        hidden_kernel, [long] * 3,
        [SMEM] + [VMEM] * PARTS + [ANY] * 2,
        [pltpu.VMEM(w_shape, LOW), pltpu.VMEM(w_shape, LOW), pltpu.SemaphoreType.DMA((4,))],
        after(meta, grad_ffn), *normed_all, *gate_up_all,
    )
    ffn_all = [grad_ffn, ffn_core, ffn_near, hop(after(ffn_near, hidden, ffn_core), "blk", 1)]
    branch_core, branch_near = (hop(after(grad_branch, ffn_near, hidden), "blk", bit) for bit in (1, 2))
    down_terms = call(
        down_kernel, [chunk] * dp_count, [SMEM] + [VMEM] * (1 + PARTS), [pltpu.VMEM((width, width), LOW)],
        after(meta, branch_core), hidden, *ffn_all,
    )
    down_got = send_terms(down_terms)
    gate_up_terms = call(
        gate_up_kernel, [chunk] * dp_count + [shape((width, width))],
        [SMEM] + [VMEM] * (2 + 2 * PARTS) + [ANY] * len(down_all),
        [pltpu.VMEM(w_shape, LOW), pltpu.VMEM((row_count, 2 * width), LOW)]
        + [pltpu.VMEM((width, width), LOW), pltpu.SemaphoreType.DMA((down_copies,))],
        after(meta, down_terms[0]), gate_factor, up_factor, *ffn_all, *normed_all, *down_all,
    )

    def sum_halves(total):
        for bit in sum_bits:
            low = total.astype(LOW)
            total = low.astype(FULL) + hop(low, "blk", bit).astype(FULL)
        return total.astype(LOW)

    branch_far = hop(after(branch_near, gate_up_terms[0], *(down_got[bit - 1] for bit in dp_bits)), "blk", 1)
    layer_got = hop(after(layer_back, branch_far), "blk", side)
    down_sum = sum_terms(down_terms, down_got)
    down_full = sum_halves(down_sum)
    gate_got = send_terms(gate_up_terms[:dp_count])
    up_sum = lax.psum_scatter(
        after(gate_up_terms[-1], branch_far).reshape(dp_count, rows, width), "dp", scatter_dimension=0, tiled=False
    )
    early = heads if spread_bits else heads - 1
    key_shape = shape((key_count, WIDE))
    back_scratch = [pltpu.VMEM((key_count, WIDE), FULL), pltpu.VMEM((key_count, 2 * WIDE), FULL)]
    back_scratch += [pltpu.VMEM((key_count, WIDE), FULL)] * 2
    *made, out_terms = call(
        functools.partial(attend_back_kernel, early, q_block),
        [wide_shape] * early + [key_shape] * (2 * early) + [wide_shape] * (heads - early) + [shape((width, columns))],
        [SMEM] * 2 + [VMEM] * (3 + 2 * PARTS + 4 * early),
        [pltpu.VMEM((PARTS, block, columns), LOW), *back_scratch] + [pltpu.VMEM((row_count, WIDE), LOW)] * early,
        after(meta, down_sum), lengths, w_o, spread, table,
        grad_branch, branch_core, branch_near, branch_far, *att_all,
        *queries[:early], *keys[:early], *values[:early], *lse[:early],
    )
    grad_q, grad_k, grad_v = (made[at * early : (at + 1) * early] for at in range(3))
    gate_sum = sum_terms(gate_up_terms, [after(got, grad_q[0], layer_got) for got in gate_got])
    gate_full = sum_halves(gate_sum)
    down_near = hop(down_full, "blk", 2)
    for bit in reversed(spread_bits):
        middle = grad_k[0].shape[0] // 2
        grad_k, grad_v = (
            [
                (one[:middle].astype(FULL) + hop(one[middle:], "blk", bit).astype(FULL)).astype(LOW)
                for one in many
            ]
            for many in (grad_k, grad_v)
        )
    back_outs = [shape((rows + EXTRA, width))] * dp_count + [shape((2, block, width), FULL), shape((2, block, width))]
    back_weights = [pltpu.VMEM((width, 3 * columns), LOW), pltpu.VMEM((width, width), LOW)]
    back_operands = (spread, sums, out_terms, *grad_q, *grad_k, *grad_v, *x_all, *qkv)
    ready = after(meta, gate_sum, down_full)
    if spread_bits:
        made = call(
            functools.partial(projections_back_kernel, heads, dp_count), back_outs,
            [SMEM] + [VMEM] * len(back_operands), back_weights, ready, *back_operands,
        )
    else:
        made = call(
            functools.partial(last_back_kernel, heads, dp_count, q_block), back_outs,
            [SMEM] * 2 + [VMEM] * (6 + len(back_operands)),
            back_weights + [pltpu.VMEM((row_count, WIDE), LOW)] * 3 + back_scratch,
            ready, lengths, table, queries[-1], keys[-1], values[-1], lse[-1], made[-1], *back_operands,
        )
    *qkv_terms, token_keep, token_send = made
    up_sum = after(up_sum, token_keep).astype(FULL)

    first_gate = (gate_full, up_sum, down_near)
    token_got = hop(after(token_send, *first_gate), "blk", 1).astype(FULL)
    up_full = sum_halves(up_sum)
    near_send = (token_keep[1] + token_got[1]).astype(LOW)
    token_near = hop(near_send, "blk", 2)
    qkv_got = send_terms(qkv_terms)
    qkv_sum = sum_terms(qkv_terms, [after(got, token_near) for got in qkv_got]).astype(LOW)
    qkv_full = sum_halves(after(qkv_sum, up_full, token_near))
    pair_full = after(jnp.stack([gate_full, up_full]), qkv_sum)
    pair_core, pair_near = hop(pair_full, "blk", 1), hop(pair_full, "blk", 2)
    down_core, down_far = (hop(after(one, pair_core), "blk", 1) for one in (down_full, down_near))
    grad_rows = after(grad_one, qkv_sum) + token_keep[0] + token_got[0] + token_near.astype(FULL)
    rows_got = hop(grad_rows[local:].astype(LOW), "blk", side).astype(FULL)
    grad_down = call(
        join_rows_kernel, [shape((ff_rows, width), FULL)], [SMEM] + [VMEM] * PARTS, [],
        meta, down_full, down_core, down_near, down_far,
    )[0]
    pair_far = hop(after(pair_near, pair_core, grad_down), "blk", 1)
    qkv_core, qkv_near = (hop(after(qkv_full, pair_near), "blk", bit) for bit in (1, 2))
    grad_gate, grad_up = call(
        join_columns_kernel, [shape((rows, ff), FULL)] * 2, [SMEM] + [VMEM] * PARTS,
        [pltpu.VMEM((PARTS, 2, rows, width), LOW)], meta, pair_full, pair_core, pair_near, pair_far,
    )
    qkv_far = hop(after(qkv_near, qkv_core, grad_gate, rows_got), "blk", 1)
    grad_tokens = jnp.where(
        first, jnp.stack([grad_rows[:local], rows_got]), jnp.stack([rows_got, grad_rows[:local]])
    )[:, None]
    layer_out = jnp.where(first, jnp.stack([layer_own, layer_got]), jnp.stack([layer_got, layer_own]))[:, None]
    grad_query, grad_key, grad_value, grad_output, *vector_sums = call(
        join_projections_kernel, [shape((rows, width), FULL)] * 4 + [shape((rows,), FULL)] * 4,
        [SMEM] + [VMEM] * PARTS, [pltpu.VMEM((PARTS, rows + EXTRA, width), LOW)], meta, qkv_full, qkv_core, qkv_near, qkv_far,
    )
    return (
        layer_out, grad_tokens, grad_query, grad_key, grad_value, grad_output, grad_gate, grad_up, grad_down,
        vector_sums[0], vector_sums[1], vector_sums[2], vector_sums[3],
    )


def solution(mesh):
    slots = P(None, "dp", "blk", None)
    matrix, vector = P("dp", None), P("dp")
    return jax.shard_map(
        shards,
        mesh=mesh,
        in_specs=(slots, P(None, "dp")) + (matrix,) * 7 + (vector,) * 4 + (slots,),
        out_specs=(slots, slots) + (matrix,) * 7 + (vector,) * 4,
        check_vma=False,
    )
```

```python
import functools

import jax
import jax.numpy as jnp
import numpy as np
from jax import lax
from jax.experimental import pallas as pl
from jax.experimental.pallas import tpu as pltpu
from jax.sharding import PartitionSpec as P

HEAD_DIM = 64
WIDE = 128
PARTS = 4
EXTRA = 16
LOW, FULL = jnp.bfloat16, jnp.float32
VMEM_MIB = {"join_rows_kernel": 30, "join_columns_kernel": 30, "join_projections_kernel": 30, "hidden_kernel": 40, "down_kernel": 40, "gate_up_kernel": 40}
VMEM = pl.BlockSpec(memory_space=pltpu.VMEM)
SMEM = pl.BlockSpec(memory_space=pltpu.SMEM)
ANY = pl.BlockSpec(memory_space=pl.ANY)
WHICH, CORE, PART, DP, STARTS = 0, 1, 2, 3, 4


def mm(left, right):
    return jnp.dot(left, right, preferred_element_type=FULL)


def mm_nt(left, right):
    return lax.dot_general(left, right, (((1,), (1,)), ((), ())), preferred_element_type=FULL)


def mm_tn(left, right):
    return lax.dot_general(left, right, (((0,), (0,)), ((), ())), preferred_element_type=FULL)


def hop(value, axis, bit):
    size = lax.axis_size(axis)
    return lax.ppermute(value, axis, [(at, at ^ bit) for at in range(size)])


def after(value, *others):
    return lax.optimization_barrier((value, *others))[0]


def bits_between(low, high):
    bits = []
    while low < high:
        bits.append(low)
        low *= 2
    return bits


def turn_table(seq_len):
    half = HEAD_DIM // 2
    frequency = np.float32(1000.0) ** (
        -(np.arange(half, dtype=np.float32) * np.float32(2.0) / np.float32(HEAD_DIM))
    )
    angles = np.arange(seq_len, dtype=np.float32)[:, None] * frequency[None, :]
    cosine = np.cos(angles).astype(np.float32)
    sine = np.sin(angles).astype(np.float32)
    return np.concatenate([cosine] * 4 + [sine, sine, -sine, -sine], axis=1)


def swap_matrix(heads, total, first, swapped):
    half = HEAD_DIM // 2
    out = np.zeros((total, heads * WIDE), np.float32)
    for h in range(heads):
        for f in range(HEAD_DIM):
            out[first + h * HEAD_DIM + f, h * WIDE + f] = 1.0
        for f in range(half if swapped else 0):
            out[first + h * HEAD_DIM + half + f, h * WIDE + HEAD_DIM + f] = -1.0
            out[first + h * HEAD_DIM + f, h * WIDE + HEAD_DIM + half + f] = 1.0
    return out


def call(body, outs, in_specs, scratch, *operands):
    name = getattr(body, "func", body).__name__
    return pl.pallas_call(
        body,
        out_shape=outs,
        in_specs=in_specs,
        out_specs=[VMEM] * len(outs),
        scratch_shapes=scratch,
        name=getattr(body, "func", body).__name__,
        compiler_params=pltpu.CompilerParams(vmem_limit_bytes=VMEM_MIB.get(name, 60) * 1024 * 1024),
        cost_estimate=pl.CostEstimate(flops=1000, bytes_accessed=1000, transcendentals=0),
    )(*operands)


def shape(dims, dtype=LOW):
    return jax.ShapeDtypeStruct(dims, dtype)


def norm_parts(rows):
    centred = rows - jnp.mean(rows, axis=-1, keepdims=True)
    scale = lax.rsqrt(jnp.mean(centred * centred, axis=-1, keepdims=True) + 1e-05)
    return centred * scale, scale


def norm_back(upstream, gain, unit, scale):
    inner = upstream * gain
    centre = jnp.mean(inner, axis=-1, keepdims=True)
    along = jnp.mean(inner * unit, axis=-1, keepdims=True)
    sums = (jnp.sum(upstream * unit, axis=0, keepdims=True), jnp.sum(upstream, axis=0, keepdims=True))
    return (inner - centre - unit * along) * scale, sums


def pack_first_kernel(
    meta, tokens, cot, w_q, w_k, w_v, w_o, w_down, gain_one, bias_one, gain_two, bias_two, tok_out, cot_out, qkv_out, down_out
):
    rows, columns = w_q.shape[0], qkv_out.shape[1] // 3
    half, third = rows // 2, rows // 6
    other = 1 - meta[0, WHICH]
    tok_out[...] = tokens[other, 0]
    cot_out[...] = cot[other, 0]
    for part in range(PARTS):

        @pl.when(meta[0, PART] == part)
        def _(part=part):
            for at, w in enumerate((w_q, w_k, w_v)):
                qkv_out[:rows, at * columns : (at + 1) * columns] = w[:, part * columns : (part + 1) * columns]

    qkv_out[rows : rows + EXTRA, :] = jnp.zeros((EXTRA, 3 * columns), LOW)
    for at, vector in enumerate((gain_one, bias_one, gain_two, bias_two)):
        qkv_out[rows + at : rows + at + 1, :rows] = vector[...].reshape(1, rows)
    for part in range(PARTS):
        low = pl.multiple_of(part * rows + meta[0, CORE] * half, half)
        down_out[part] = w_down[pl.ds(low, half), :]
    out_rows = w_o[pl.ds(pl.multiple_of(meta[0, CORE] * half, half), half), :]
    at = rows + EXTRA
    qkv_out[at : at + half, :] = out_rows[:, : 3 * columns]
    at += half
    for g in range(3):
        qkv_out[at : at + third, g * columns : (g + 1) * columns] = out_rows[g * third : (g + 1) * third, 3 * columns :]


def pack_second_kernel(meta, w_gate, w_up, out):
    half, width = out.shape[1], out.shape[2]
    step = 2 * half
    low = pl.multiple_of(meta[0, CORE] * half, half)
    for base, w in ((0, w_gate), (PARTS, w_up)):
        for part in range(PARTS):
            for block in range(width // step):
                start = (block * PARTS + part) * step
                out[base + part, :, block * step : (block + 1) * step] = w[pl.ds(low, half), start : start + step]


def project_kernel(heads, pieces, meta, table_ref, swap_q, swap_k, spread_v, *refs):
    x_refs, w_refs, (q_refs, k_refs, v_refs) = refs[:PARTS], refs[PARTS : PARTS + pieces], [refs[-2 - 3 * heads + at * heads : -2 - 2 * heads + at * heads] for at in range(3)]
    w_all, turn = refs[-2:]
    rows = w_all.shape[0] // pieces
    block = x_refs[0].shape[0]
    local = block // 2
    for distance, w in enumerate(w_refs):
        w_all[pl.ds(pl.multiple_of((meta[0, DP] ^ distance) * rows, rows), rows), :] = w[:rows, :]
    for at in range(2 * PARTS):
        start = pl.multiple_of(meta[0, STARTS + at], local)
        turn[at * local : (at + 1) * local, :] = table_ref[pl.ds(start, local), :]
    weights = w_all[...]
    w_q, w_k, w_v = (mm(weights, m[...]).astype(LOW) for m in (swap_q, swap_k, spread_v))
    for r in range(PARTS):
        out_rows = slice(r * block, (r + 1) * block)
        x = x_refs[r][...]
        cosine, sine = turn[out_rows, :WIDE], turn[out_rows, WIDE:]
        for out_refs, w, scale in ((q_refs, w_q, 0.0625), (k_refs, w_k, None)):
            made = mm(x, w)
            for h in range(heads):
                one = made[:, h * WIDE : (h + 1) * WIDE]
                turned = (one * cosine + pltpu.roll(one, HEAD_DIM, 1) * sine).astype(LOW)
                out_refs[h][out_rows, :] = turned if scale is None else turned * jnp.asarray(scale, LOW)
        made = mm(x, w_v).astype(LOW)
        for h in range(heads):
            v_refs[h][out_rows, :] = made[:, h * WIDE : (h + 1) * WIDE]


def fill_bias(meta, length, bias_ref, local):
    for at in range(bias_ref.shape[0] // local):
        place = meta[0, STARTS + at] + lax.broadcasted_iota(jnp.int32, (local, WIDE), 0)
        bias_ref[at * local : (at + 1) * local, :] = jnp.where(place < length, 0.0, -1e30)


def each_block(count, step):
    if count <= 4:
        for number in range(count):
            step(number)
    else:
        lax.fori_loop(0, count, lambda number, carry: step(number) or carry, 0)


def block_rows(number, block):
    if isinstance(number, int):
        return slice(number * block, (number + 1) * block)
    return pl.ds(pl.multiple_of(number * block, block), block)


def attend_kernel(heads, block, meta, lengths, *refs):
    q_refs, k_refs, v_refs, spread_ref = refs[:heads], refs[heads : 2 * heads], refs[2 * heads : 3 * heads], refs[3 * heads]
    out, lse_refs, wide_ref = refs[3 * heads + 1], refs[-1 - heads : -1], refs[-1]
    row_count, key_count = q_refs[0].shape[0], k_refs[0].shape[0]
    span = row_count // PARTS
    local = span // 2
    length = lengths[meta[0, WHICH], 0]
    places = [meta[0, STARTS + at] + lax.broadcasted_iota(jnp.int32, (1, local), 1) for at in range(key_count // local)]
    bias = jnp.where(jnp.concatenate(places, axis=1) < length, 0.0, -1e30)
    for h in range(heads):

        def step(number, h=h):
            rows = block_rows(number, block)
            scores = mm_nt(q_refs[h][rows, :], k_refs[h][...]) + bias
            top = jnp.max(scores, axis=1, keepdims=True)
            weights = jnp.exp(scores - top)
            total = jnp.sum(weights, axis=1, keepdims=True)
            wide_ref[rows, h * WIDE : (h + 1) * WIDE] = (mm(weights.astype(LOW), v_refs[h][...]) / total).astype(LOW)
            lse_refs[h][:, rows] = jnp.broadcast_to(top + jnp.log(total), (block, WIDE)).T[:1, :]

        each_block(row_count // block, step)
    for r in range(PARTS):
        out[r] = mm_nt(wide_ref[r * span : (r + 1) * span, :], spread_ref[...]).astype(LOW)


class Turn:
    def __init__(self, meta, lengths, table_ref, bias_ref, turn, local):
        fill_bias(meta, lengths[meta[0, WHICH], 0], bias_ref, local)
        for at in range(turn.shape[0] // local):
            start = pl.multiple_of(meta[0, STARTS + at], local)
            turn[at * local : (at + 1) * local, :] = table_ref[pl.ds(start, local), :]
        self.turn = turn

    def back(self, value, rows):
        cosine, sine = self.turn[rows, :WIDE], self.turn[rows, WIDE:]
        return (value * cosine - pltpu.roll(value, HEAD_DIM, 1) * sine).astype(LOW)


def back_head(block, turn, bias_ref, sums, q_ref, k_ref, v_ref, lse_ref, grad_ref, dq_ref, dk_ref, dv_ref):
    dk_sum, dv_sum = sums
    keys, values = k_ref[...], v_ref[...]
    keys_t = keys.T
    dk_sum[...] = jnp.zeros_like(dk_sum)
    dv_sum[...] = jnp.zeros_like(dv_sum)

    def step(number):
        rows = block_rows(number, block)
        bias = jnp.concatenate([bias_ref[...]] * (block // WIDE), axis=1)
        queries, grads = q_ref[rows, :], grad_ref[rows, :]
        probs = jnp.exp(mm_nt(keys, queries) + bias - lse_ref[:, rows])
        grad_probs = mm_nt(values, grads)
        delta = jnp.sum(probs * grad_probs, axis=0, keepdims=True)
        grad_scores = (probs * (grad_probs - delta)).astype(LOW)
        dv_sum[...] += mm(probs.astype(LOW), grads)
        dk_sum[...] += mm(grad_scores, queries)
        dq_ref[rows, :] = turn.back(mm(keys_t, grad_scores).T * 0.125, rows)

    each_block(q_ref.shape[0] // block, step)
    dk_ref[...] = turn.back(dk_sum[...] * 2.0, slice(None))
    dv_ref[...] = dv_sum[...].astype(LOW)


def attend_back_kernel(heads, block, meta, lengths, w_o, spread_ref, table_ref, *refs):
    grads_in, att_in, refs = refs[:PARTS], refs[PARTS : 2 * PARTS], refs[2 * PARTS :]
    ins, refs = [refs[at * heads : (at + 1) * heads] for at in range(4)], refs[4 * heads :]
    outs, refs = [refs[at * heads : (at + 1) * heads] for at in range(3)], refs[3 * heads :]
    *later, dw_ref, grad_part, bias_ref, turn_ref, dk_sum, dv_sum = refs[: -heads]
    wide = [*refs[-heads:], *later]
    columns = w_o.shape[0]
    weights = mm_tn(spread_ref[...], w_o[...]).astype(LOW)
    span = grads_in[0].shape[0]
    for r in range(PARTS):
        made = mm_nt(grads_in[r][...], weights).astype(LOW)
        for h, out in enumerate(wide):
            out[r * span : (r + 1) * span, :] = made[:, h * WIDE : (h + 1) * WIDE]
        for part in range(PARTS):

            @pl.when(meta[0, PART] == part)
            def _(r=r, part=part):
                grad_part[r] = grads_in[r][:, part * columns : (part + 1) * columns]

    for distance in range(PARTS):
        total = mm_tn(att_in[distance][distance], grad_part[0])
        for r in range(1, PARTS):
            total = total + mm_tn(att_in[distance][r ^ distance], grad_part[r])
        low = pl.multiple_of((meta[0, PART] ^ distance) * columns, columns)
        dw_ref[pl.ds(low, columns), :] = total.astype(LOW)
    turn = Turn(meta, lengths, table_ref, bias_ref, turn_ref, span // 2)
    for h in range(heads):
        q_ref, k_ref, v_ref, lse_ref = (some[h] for some in ins)
        back_head(block, turn, bias_ref, (dk_sum, dv_sum), q_ref, k_ref, v_ref, lse_ref, wide[h], *(o[h] for o in outs))


def place_gate_up(meta, refs, block, target, sems, at):
    half = refs[0].shape[2]
    copies = []
    for side, ref in enumerate(refs):
        low = pl.multiple_of((meta[0, CORE] ^ side) * half, half)
        copy = pltpu.make_async_copy(ref.at[:, block], target.at[:, pl.ds(low, half), :], sems.at[at + side])
        copy.start()
        copies.append(copy)
    return copies, at + 2


def place_down(meta, own, refs, block, target, sems, at):
    count, rows = target.shape[0], target.shape[1]
    half = rows // 2
    low = pl.multiple_of(block * rows, rows)
    copies = [pltpu.make_async_copy(own.at[pl.ds(low, rows), :], target.at[meta[0, DP]], sems.at[at])]
    for number, ref in enumerate(refs):
        distance, side = number % (count - 1) + 1, number // (count - 1)
        low = pl.multiple_of((meta[0, CORE] ^ side) * half, half)
        to = target.at[meta[0, DP] ^ distance, pl.ds(low, half), :]
        copies.append(pltpu.make_async_copy(ref.at[block], to, sems.at[at + 1 + number]))
    for copy in copies:
        copy.start()
    return copies, at + len(copies)


def wait_all(copies):
    for copy in copies:
        copy.wait()


def residual_kernel(pieces, meta, x_ref, w_own, *refs):
    att, w_refs, w_core, refs = refs[:PARTS], refs[PARTS : PARTS + pieces], refs[PARTS + pieces], refs[PARTS + pieces + 1 :]
    residual_out, low_out, vector_out, w_out, w_o, gathered = refs
    columns, rows = att[0].shape[2], w_own.shape[0]
    half, third = rows // 2, rows // 6
    w_o[pl.ds(pl.multiple_of(meta[0, DP] * rows, rows), rows), :] = w_own[...]

    def fill(ref, low):
        w_o[pl.ds(pl.multiple_of(low, half), half), : 3 * columns] = ref[:half, :]
        for g in range(3):
            to = pl.ds(pl.multiple_of(low + g * third, third), third)
            w_o[to, 3 * columns :] = ref[half:, g * columns : (g + 1) * columns]

    for distance, ref in enumerate(w_refs):
        gathered[meta[0, DP] ^ distance] = ref[rows : rows + EXTRA, :]
        if distance:
            low = (meta[0, DP] ^ distance) * rows
            fill(ref[rows + EXTRA :, :], low + meta[0, CORE] * half)
            fill(w_core[distance - 1], low + (1 - meta[0, CORE]) * half)
    vectors = jnp.concatenate([gathered[d][:8, :rows] for d in range(pieces)], axis=1).astype(FULL)
    vector_out[...] = vectors
    residual = x_ref[...].astype(FULL)
    for r in range(PARTS):
        low = pl.multiple_of((meta[0, PART] ^ r) * columns, columns)
        residual = residual + mm(att[r][r], w_o[pl.ds(low, columns), :])
    w_out[...] = w_o[pl.ds(pl.multiple_of(meta[0, PART] * columns, columns), columns), :]
    residual_out[...] = residual
    unit, _ = norm_parts(residual)
    low_out[...] = (unit * vectors[0:1] + vectors[1:2]).astype(LOW)


def feed_kernel(meta, lengths, residual_ref, vectors, cot_ref, cot_got, *refs):
    gu_refs, down_own, down_refs, refs = refs[:2], refs[2], refs[3:-10], refs[-10:]
    grad_ffn_out, grad_branch_out, grad_one_out, own_out, back_out, sums_out, held, gates, ups, sems = refs
    width = residual_ref.shape[1]
    copies, at = [], 0
    for part in range(PARTS):
        gate, at = place_gate_up(meta, gu_refs, part, held.at[part], sems, at)
        up, at = place_gate_up(meta, gu_refs, PARTS + part, held.at[PARTS + part], sems, at)
        down, at = place_down(meta, down_own, down_refs, part, held.at[2 * PARTS + part], sems, at)
        copies.append(gate + up + down)

    def weights(number):
        return held[number].reshape(width, width)

    which = meta[0, WHICH]
    local = cot_got.shape[0]
    unit_one, scale_one = norm_parts(residual_ref[...])
    normed = unit_one * vectors[0:1] + vectors[1:2]
    normed_low = normed.astype(LOW)
    residual = normed

    def pre(part):
        wait_all(copies[part])
        return mm(normed_low, weights(part)), mm(normed_low, weights(PARTS + part))

    ahead = pre(0)
    for part in range(PARTS):
        gate, up = ahead
        if part + 1 < PARTS:
            ahead = pre(part + 1)
        sigma = 0.5 * jnp.tanh(0.5 * gate) + 0.5
        silu = gate * sigma
        residual = residual + mm((silu * up).astype(LOW), weights(2 * PARTS + part))
        gates[part] = up * (sigma + silu * (1.0 - sigma))
        ups[part] = silu
    unit_two, scale_two = norm_parts(residual)
    layer = unit_two * vectors[2:3] + vectors[3:4]
    length = lengths[which, 0]
    upstream = []
    for half, (out, cot) in enumerate(((own_out, cot_ref[which, 0]), (back_out, cot_got[...]))):
        place = meta[0, STARTS + half] + lax.broadcasted_iota(jnp.int32, (local, 1), 0)
        valid = place < length
        out[...] = jnp.where(valid, layer[half * local : (half + 1) * local], 0.0).astype(LOW)
        upstream.append(jnp.where(valid, cot.astype(FULL), 0.0))
    grad_two, sums_two = norm_back(jnp.concatenate(upstream, axis=0), vectors[2:3], unit_two, scale_two)
    grad_ffn = grad_two.astype(LOW)
    grad_ffn_out[...] = grad_ffn
    grad_normed = grad_two
    for part in range(PARTS):
        grad_hidden = mm_nt(grad_ffn, weights(2 * PARTS + part))
        grad_normed = (
            grad_normed
            + mm_nt((grad_hidden * gates[part]).astype(LOW), weights(part))
            + mm_nt((grad_hidden * ups[part]).astype(LOW), weights(PARTS + part))
        )
    grad_one, sums_one = norm_back(grad_normed, vectors[0:1], unit_one, scale_one)
    grad_one_out[...] = grad_one
    grad_branch_out[...] = grad_one.astype(LOW)
    sums_out[...] = jnp.concatenate([*sums_one, *sums_two, jnp.zeros((4, width), FULL)], axis=0)


def hidden_kernel(meta, *refs):
    x_refs, gu_refs, refs = refs[:PARTS], refs[PARTS : PARTS + 2], refs[PARTS + 2 :]
    hidden_out, gate_out, up_out, held_gate, held_up, sems = refs
    part, width = meta[0, PART], hidden_out.shape[1]
    first, at = place_gate_up(meta, gu_refs, part, held_gate, sems, 0)
    second, at = place_gate_up(meta, gu_refs, PARTS + part, held_up, sems, at)
    wait_all(first + second)
    w_gate, w_up = held_gate[...].reshape(width, width), held_up[...].reshape(width, width)
    block = x_refs[0].shape[0]
    for r in range(PARTS):
        rows = slice(r * block, (r + 1) * block)
        x = x_refs[r][...]
        gate, up = mm(x, w_gate), mm(x, w_up)
        sigma = 0.5 * jnp.tanh(0.5 * gate) + 0.5
        silu = gate * sigma
        hidden_out[rows, :] = (silu * up).astype(LOW)
        gate_out[rows, :] = (up * (sigma + silu * (1.0 - sigma))).astype(LOW)
        up_out[rows, :] = silu.astype(LOW)


def split_terms(meta, terms, outs):
    rows = terms.shape[0] // len(outs)
    for distance, out in enumerate(outs):
        low = pl.multiple_of((meta[0, DP] ^ distance) * rows, rows)
        out[:rows, :] = terms[pl.ds(low, rows), :]


def down_kernel(meta, hidden_ref, *refs):
    grads, outs, terms = refs[:PARTS], refs[PARTS:-1], refs[-1]
    block = grads[0].shape[0]
    total = mm_tn(hidden_ref[:block, :], grads[0][...])
    for r in range(1, PARTS):
        total = total + mm_tn(hidden_ref[r * block : (r + 1) * block, :], grads[r][...])
    terms[...] = total.astype(LOW)
    split_terms(meta, terms, outs)


def gate_up_kernel(meta, gate_ref, up_ref, *refs):
    grads, x_refs, down_own, refs = refs[:PARTS], refs[PARTS : 2 * PARTS], refs[2 * PARTS], refs[2 * PARTS + 1 :]
    held, low, terms, sems = refs[-4:]
    count = held.shape[0]
    down_refs, outs = refs[: 2 * count - 2], refs[2 * count - 2 : -4]
    width = terms.shape[0]
    copies, _ = place_down(meta, down_own, down_refs, meta[0, PART], held, sems, 0)
    wait_all(copies)
    w_down = held[...].reshape(terms.shape)
    block = grads[0].shape[0]
    for r in range(PARTS):
        rows = slice(r * block, (r + 1) * block)
        grad_hidden = mm_nt(grads[r][...], w_down)
        low[rows, :width] = (grad_hidden * gate_ref[rows, :].astype(FULL)).astype(LOW)
        low[rows, width:] = (grad_hidden * up_ref[rows, :].astype(FULL)).astype(LOW)
    total = mm_tn(x_refs[0][...], low[:block, :])
    for r in range(1, PARTS):
        total = total + mm_tn(x_refs[r][...], low[r * block : (r + 1) * block, :])
    terms[...] = total[:, :width].astype(LOW)
    split_terms(meta, terms, outs[:-1])
    outs[-1][...] = total[:, width:].astype(LOW)


def last_back_kernel(heads, pieces, block, meta, lengths, table_ref, q_ref, k_ref, v_ref, lse_ref, grad_ref, *refs):
    *refs, dq, dk, dv, bias_ref, turn_ref, dk_sum, dv_sum = refs
    turn = Turn(meta, lengths, table_ref, bias_ref, turn_ref, q_ref.shape[0] // PARTS // 2)
    back_head(block, turn, bias_ref, (dk_sum, dv_sum), q_ref, k_ref, v_ref, lse_ref, grad_ref, dq, dk, dv)
    count = heads - 1
    first = [refs[3 + at * count : 3 + (at + 1) * count] for at in range(3)]
    grads = [ref for some, last in zip(first, (dq, dk, dv)) for ref in (*some, last)]
    projections_back_kernel(heads, pieces, meta, *refs[:3], *grads, *refs[3 + 3 * count :])


def projections_back_kernel(heads, pieces, meta, spread, sums, out_terms, *refs):
    grads, refs = [refs[at * heads : (at + 1) * heads] for at in range(3)], refs[3 * heads :]
    x_refs, w_refs, refs = refs[:PARTS], refs[PARTS : PARTS + pieces], refs[PARTS + pieces :]
    outs, (near_out, far_out, w_all, terms) = refs[:pieces], refs[pieces:]
    rows = w_all.shape[0] // pieces
    for distance, w in enumerate(w_refs):
        w_all[pl.ds(pl.multiple_of((meta[0, DP] ^ distance) * rows, rows), rows), :] = w[:rows, :]
    block = x_refs[0].shape[0]
    columns = w_all.shape[1] // 3
    totals = [None] * 3
    for r in range(PARTS):
        span = slice(r * block, (r + 1) * block)
        x, onward = x_refs[r][...], 0.0
        for at, of_heads in enumerate(grads):
            wide = jnp.concatenate([ref[span, :] for ref in of_heads], axis=1)
            low = mm_nt(wide, spread[...]).astype(LOW)
            term = mm_tn(x, low)
            totals[at] = term if r == 0 else totals[at] + term
            onward = onward + mm_nt(low, w_all[:, at * columns : (at + 1) * columns])
        if r % 2 == 0:
            near_out[r // 2] = onward
        else:
            far_out[r // 2] = onward.astype(LOW)
    for at, total in enumerate(totals):
        terms[:, at * columns : (at + 1) * columns] = total.astype(LOW)
    terms[:, 3 * columns :] = out_terms[...]
    split_terms(meta, terms, outs)
    for distance, out in enumerate(outs):
        out[rows:, :] = jnp.zeros((EXTRA, terms.shape[1]), LOW)
        for block_at in range(pieces):

            @pl.when(meta[0, DP] ^ distance == block_at)
            def _(out=out, block_at=block_at):
                out[rows : rows + 8, :rows] = sums[:, block_at * rows : (block_at + 1) * rows].astype(LOW)


def join_rows_kernel(meta, *refs):
    out = refs[-1]
    rows = refs[0].shape[0]
    for r in range(PARTS):
        low = pl.multiple_of((meta[0, PART] ^ r) * rows, rows)
        out[pl.ds(low, rows), :] = refs[r][...].astype(FULL)


def join_columns_kernel(meta, *refs):
    outs, held = refs[PARTS:-1], refs[-1]
    step = outs[0].shape[0]
    for r in range(PARTS):
        held[meta[0, PART] ^ r] = refs[r][...]
    for at, out in enumerate(outs):
        for part in range(PARTS):
            value = held[part, at].astype(FULL)
            for block in range(value.shape[1] // step):
                start = (block * PARTS + part) * step
                out[:, start : start + step] = value[:, block * step : (block + 1) * step]


def join_projections_kernel(meta, *refs):
    outs, sum_outs, held = refs[PARTS:-5], refs[-5:-1], refs[-1]
    rows, columns = outs[0].shape[0], refs[0].shape[1] // len(outs)
    for r in range(PARTS):
        held[meta[0, PART] ^ r] = refs[r][...]
    sums = jnp.zeros((8, rows), FULL)
    for part in range(PARTS):
        value = held[part].astype(FULL)
        for at, out in enumerate(outs):
            out[:, part * columns : (part + 1) * columns] = value[:rows, at * columns : (at + 1) * columns]
        sums = sums + value[rows : rows + 8, :rows]
    for at, out in enumerate(sum_outs):
        out[...] = sums[at]


def gather_pieces(own, bits, starts=None, gate=None):
    held = {0: own}
    for bit in bits:
        for distance in list(held):
            source = held[distance]
            if distance == 0 and starts is not None:
                source = after(source, *starts)
            elif distance != 0 and gate is not None:
                source = after(source, gate)
            held[distance | bit] = hop(source, "dp", bit)
    return [held[distance] for distance in range(len(held))]


def send_terms(chunks, gate=None):
    return [
        hop(chunk if gate is None else after(chunk, *gate), "dp", distance)
        for distance, chunk in enumerate(chunks)
        if distance
    ]


def sum_terms(chunks, got):
    total = chunks[0].astype(FULL)
    for one in got:
        total = total + one.astype(FULL)
    return total


def shards(
    tokens, lengths, w_query, w_key, w_value, w_output, w_gate, w_up, w_down,
    first_gain, first_bias, second_gain, second_bias, cotangent,
):
    _, _, local, width = tokens.shape
    dp_count, blk_count = lax.axis_size("dp"), lax.axis_size("blk")
    dp, blk = lax.axis_index("dp"), lax.axis_index("blk")
    side = blk_count // 2
    which = blk // side
    first = which == 0
    core, part = blk % 2, blk % PARTS
    heads = width // HEAD_DIM // PARTS
    columns = heads * HEAD_DIM
    rows, ff_rows = w_query.shape[0], w_down.shape[0]
    half, ff = rows // 2, w_gate.shape[1]
    block = 2 * local
    row_count = PARTS * block
    spread_bits = bits_between(PARTS, side)
    sum_bits = bits_between(PARTS, blk_count)
    dp_bits = bits_between(1, dp_count)
    back_bits = dp_bits[::-1]
    table = jnp.asarray(turn_table(local * blk_count))
    swap_q, swap_k, spread_v = (
        jnp.asarray(swap_matrix(heads, 3 * columns, at * columns, at < 2), LOW) for at in range(3)
    )
    spread = jnp.asarray(swap_matrix(heads, columns, 0, False), LOW)

    starts = [(blk ^ distance ^ away) * local for distance in range(side) for away in (0, side)]
    meta = jnp.stack([which, core, part, dp, *starts]).astype(jnp.int32).reshape(1, -1)

    gate_up_own = call(
        pack_second_kernel, [shape((2 * PARTS, half, width))], [SMEM] + [VMEM] * 2, [], meta, w_gate, w_up
    )[0]
    gate_up_core = lax.all_gather(gate_up_own, "dp", axis=0, tiled=False)
    tok_send, cot_send, qkv_own, down_own = call(
        pack_first_kernel,
        [shape((local, width)), shape((local, width)), shape((rows + EXTRA + half + half // 3, 3 * columns))]
        + [shape((PARTS, half, width))],
        [SMEM] + [VMEM] * 11, [], after(meta, gate_up_own), tokens, cotangent, w_query, w_key, w_value, w_output, w_down,
        first_gain, first_bias, second_gain, second_bias,
    )
    tok_got = hop(tok_send, "blk", side)
    qkv = gather_pieces(qkv_own, dp_bits)
    x_own = jnp.concatenate([jnp.where(first, tokens[0, 0], tokens[1, 0]), tok_got])
    x_core, x_near = hop(x_own, "blk", 1), hop(x_own, "blk", 2)
    x_far = hop(after(x_near, x_core, *(qkv[bit] for bit in dp_bits)), "blk", 1)
    x_all = [x_own, x_core, x_near, x_far]
    down_pieces = {0: down_own}
    for bit in dp_bits[:2]:
        down_pieces[bit] = hop(after(down_own, *qkv[1:]), "dp", bit)
    cot_got = hop(after(cot_send, x_near), "blk", side)

    wide_shape = shape((row_count, WIDE))
    made = call(
        functools.partial(project_kernel, heads, dp_count), [wide_shape] * (3 * heads),
        [SMEM] + [VMEM] * (4 + PARTS + dp_count),
        [pltpu.VMEM((width, 3 * columns), LOW), pltpu.VMEM((row_count, 2 * WIDE), FULL)],
        after(meta, cot_got), table, swap_q, swap_k, spread_v, *x_all, *qkv,
    )
    queries, keys, values = (made[at * heads : (at + 1) * heads] for at in range(3))
    out_rows = rows + EXTRA
    qkv_core = hop(after(jnp.stack([piece[out_rows:] for piece in qkv[1:]]), queries[0]), "blk", 1)
    for bit in spread_bits:
        keys, values = ([jnp.concatenate([one, hop(one, "blk", bit)]) for one in many] for many in (keys, values))
    key_count = keys[0].shape[0]
    q_block = max(WIDE, min(row_count, 512 * 1024 // key_count))
    attended = call(
        functools.partial(attend_kernel, heads, q_block),
        [shape((PARTS, block, columns))] + [shape((1, row_count), FULL)] * heads,
        [SMEM] * 2 + [VMEM] * (1 + 3 * heads),
        [pltpu.VMEM((row_count, heads * WIDE), LOW)],
        meta, lengths, *queries, *keys, *values, spread,
    )
    attended, lse = attended[0], attended[1:]
    att_send = after(attended, qkv_core, *(down_pieces[bit] for bit in dp_bits[:2]))
    att_core, att_near = hop(att_send, "blk", 1), hop(att_send, "blk", 2)
    att_all = [attended, att_core, att_near, hop(after(att_near, att_core), "blk", 1)]
    middle = PARTS // 2
    down_pieces[3] = jnp.concatenate(
        [hop(down_pieces[1][:middle], "dp", 2), hop(down_pieces[2][middle:], "dp", 1)]
    )
    for bit in dp_bits[2:]:
        for distance in range(bit):
            down_pieces[distance | bit] = hop(down_pieces[distance], "dp", bit)
    down_pieces = [down_pieces[distance] for distance in range(dp_count)]
    residual_one, normed_low, all_vectors, w_o = call(
        functools.partial(residual_kernel, dp_count),
        [shape((block, width), FULL), shape((block, width)), shape((8, width), FULL), shape((columns, width))],
        [SMEM] + [VMEM] * (2 + PARTS + dp_count + 1),
        [pltpu.VMEM((width, width), LOW), pltpu.VMEM((dp_count, EXTRA, 3 * columns), LOW)],
        after(meta, down_pieces[3]), x_own, w_output, *att_all, *qkv, qkv_core,
    )
    normed_core, normed_near = hop(normed_low, "blk", 1), hop(normed_low, "blk", 2)
    down_core = [hop(after(piece, normed_low), "blk", 1) for piece in down_pieces[1:]]
    down_all = (w_down, *down_pieces[1:], *down_core)
    gate_up_all = (gate_up_core, hop(after(gate_up_core, att_all[3], down_pieces[3]), "blk", 1))

    part_shape, w_shape = (PARTS, block, width), (dp_count, rows, width)
    down_copies = 2 * dp_count - 1
    grad_ffn, grad_branch, grad_one, layer_own, layer_back, sums = call(
        feed_kernel,
        [shape((block, width))] * 2 + [shape((block, width), FULL)] + [shape((local, width))] * 2
        + [shape((8, width), FULL)],
        [SMEM] * 2 + [VMEM] * 4 + [ANY] * (2 + len(down_all)),
        [
            pltpu.VMEM((3 * PARTS, *w_shape), LOW),
            pltpu.VMEM(part_shape, FULL),
            pltpu.VMEM(part_shape, FULL),
            pltpu.SemaphoreType.DMA((PARTS * (4 + down_copies),)),
        ],
        after(meta, normed_core), lengths, residual_one, all_vectors, cotangent, cot_got, *gate_up_all, *down_all,
    )
    ffn_core, ffn_near = hop(grad_ffn, "blk", 1), hop(grad_ffn, "blk", 2)
    normed_all = [normed_low, normed_core, normed_near, hop(after(normed_near, grad_ffn), "blk", 1)]

    long, chunk = shape((row_count, width)), shape((rows, width))
    hidden, gate_factor, up_factor = call(
        hidden_kernel, [long] * 3,
        [SMEM] + [VMEM] * PARTS + [ANY] * 2,
        [pltpu.VMEM(w_shape, LOW), pltpu.VMEM(w_shape, LOW), pltpu.SemaphoreType.DMA((4,))],
        after(meta, grad_ffn), *normed_all, *gate_up_all,
    )
    ffn_all = [grad_ffn, ffn_core, ffn_near, hop(after(ffn_near, hidden, ffn_core), "blk", 1)]
    branch_core, branch_near = (hop(after(grad_branch, ffn_near, hidden), "blk", bit) for bit in (1, 2))
    down_terms = call(
        down_kernel, [chunk] * dp_count, [SMEM] + [VMEM] * (1 + PARTS), [pltpu.VMEM((width, width), LOW)],
        after(meta, branch_core), hidden, *ffn_all,
    )
    down_got = send_terms(down_terms)
    gate_up_terms = call(
        gate_up_kernel, [chunk] * dp_count + [shape((width, width))],
        [SMEM] + [VMEM] * (2 + 2 * PARTS) + [ANY] * len(down_all),
        [pltpu.VMEM(w_shape, LOW), pltpu.VMEM((row_count, 2 * width), LOW)]
        + [pltpu.VMEM((width, width), LOW), pltpu.SemaphoreType.DMA((down_copies,))],
        after(meta, down_terms[0]), gate_factor, up_factor, *ffn_all, *normed_all, *down_all,
    )

    def sum_halves(total):
        for bit in sum_bits:
            low = total.astype(LOW)
            total = low.astype(FULL) + hop(low, "blk", bit).astype(FULL)
        return total.astype(LOW)

    branch_far = hop(after(branch_near, gate_up_terms[0], *(down_got[bit - 1] for bit in dp_bits)), "blk", 1)
    layer_got = hop(after(layer_back, branch_far), "blk", side)
    down_sum = sum_terms(down_terms, down_got)
    down_full = sum_halves(down_sum)
    gate_got = send_terms(gate_up_terms[:dp_count])
    up_sum = lax.psum_scatter(
        after(gate_up_terms[-1], branch_far).reshape(dp_count, rows, width), "dp", scatter_dimension=0, tiled=False
    )
    early = heads if spread_bits else heads - 1
    key_shape = shape((key_count, WIDE))
    back_scratch = [pltpu.VMEM((key_count, WIDE), FULL), pltpu.VMEM((key_count, 2 * WIDE), FULL)]
    back_scratch += [pltpu.VMEM((key_count, WIDE), FULL)] * 2
    *made, out_terms = call(
        functools.partial(attend_back_kernel, early, q_block),
        [wide_shape] * early + [key_shape] * (2 * early) + [wide_shape] * (heads - early) + [shape((width, columns))],
        [SMEM] * 2 + [VMEM] * (3 + 2 * PARTS + 4 * early),
        [pltpu.VMEM((PARTS, block, columns), LOW), *back_scratch] + [pltpu.VMEM((row_count, WIDE), LOW)] * early,
        after(meta, down_sum), lengths, w_o, spread, table,
        grad_branch, branch_core, branch_near, branch_far, *att_all,
        *queries[:early], *keys[:early], *values[:early], *lse[:early],
    )
    grad_q, grad_k, grad_v = (made[at * early : (at + 1) * early] for at in range(3))
    gate_sum = sum_terms(gate_up_terms, [after(got, grad_q[0], layer_got) for got in gate_got])
    gate_full = sum_halves(gate_sum)
    down_near = hop(down_full, "blk", 2)
    for bit in reversed(spread_bits):
        middle = grad_k[0].shape[0] // 2
        grad_k, grad_v = (
            [
                (one[:middle].astype(FULL) + hop(one[middle:], "blk", bit).astype(FULL)).astype(LOW)
                for one in many
            ]
            for many in (grad_k, grad_v)
        )
    back_outs = [shape((rows + EXTRA, width))] * dp_count + [shape((2, block, width), FULL), shape((2, block, width))]
    back_weights = [pltpu.VMEM((width, 3 * columns), LOW), pltpu.VMEM((width, width), LOW)]
    back_operands = (spread, sums, out_terms, *grad_q, *grad_k, *grad_v, *x_all, *qkv)
    ready = after(meta, gate_sum, down_full)
    if spread_bits:
        made = call(
            functools.partial(projections_back_kernel, heads, dp_count), back_outs,
            [SMEM] + [VMEM] * len(back_operands), back_weights, ready, *back_operands,
        )
    else:
        made = call(
            functools.partial(last_back_kernel, heads, dp_count, q_block), back_outs,
            [SMEM] * 2 + [VMEM] * (6 + len(back_operands)),
            back_weights + [pltpu.VMEM((row_count, WIDE), LOW)] * 3 + back_scratch,
            ready, lengths, table, queries[-1], keys[-1], values[-1], lse[-1], made[-1], *back_operands,
        )
    *qkv_terms, token_keep, token_send = made
    up_sum = after(up_sum, token_keep).astype(FULL)

    first_gate = (gate_full, up_sum, down_near)
    token_got = hop(after(token_send, *first_gate), "blk", 1).astype(FULL)
    up_full = sum_halves(up_sum)
    near_send = (token_keep[1] + token_got[1]).astype(LOW)
    token_near = hop(near_send, "blk", 2)
    qkv_got = send_terms(qkv_terms)
    qkv_sum = sum_terms(qkv_terms, [after(got, token_near) for got in qkv_got]).astype(LOW)
    qkv_full = sum_halves(after(qkv_sum, up_full, token_near))
    pair_full = after(jnp.stack([gate_full, up_full]), qkv_sum)
    pair_core, pair_near = hop(pair_full, "blk", 1), hop(pair_full, "blk", 2)
    down_core, down_far = (hop(after(one, pair_core), "blk", 1) for one in (down_full, down_near))
    grad_rows = after(grad_one, qkv_sum) + token_keep[0] + token_got[0] + token_near.astype(FULL)
    rows_got = hop(grad_rows[local:].astype(LOW), "blk", side).astype(FULL)
    grad_down = call(
        join_rows_kernel, [shape((ff_rows, width), FULL)], [SMEM] + [VMEM] * PARTS, [],
        meta, down_full, down_core, down_near, down_far,
    )[0]
    pair_far = hop(after(pair_near, pair_core, grad_down), "blk", 1)
    qkv_core, qkv_near = (hop(after(qkv_full, pair_near), "blk", bit) for bit in (1, 2))
    grad_gate, grad_up = call(
        join_columns_kernel, [shape((rows, ff), FULL)] * 2, [SMEM] + [VMEM] * PARTS,
        [pltpu.VMEM((PARTS, 2, rows, width), LOW)], meta, pair_full, pair_core, pair_near, pair_far,
    )
    qkv_far = hop(after(qkv_near, qkv_core, grad_gate, rows_got), "blk", 1)
    grad_tokens = jnp.where(
        first, jnp.stack([grad_rows[:local], rows_got]), jnp.stack([rows_got, grad_rows[:local]])
    )[:, None]
    layer_out = jnp.where(first, jnp.stack([layer_own, layer_got]), jnp.stack([layer_got, layer_own]))[:, None]
    grad_query, grad_key, grad_value, grad_output, *vector_sums = call(
        join_projections_kernel, [shape((rows, width), FULL)] * 4 + [shape((rows,), FULL)] * 4,
        [SMEM] + [VMEM] * PARTS, [pltpu.VMEM((PARTS, rows + EXTRA, width), LOW)], meta, qkv_full, qkv_core, qkv_near, qkv_far,
    )
    return (
        layer_out, grad_tokens, grad_query, grad_key, grad_value, grad_output, grad_gate, grad_up, grad_down,
        vector_sums[0], vector_sums[1], vector_sums[2], vector_sums[3],
    )


def solution(mesh):
    slots = P(None, "dp", "blk", None)
    matrix, vector = P("dp", None), P("dp")
    return jax.shard_map(
        shards,
        mesh=mesh,
        in_specs=(slots, P(None, "dp")) + (matrix,) * 7 + (vector,) * 4 + (slots,),
        out_specs=(slots, slots) + (matrix,) * 7 + (vector,) * 4,
        check_vma=False,
    )
```

```python
import functools

import jax
import jax.numpy as jnp
import numpy as np
from jax import lax
from jax.experimental import pallas as pl
from jax.experimental.pallas import tpu as pltpu
from jax.sharding import PartitionSpec as P

HEAD_DIM = 64
WIDE = 128
PARTS = 4
EXTRA = 16
LOW, FULL = jnp.bfloat16, jnp.float32
VMEM_MIB = {"join_rows_kernel": 30, "join_columns_kernel": 30, "join_projections_kernel": 30, "hidden_kernel": 40, "down_kernel": 40, "gate_up_kernel": 40}
VMEM = pl.BlockSpec(memory_space=pltpu.VMEM)
SMEM = pl.BlockSpec(memory_space=pltpu.SMEM)
ANY = pl.BlockSpec(memory_space=pl.ANY)
WHICH, CORE, PART, DP, STARTS = 0, 1, 2, 3, 4


def mm(left, right):
    return jnp.dot(left, right, preferred_element_type=FULL)


def mm_nt(left, right):
    return lax.dot_general(left, right, (((1,), (1,)), ((), ())), preferred_element_type=FULL)


def mm_tn(left, right):
    return lax.dot_general(left, right, (((0,), (0,)), ((), ())), preferred_element_type=FULL)


def hop(value, axis, bit):
    size = lax.axis_size(axis)
    return lax.ppermute(value, axis, [(at, at ^ bit) for at in range(size)])


def after(value, *others):
    return lax.optimization_barrier((value, *others))[0]


def bits_between(low, high):
    bits = []
    while low < high:
        bits.append(low)
        low *= 2
    return bits


def turn_table(seq_len):
    half = HEAD_DIM // 2
    frequency = np.float32(1000.0) ** (
        -(np.arange(half, dtype=np.float32) * np.float32(2.0) / np.float32(HEAD_DIM))
    )
    angles = np.arange(seq_len, dtype=np.float32)[:, None] * frequency[None, :]
    cosine = np.cos(angles).astype(np.float32)
    sine = np.sin(angles).astype(np.float32)
    return np.concatenate([cosine] * 4 + [sine, sine, -sine, -sine], axis=1)


def swap_matrix(heads, total, first, swapped):
    half = HEAD_DIM // 2
    out = np.zeros((total, heads * WIDE), np.float32)
    for h in range(heads):
        for f in range(HEAD_DIM):
            out[first + h * HEAD_DIM + f, h * WIDE + f] = 1.0
        for f in range(half if swapped else 0):
            out[first + h * HEAD_DIM + half + f, h * WIDE + HEAD_DIM + f] = -1.0
            out[first + h * HEAD_DIM + f, h * WIDE + HEAD_DIM + half + f] = 1.0
    return out


def call(body, outs, in_specs, scratch, *operands):
    name = getattr(body, "func", body).__name__
    return pl.pallas_call(
        body,
        out_shape=outs,
        in_specs=in_specs,
        out_specs=[VMEM] * len(outs),
        scratch_shapes=scratch,
        name=getattr(body, "func", body).__name__,
        compiler_params=pltpu.CompilerParams(vmem_limit_bytes=VMEM_MIB.get(name, 60) * 1024 * 1024),
        cost_estimate=pl.CostEstimate(flops=1000, bytes_accessed=1000, transcendentals=0),
    )(*operands)


def shape(dims, dtype=LOW):
    return jax.ShapeDtypeStruct(dims, dtype)


def norm_parts(rows):
    centred = rows - jnp.mean(rows, axis=-1, keepdims=True)
    scale = lax.rsqrt(jnp.mean(centred * centred, axis=-1, keepdims=True) + 1e-05)
    return centred * scale, scale


def norm_back(upstream, gain, unit, scale):
    inner = upstream * gain
    centre = jnp.mean(inner, axis=-1, keepdims=True)
    along = jnp.mean(inner * unit, axis=-1, keepdims=True)
    sums = (jnp.sum(upstream * unit, axis=0, keepdims=True), jnp.sum(upstream, axis=0, keepdims=True))
    return (inner - centre - unit * along) * scale, sums


def pack_first_kernel(
    meta, tokens, cot, w_q, w_k, w_v, w_o, w_down, gain_one, bias_one, gain_two, bias_two, tok_out, cot_out, qkv_out, down_out
):
    rows, columns = w_q.shape[0], qkv_out.shape[1] // 3
    half, third = rows // 2, rows // 6
    other = 1 - meta[0, WHICH]
    tok_out[...] = tokens[other, 0]
    cot_out[...] = cot[other, 0]
    for part in range(PARTS):

        @pl.when(meta[0, PART] == part)
        def _(part=part):
            for at, w in enumerate((w_q, w_k, w_v)):
                qkv_out[:rows, at * columns : (at + 1) * columns] = w[:, part * columns : (part + 1) * columns]

    qkv_out[rows : rows + EXTRA, :] = jnp.zeros((EXTRA, 3 * columns), LOW)
    vectors = [vector[...].reshape(1, rows).astype(FULL) for vector in (gain_one, bias_one, gain_two, bias_two)]
    vectors = jnp.concatenate([*vectors, jnp.zeros((EXTRA - 4, rows), FULL)], axis=0)
    qkv_out[rows : rows + EXTRA, :rows] = vectors.astype(LOW)
    for part in range(PARTS):
        low = pl.multiple_of(part * rows + meta[0, CORE] * half, half)
        down_out[part] = w_down[pl.ds(low, half), :]
    out_rows = w_o[pl.ds(pl.multiple_of(meta[0, CORE] * half, half), half), :]
    at = rows + EXTRA
    qkv_out[at : at + half, :] = out_rows[:, : 3 * columns]
    at += half
    for g in range(3):
        qkv_out[at : at + third, g * columns : (g + 1) * columns] = out_rows[g * third : (g + 1) * third, 3 * columns :]


def pack_second_kernel(meta, w_gate, w_up, out):
    half, width = out.shape[1], out.shape[2]
    step = 2 * half
    low = pl.multiple_of(meta[0, CORE] * half, half)
    for base, w in ((0, w_gate), (PARTS, w_up)):
        for part in range(PARTS):
            for block in range(width // step):
                start = (block * PARTS + part) * step
                out[base + part, :, block * step : (block + 1) * step] = w[pl.ds(low, half), start : start + step]


def project_kernel(heads, pieces, meta, table_ref, swap_q, swap_k, spread_v, *refs):
    x_refs, w_refs, (q_refs, k_refs, v_refs) = refs[:PARTS], refs[PARTS : PARTS + pieces], [refs[-2 - 3 * heads + at * heads : -2 - 2 * heads + at * heads] for at in range(3)]
    w_all, turn = refs[-2:]
    rows = w_all.shape[0] // pieces
    block = x_refs[0].shape[0]
    local = block // 2
    for distance, w in enumerate(w_refs):
        w_all[pl.ds(pl.multiple_of((meta[0, DP] ^ distance) * rows, rows), rows), :] = w[:rows, :]
    for at in range(2 * PARTS):
        start = pl.multiple_of(meta[0, STARTS + at], local)
        turn[at * local : (at + 1) * local, :] = table_ref[pl.ds(start, local), :]
    weights = w_all[...]
    w_q, w_k, w_v = (mm(weights, m[...]).astype(LOW) for m in (swap_q, swap_k, spread_v))
    for r in range(PARTS):
        out_rows = slice(r * block, (r + 1) * block)
        x = x_refs[r][...]
        cosine, sine = turn[out_rows, :WIDE], turn[out_rows, WIDE:]
        for out_refs, w, scale in ((q_refs, w_q, 0.0625), (k_refs, w_k, None)):
            made = mm(x, w)
            for h in range(heads):
                one = made[:, h * WIDE : (h + 1) * WIDE]
                turned = (one * cosine + pltpu.roll(one, HEAD_DIM, 1) * sine).astype(LOW)
                out_refs[h][out_rows, :] = turned if scale is None else turned * jnp.asarray(scale, LOW)
        made = mm(x, w_v).astype(LOW)
        for h in range(heads):
            v_refs[h][out_rows, :] = made[:, h * WIDE : (h + 1) * WIDE]


def fill_bias(meta, length, bias_ref, local):
    for at in range(bias_ref.shape[0] // local):
        place = meta[0, STARTS + at] + lax.broadcasted_iota(jnp.int32, (local, WIDE), 0)
        bias_ref[at * local : (at + 1) * local, :] = jnp.where(place < length, 0.0, -1e30)


def each_block(count, step):
    if count <= 4:
        for number in range(count):
            step(number)
    else:
        lax.fori_loop(0, count, lambda number, carry: step(number) or carry, 0)


def block_rows(number, block):
    if isinstance(number, int):
        return slice(number * block, (number + 1) * block)
    return pl.ds(pl.multiple_of(number * block, block), block)


def attend_kernel(heads, block, meta, lengths, *refs):
    q_refs, k_refs, v_refs, spread_ref = refs[:heads], refs[heads : 2 * heads], refs[2 * heads : 3 * heads], refs[3 * heads]
    out, lse_refs, wide_ref = refs[3 * heads + 1], refs[-1 - heads : -1], refs[-1]
    row_count, key_count = q_refs[0].shape[0], k_refs[0].shape[0]
    span = row_count // PARTS
    local = span // 2
    length = lengths[meta[0, WHICH], 0]
    places = [meta[0, STARTS + at] + lax.broadcasted_iota(jnp.int32, (1, local), 1) for at in range(key_count // local)]
    bias = jnp.where(jnp.concatenate(places, axis=1) < length, 0.0, -1e30)
    for h in range(heads):

        def step(number, h=h):
            rows = block_rows(number, block)
            scores = mm_nt(q_refs[h][rows, :], k_refs[h][...]) + bias
            top = jnp.max(scores, axis=1, keepdims=True)
            weights = jnp.exp(scores - top)
            total = jnp.sum(weights, axis=1, keepdims=True)
            wide_ref[rows, h * WIDE : (h + 1) * WIDE] = (mm(weights.astype(LOW), v_refs[h][...]) / total).astype(LOW)
            lse_refs[h][:, rows] = jnp.broadcast_to(top + jnp.log(total), (block, WIDE)).T[:1, :]

        each_block(row_count // block, step)
    for r in range(PARTS):
        out[r] = mm_nt(wide_ref[r * span : (r + 1) * span, :], spread_ref[...]).astype(LOW)


class Turn:
    def __init__(self, meta, lengths, table_ref, bias_ref, turn, local):
        fill_bias(meta, lengths[meta[0, WHICH], 0], bias_ref, local)
        for at in range(turn.shape[0] // local):
            start = pl.multiple_of(meta[0, STARTS + at], local)
            turn[at * local : (at + 1) * local, :] = table_ref[pl.ds(start, local), :]
        self.turn = turn

    def back(self, value, rows):
        cosine, sine = self.turn[rows, :WIDE], self.turn[rows, WIDE:]
        return (value * cosine - pltpu.roll(value, HEAD_DIM, 1) * sine).astype(LOW)


def back_head(block, turn, bias_ref, sums, q_ref, k_ref, v_ref, lse_ref, grad_ref, dq_ref, dk_ref, dv_ref):
    dk_sum, dv_sum = sums
    keys, values = k_ref[...], v_ref[...]
    keys_t = keys.T
    dk_sum[...] = jnp.zeros_like(dk_sum)
    dv_sum[...] = jnp.zeros_like(dv_sum)

    def step(number):
        rows = block_rows(number, block)
        bias = jnp.concatenate([bias_ref[...]] * (block // WIDE), axis=1)
        queries, grads = q_ref[rows, :], grad_ref[rows, :]
        probs = jnp.exp(mm_nt(keys, queries) + bias - lse_ref[:, rows])
        grad_probs = mm_nt(values, grads)
        delta = jnp.sum(probs * grad_probs, axis=0, keepdims=True)
        grad_scores = (probs * (grad_probs - delta)).astype(LOW)
        dv_sum[...] += mm(probs.astype(LOW), grads)
        dk_sum[...] += mm(grad_scores, queries)
        dq_ref[rows, :] = turn.back(mm(keys_t, grad_scores).T * 0.125, rows)

    each_block(q_ref.shape[0] // block, step)
    dk_ref[...] = turn.back(dk_sum[...] * 2.0, slice(None))
    dv_ref[...] = dv_sum[...].astype(LOW)


def attend_back_kernel(heads, block, meta, lengths, w_o, spread_ref, table_ref, *refs):
    grads_in, att_in, refs = refs[:PARTS], refs[PARTS : 2 * PARTS], refs[2 * PARTS :]
    ins, refs = [refs[at * heads : (at + 1) * heads] for at in range(4)], refs[4 * heads :]
    outs, refs = [refs[at * heads : (at + 1) * heads] for at in range(3)], refs[3 * heads :]
    *later, dw_ref, grad_part, bias_ref, turn_ref, dk_sum, dv_sum = refs[: -heads]
    wide = [*refs[-heads:], *later]
    columns = w_o.shape[0]
    weights = mm_tn(spread_ref[...], w_o[...]).astype(LOW)
    span = grads_in[0].shape[0]
    for r in range(PARTS):
        made = mm_nt(grads_in[r][...], weights).astype(LOW)
        for h, out in enumerate(wide):
            out[r * span : (r + 1) * span, :] = made[:, h * WIDE : (h + 1) * WIDE]
        for part in range(PARTS):

            @pl.when(meta[0, PART] == part)
            def _(r=r, part=part):
                grad_part[r] = grads_in[r][:, part * columns : (part + 1) * columns]

    for distance in range(PARTS):
        total = mm_tn(att_in[distance][distance], grad_part[0])
        for r in range(1, PARTS):
            total = total + mm_tn(att_in[distance][r ^ distance], grad_part[r])
        low = pl.multiple_of((meta[0, PART] ^ distance) * columns, columns)
        dw_ref[pl.ds(low, columns), :] = total.astype(LOW)
    turn = Turn(meta, lengths, table_ref, bias_ref, turn_ref, span // 2)
    for h in range(heads):
        q_ref, k_ref, v_ref, lse_ref = (some[h] for some in ins)
        back_head(block, turn, bias_ref, (dk_sum, dv_sum), q_ref, k_ref, v_ref, lse_ref, wide[h], *(o[h] for o in outs))


def place_gate_up(meta, refs, block, target, sems, at):
    half = refs[0].shape[2]
    copies = []
    for side, ref in enumerate(refs):
        low = pl.multiple_of((meta[0, CORE] ^ side) * half, half)
        copy = pltpu.make_async_copy(ref.at[:, block], target.at[:, pl.ds(low, half), :], sems.at[at + side])
        copy.start()
        copies.append(copy)
    return copies, at + 2


def place_down(meta, own, refs, block, target, sems, at):
    count, rows = target.shape[0], target.shape[1]
    half = rows // 2
    low = pl.multiple_of(block * rows, rows)
    copies = [pltpu.make_async_copy(own.at[pl.ds(low, rows), :], target.at[meta[0, DP]], sems.at[at])]
    for number, ref in enumerate(refs):
        distance, side = number % (count - 1) + 1, number // (count - 1)
        low = pl.multiple_of((meta[0, CORE] ^ side) * half, half)
        to = target.at[meta[0, DP] ^ distance, pl.ds(low, half), :]
        copies.append(pltpu.make_async_copy(ref.at[block], to, sems.at[at + 1 + number]))
    for copy in copies:
        copy.start()
    return copies, at + len(copies)


def wait_all(copies):
    for copy in copies:
        copy.wait()


def residual_kernel(pieces, meta, x_ref, w_own, *refs):
    att, w_refs, w_core, refs = refs[:PARTS], refs[PARTS : PARTS + pieces], refs[PARTS + pieces], refs[PARTS + pieces + 1 :]
    residual_out, low_out, vector_out, w_out, w_o, gathered = refs
    columns, rows = att[0].shape[2], w_own.shape[0]
    half, third = rows // 2, rows // 6
    w_o[pl.ds(pl.multiple_of(meta[0, DP] * rows, rows), rows), :] = w_own[...]

    def fill(ref, low):
        w_o[pl.ds(pl.multiple_of(low, half), half), : 3 * columns] = ref[:half, :]
        for g in range(3):
            to = pl.ds(pl.multiple_of(low + g * third, third), third)
            w_o[to, 3 * columns :] = ref[half:, g * columns : (g + 1) * columns]

    for distance, ref in enumerate(w_refs):
        gathered[meta[0, DP] ^ distance] = ref[rows : rows + EXTRA, :]
        if distance:
            low = (meta[0, DP] ^ distance) * rows
            fill(ref[rows + EXTRA :, :], low + meta[0, CORE] * half)
            fill(w_core[distance - 1], low + (1 - meta[0, CORE]) * half)
    vectors = jnp.concatenate([gathered[d][:, :rows] for d in range(pieces)], axis=1).astype(FULL)[:8]
    vector_out[...] = vectors
    residual = x_ref[...].astype(FULL)
    for r in range(PARTS):
        low = pl.multiple_of((meta[0, PART] ^ r) * columns, columns)
        residual = residual + mm(att[r][r], w_o[pl.ds(low, columns), :])
    w_out[...] = w_o[pl.ds(pl.multiple_of(meta[0, PART] * columns, columns), columns), :]
    residual_out[...] = residual
    unit, _ = norm_parts(residual)
    low_out[...] = (unit * vectors[0:1] + vectors[1:2]).astype(LOW)


def feed_kernel(meta, lengths, residual_ref, vectors, cot_ref, cot_got, *refs):
    gu_refs, down_own, down_refs, refs = refs[:2], refs[2], refs[3:-10], refs[-10:]
    grad_ffn_out, grad_branch_out, grad_one_out, own_out, back_out, sums_out, held, gates, ups, sems = refs
    width = residual_ref.shape[1]
    copies, at = [], 0
    for part in range(PARTS):
        gate, at = place_gate_up(meta, gu_refs, part, held.at[part], sems, at)
        up, at = place_gate_up(meta, gu_refs, PARTS + part, held.at[PARTS + part], sems, at)
        down, at = place_down(meta, down_own, down_refs, part, held.at[2 * PARTS + part], sems, at)
        copies.append(gate + up + down)

    def weights(number):
        return held[number].reshape(width, width)

    which = meta[0, WHICH]
    local = cot_got.shape[0]
    unit_one, scale_one = norm_parts(residual_ref[...])
    normed = unit_one * vectors[0:1] + vectors[1:2]
    normed_low = normed.astype(LOW)
    residual = normed

    def pre(part):
        wait_all(copies[part])
        return mm(normed_low, weights(part)), mm(normed_low, weights(PARTS + part))

    ahead = pre(0)
    for part in range(PARTS):
        gate, up = ahead
        if part + 1 < PARTS:
            ahead = pre(part + 1)
        sigma = 0.5 * jnp.tanh(0.5 * gate) + 0.5
        silu = gate * sigma
        residual = residual + mm((silu * up).astype(LOW), weights(2 * PARTS + part))
        gates[part] = up * (sigma + silu * (1.0 - sigma))
        ups[part] = silu
    unit_two, scale_two = norm_parts(residual)
    layer = unit_two * vectors[2:3] + vectors[3:4]
    length = lengths[which, 0]
    upstream = []
    for half, (out, cot) in enumerate(((own_out, cot_ref[which, 0]), (back_out, cot_got[...]))):
        place = meta[0, STARTS + half] + lax.broadcasted_iota(jnp.int32, (local, 1), 0)
        valid = place < length
        out[...] = jnp.where(valid, layer[half * local : (half + 1) * local], 0.0).astype(LOW)
        upstream.append(jnp.where(valid, cot.astype(FULL), 0.0))
    grad_two, sums_two = norm_back(jnp.concatenate(upstream, axis=0), vectors[2:3], unit_two, scale_two)
    grad_ffn = grad_two.astype(LOW)
    grad_ffn_out[...] = grad_ffn
    grad_normed = grad_two
    for part in range(PARTS):
        grad_hidden = mm_nt(grad_ffn, weights(2 * PARTS + part))
        grad_normed = (
            grad_normed
            + mm_nt((grad_hidden * gates[part]).astype(LOW), weights(part))
            + mm_nt((grad_hidden * ups[part]).astype(LOW), weights(PARTS + part))
        )
    grad_one, sums_one = norm_back(grad_normed, vectors[0:1], unit_one, scale_one)
    grad_one_out[...] = grad_one
    grad_branch_out[...] = grad_one.astype(LOW)
    sums_out[...] = jnp.concatenate([*sums_one, *sums_two, jnp.zeros((4, width), FULL)], axis=0)


def hidden_kernel(meta, *refs):
    x_refs, gu_refs, refs = refs[:PARTS], refs[PARTS : PARTS + 2], refs[PARTS + 2 :]
    hidden_out, gate_out, up_out, held_gate, held_up, sems = refs
    part, width = meta[0, PART], hidden_out.shape[1]
    first, at = place_gate_up(meta, gu_refs, part, held_gate, sems, 0)
    second, at = place_gate_up(meta, gu_refs, PARTS + part, held_up, sems, at)
    wait_all(first + second)
    w_gate, w_up = held_gate[...].reshape(width, width), held_up[...].reshape(width, width)
    block = x_refs[0].shape[0]
    for r in range(PARTS):
        rows = slice(r * block, (r + 1) * block)
        x = x_refs[r][...]
        gate, up = mm(x, w_gate), mm(x, w_up)
        sigma = 0.5 * jnp.tanh(0.5 * gate) + 0.5
        silu = gate * sigma
        hidden_out[rows, :] = (silu * up).astype(LOW)
        gate_out[rows, :] = (up * (sigma + silu * (1.0 - sigma))).astype(LOW)
        up_out[rows, :] = silu.astype(LOW)


def split_terms(meta, terms, outs):
    rows = terms.shape[0] // len(outs)
    for distance, out in enumerate(outs):
        low = pl.multiple_of((meta[0, DP] ^ distance) * rows, rows)
        out[:rows, :] = terms[pl.ds(low, rows), :]


def down_kernel(meta, hidden_ref, *refs):
    grads, outs, terms = refs[:PARTS], refs[PARTS:-1], refs[-1]
    block = grads[0].shape[0]
    total = mm_tn(hidden_ref[:block, :], grads[0][...])
    for r in range(1, PARTS):
        total = total + mm_tn(hidden_ref[r * block : (r + 1) * block, :], grads[r][...])
    terms[...] = total.astype(LOW)
    split_terms(meta, terms, outs)


def gate_up_kernel(meta, gate_ref, up_ref, *refs):
    grads, x_refs, down_own, refs = refs[:PARTS], refs[PARTS : 2 * PARTS], refs[2 * PARTS], refs[2 * PARTS + 1 :]
    held, low, terms, sems = refs[-4:]
    count = held.shape[0]
    down_refs, outs = refs[: 2 * count - 2], refs[2 * count - 2 : -4]
    width = terms.shape[0]
    copies, _ = place_down(meta, down_own, down_refs, meta[0, PART], held, sems, 0)
    wait_all(copies)
    w_down = held[...].reshape(terms.shape)
    block = grads[0].shape[0]
    for r in range(PARTS):
        rows = slice(r * block, (r + 1) * block)
        grad_hidden = mm_nt(grads[r][...], w_down)
        low[rows, :width] = (grad_hidden * gate_ref[rows, :].astype(FULL)).astype(LOW)
        low[rows, width:] = (grad_hidden * up_ref[rows, :].astype(FULL)).astype(LOW)
    total = mm_tn(x_refs[0][...], low[:block, :])
    for r in range(1, PARTS):
        total = total + mm_tn(x_refs[r][...], low[r * block : (r + 1) * block, :])
    terms[...] = total[:, :width].astype(LOW)
    split_terms(meta, terms, outs[:-1])
    outs[-1][...] = total[:, width:].astype(LOW)


def last_back_kernel(heads, pieces, block, meta, lengths, table_ref, q_ref, k_ref, v_ref, lse_ref, grad_ref, *refs):
    *refs, dq, dk, dv, bias_ref, turn_ref, dk_sum, dv_sum = refs
    turn = Turn(meta, lengths, table_ref, bias_ref, turn_ref, q_ref.shape[0] // PARTS // 2)
    back_head(block, turn, bias_ref, (dk_sum, dv_sum), q_ref, k_ref, v_ref, lse_ref, grad_ref, dq, dk, dv)
    count = heads - 1
    first = [refs[3 + at * count : 3 + (at + 1) * count] for at in range(3)]
    grads = [ref for some, last in zip(first, (dq, dk, dv)) for ref in (*some, last)]
    projections_back_kernel(heads, pieces, meta, *refs[:3], *grads, *refs[3 + 3 * count :])


def projections_back_kernel(heads, pieces, meta, spread, sums, out_terms, *refs):
    grads, refs = [refs[at * heads : (at + 1) * heads] for at in range(3)], refs[3 * heads :]
    x_refs, w_refs, refs = refs[:PARTS], refs[PARTS : PARTS + pieces], refs[PARTS + pieces :]
    outs, (near_out, far_out, w_all, terms) = refs[:pieces], refs[pieces:]
    rows = w_all.shape[0] // pieces
    for distance, w in enumerate(w_refs):
        w_all[pl.ds(pl.multiple_of((meta[0, DP] ^ distance) * rows, rows), rows), :] = w[:rows, :]
    block = x_refs[0].shape[0]
    columns = w_all.shape[1] // 3
    totals = [None] * 3
    for r in range(PARTS):
        span = slice(r * block, (r + 1) * block)
        x, onward = x_refs[r][...], 0.0
        for at, of_heads in enumerate(grads):
            wide = jnp.concatenate([ref[span, :] for ref in of_heads], axis=1)
            low = mm_nt(wide, spread[...]).astype(LOW)
            term = mm_tn(x, low)
            totals[at] = term if r == 0 else totals[at] + term
            onward = onward + mm_nt(low, w_all[:, at * columns : (at + 1) * columns])
        if r % 2 == 0:
            near_out[r // 2] = onward
        else:
            far_out[r // 2] = onward.astype(LOW)
    for at, total in enumerate(totals):
        terms[:, at * columns : (at + 1) * columns] = total.astype(LOW)
    terms[:, 3 * columns :] = out_terms[...]
    split_terms(meta, terms, outs)
    for distance, out in enumerate(outs):
        out[rows:, :] = jnp.zeros((EXTRA, terms.shape[1]), LOW)
        for block_at in range(pieces):

            @pl.when(meta[0, DP] ^ distance == block_at)
            def _(out=out, block_at=block_at):
                some = sums[:, block_at * rows : (block_at + 1) * rows]
                some = jnp.concatenate([some, jnp.zeros((EXTRA - some.shape[0], rows), FULL)], axis=0)
                out[rows : rows + EXTRA, :rows] = some.astype(LOW)


def join_rows_kernel(meta, *refs):
    out = refs[-1]
    rows = refs[0].shape[0]
    for r in range(PARTS):
        low = pl.multiple_of((meta[0, PART] ^ r) * rows, rows)
        out[pl.ds(low, rows), :] = refs[r][...].astype(FULL)


def join_columns_kernel(meta, *refs):
    outs, held = refs[PARTS:-1], refs[-1]
    step = outs[0].shape[0]
    for r in range(PARTS):
        held[meta[0, PART] ^ r] = refs[r][...]
    for at, out in enumerate(outs):
        for part in range(PARTS):
            value = held[part, at].astype(FULL)
            for block in range(value.shape[1] // step):
                start = (block * PARTS + part) * step
                out[:, start : start + step] = value[:, block * step : (block + 1) * step]


def join_projections_kernel(meta, *refs):
    outs, sum_outs, held = refs[PARTS:-5], refs[-5:-1], refs[-1]
    rows, columns = outs[0].shape[0], refs[0].shape[1] // len(outs)
    for r in range(PARTS):
        held[meta[0, PART] ^ r] = refs[r][...]
    sums = jnp.zeros((8, rows), FULL)
    for part in range(PARTS):
        value = held[part].astype(FULL)
        for at, out in enumerate(outs):
            out[:, part * columns : (part + 1) * columns] = value[:rows, at * columns : (at + 1) * columns]
        sums = sums + value[rows : rows + 8, :rows]
    for at, out in enumerate(sum_outs):
        out[...] = sums[at]


def gather_pieces(own, bits, starts=None, gate=None):
    held = {0: own}
    for bit in bits:
        for distance in list(held):
            source = held[distance]
            if distance == 0 and starts is not None:
                source = after(source, *starts)
            elif distance != 0 and gate is not None:
                source = after(source, gate)
            held[distance | bit] = hop(source, "dp", bit)
    return [held[distance] for distance in range(len(held))]


def send_terms(chunks, gate=None):
    return [
        hop(chunk if gate is None else after(chunk, *gate), "dp", distance)
        for distance, chunk in enumerate(chunks)
        if distance
    ]


def sum_terms(chunks, got):
    total = chunks[0].astype(FULL)
    for one in got:
        total = total + one.astype(FULL)
    return total


def shards(
    tokens, lengths, w_query, w_key, w_value, w_output, w_gate, w_up, w_down,
    first_gain, first_bias, second_gain, second_bias, cotangent,
):
    _, _, local, width = tokens.shape
    dp_count, blk_count = lax.axis_size("dp"), lax.axis_size("blk")
    dp, blk = lax.axis_index("dp"), lax.axis_index("blk")
    side = blk_count // 2
    which = blk // side
    first = which == 0
    core, part = blk % 2, blk % PARTS
    heads = width // HEAD_DIM // PARTS
    columns = heads * HEAD_DIM
    rows, ff_rows = w_query.shape[0], w_down.shape[0]
    half, ff = rows // 2, w_gate.shape[1]
    block = 2 * local
    row_count = PARTS * block
    spread_bits = bits_between(PARTS, side)
    sum_bits = bits_between(PARTS, blk_count)
    dp_bits = bits_between(1, dp_count)
    back_bits = dp_bits[::-1]
    table = jnp.asarray(turn_table(local * blk_count))
    swap_q, swap_k, spread_v = (
        jnp.asarray(swap_matrix(heads, 3 * columns, at * columns, at < 2), LOW) for at in range(3)
    )
    spread = jnp.asarray(swap_matrix(heads, columns, 0, False), LOW)

    starts = [(blk ^ distance ^ away) * local for distance in range(side) for away in (0, side)]
    meta = jnp.stack([which, core, part, dp, *starts]).astype(jnp.int32).reshape(1, -1)

    gate_up_own = call(
        pack_second_kernel, [shape((2 * PARTS, half, width))], [SMEM] + [VMEM] * 2, [], meta, w_gate, w_up
    )[0]
    gate_up_core = lax.all_gather(gate_up_own, "dp", axis=0, tiled=False)
    tok_send, cot_send, qkv_own, down_own = call(
        pack_first_kernel,
        [shape((local, width)), shape((local, width)), shape((rows + EXTRA + half + half // 3, 3 * columns))]
        + [shape((PARTS, half, width))],
        [SMEM] + [VMEM] * 11, [], after(meta, gate_up_own), tokens, cotangent, w_query, w_key, w_value, w_output, w_down,
        first_gain, first_bias, second_gain, second_bias,
    )
    tok_got = hop(tok_send, "blk", side)
    qkv = gather_pieces(qkv_own, dp_bits)
    x_own = jnp.concatenate([jnp.where(first, tokens[0, 0], tokens[1, 0]), tok_got])
    x_core, x_near = hop(x_own, "blk", 1), hop(x_own, "blk", 2)
    x_far = hop(after(x_near, x_core, *(qkv[bit] for bit in dp_bits)), "blk", 1)
    x_all = [x_own, x_core, x_near, x_far]
    down_pieces = {0: down_own}
    for bit in dp_bits[:2]:
        down_pieces[bit] = hop(after(down_own, *qkv[1:]), "dp", bit)
    cot_got = hop(after(cot_send, x_near), "blk", side)

    wide_shape = shape((row_count, WIDE))
    made = call(
        functools.partial(project_kernel, heads, dp_count), [wide_shape] * (3 * heads),
        [SMEM] + [VMEM] * (4 + PARTS + dp_count),
        [pltpu.VMEM((width, 3 * columns), LOW), pltpu.VMEM((row_count, 2 * WIDE), FULL)],
        after(meta, cot_got), table, swap_q, swap_k, spread_v, *x_all, *qkv,
    )
    queries, keys, values = (made[at * heads : (at + 1) * heads] for at in range(3))
    out_rows = rows + EXTRA
    qkv_core = hop(after(jnp.stack([piece[out_rows:] for piece in qkv[1:]]), queries[0]), "blk", 1)
    for bit in spread_bits:
        keys, values = ([jnp.concatenate([one, hop(one, "blk", bit)]) for one in many] for many in (keys, values))
    key_count = keys[0].shape[0]
    q_block = max(WIDE, min(row_count, 512 * 1024 // key_count))
    attended = call(
        functools.partial(attend_kernel, heads, q_block),
        [shape((PARTS, block, columns))] + [shape((1, row_count), FULL)] * heads,
        [SMEM] * 2 + [VMEM] * (1 + 3 * heads),
        [pltpu.VMEM((row_count, heads * WIDE), LOW)],
        meta, lengths, *queries, *keys, *values, spread,
    )
    attended, lse = attended[0], attended[1:]
    att_send = after(attended, qkv_core, *(down_pieces[bit] for bit in dp_bits[:2]))
    att_core, att_near = hop(att_send, "blk", 1), hop(att_send, "blk", 2)
    att_all = [attended, att_core, att_near, hop(after(att_near, att_core), "blk", 1)]
    middle = PARTS // 2
    down_pieces[3] = jnp.concatenate(
        [hop(down_pieces[1][:middle], "dp", 2), hop(down_pieces[2][middle:], "dp", 1)]
    )
    for bit in dp_bits[2:]:
        for distance in range(bit):
            down_pieces[distance | bit] = hop(down_pieces[distance], "dp", bit)
    down_pieces = [down_pieces[distance] for distance in range(dp_count)]
    residual_one, normed_low, all_vectors, w_o = call(
        functools.partial(residual_kernel, dp_count),
        [shape((block, width), FULL), shape((block, width)), shape((8, width), FULL), shape((columns, width))],
        [SMEM] + [VMEM] * (2 + PARTS + dp_count + 1),
        [pltpu.VMEM((width, width), LOW), pltpu.VMEM((dp_count, EXTRA, 3 * columns), LOW)],
        after(meta, down_pieces[3]), x_own, w_output, *att_all, *qkv, qkv_core,
    )
    normed_core, normed_near = hop(normed_low, "blk", 1), hop(normed_low, "blk", 2)
    down_core = [hop(after(piece, normed_low), "blk", 1) for piece in down_pieces[1:]]
    down_all = (w_down, *down_pieces[1:], *down_core)
    gate_up_all = (gate_up_core, hop(after(gate_up_core, att_all[3], down_pieces[3]), "blk", 1))

    part_shape, w_shape = (PARTS, block, width), (dp_count, rows, width)
    down_copies = 2 * dp_count - 1
    grad_ffn, grad_branch, grad_one, layer_own, layer_back, sums = call(
        feed_kernel,
        [shape((block, width))] * 2 + [shape((block, width), FULL)] + [shape((local, width))] * 2
        + [shape((8, width), FULL)],
        [SMEM] * 2 + [VMEM] * 4 + [ANY] * (2 + len(down_all)),
        [
            pltpu.VMEM((3 * PARTS, *w_shape), LOW),
            pltpu.VMEM(part_shape, FULL),
            pltpu.VMEM(part_shape, FULL),
            pltpu.SemaphoreType.DMA((PARTS * (4 + down_copies),)),
        ],
        after(meta, normed_core), lengths, residual_one, all_vectors, cotangent, cot_got, *gate_up_all, *down_all,
    )
    ffn_core, ffn_near = hop(grad_ffn, "blk", 1), hop(grad_ffn, "blk", 2)
    normed_all = [normed_low, normed_core, normed_near, hop(after(normed_near, grad_ffn), "blk", 1)]

    long, chunk = shape((row_count, width)), shape((rows, width))
    hidden, gate_factor, up_factor = call(
        hidden_kernel, [long] * 3,
        [SMEM] + [VMEM] * PARTS + [ANY] * 2,
        [pltpu.VMEM(w_shape, LOW), pltpu.VMEM(w_shape, LOW), pltpu.SemaphoreType.DMA((4,))],
        after(meta, grad_ffn), *normed_all, *gate_up_all,
    )
    ffn_all = [grad_ffn, ffn_core, ffn_near, hop(after(ffn_near, hidden, ffn_core), "blk", 1)]
    branch_core, branch_near = (hop(after(grad_branch, ffn_near, hidden), "blk", bit) for bit in (1, 2))
    down_terms = call(
        down_kernel, [chunk] * dp_count, [SMEM] + [VMEM] * (1 + PARTS), [pltpu.VMEM((width, width), LOW)],
        after(meta, branch_core), hidden, *ffn_all,
    )
    down_got = send_terms(down_terms)
    gate_up_terms = call(
        gate_up_kernel, [chunk] * dp_count + [shape((width, width))],
        [SMEM] + [VMEM] * (2 + 2 * PARTS) + [ANY] * len(down_all),
        [pltpu.VMEM(w_shape, LOW), pltpu.VMEM((row_count, 2 * width), LOW)]
        + [pltpu.VMEM((width, width), LOW), pltpu.SemaphoreType.DMA((down_copies,))],
        after(meta, down_terms[0]), gate_factor, up_factor, *ffn_all, *normed_all, *down_all,
    )

    def sum_halves(total):
        for bit in sum_bits:
            low = total.astype(LOW)
            total = low.astype(FULL) + hop(low, "blk", bit).astype(FULL)
        return total.astype(LOW)

    branch_far = hop(after(branch_near, gate_up_terms[0], *(down_got[bit - 1] for bit in dp_bits)), "blk", 1)
    layer_got = hop(after(layer_back, branch_far), "blk", side)
    down_sum = sum_terms(down_terms, down_got)
    down_full = sum_halves(down_sum)
    gate_got = send_terms(gate_up_terms[:dp_count])
    up_sum = lax.psum_scatter(
        after(gate_up_terms[-1], branch_far).reshape(dp_count, rows, width), "dp", scatter_dimension=0, tiled=False
    )
    early = heads if spread_bits else heads - 1
    key_shape = shape((key_count, WIDE))
    back_scratch = [pltpu.VMEM((key_count, WIDE), FULL), pltpu.VMEM((key_count, 2 * WIDE), FULL)]
    back_scratch += [pltpu.VMEM((key_count, WIDE), FULL)] * 2
    *made, out_terms = call(
        functools.partial(attend_back_kernel, early, q_block),
        [wide_shape] * early + [key_shape] * (2 * early) + [wide_shape] * (heads - early) + [shape((width, columns))],
        [SMEM] * 2 + [VMEM] * (3 + 2 * PARTS + 4 * early),
        [pltpu.VMEM((PARTS, block, columns), LOW), *back_scratch] + [pltpu.VMEM((row_count, WIDE), LOW)] * early,
        after(meta, down_sum), lengths, w_o, spread, table,
        grad_branch, branch_core, branch_near, branch_far, *att_all,
        *queries[:early], *keys[:early], *values[:early], *lse[:early],
    )
    grad_q, grad_k, grad_v = (made[at * early : (at + 1) * early] for at in range(3))
    gate_sum = sum_terms(gate_up_terms, [after(got, grad_q[0], layer_got) for got in gate_got])
    gate_full = sum_halves(gate_sum)
    down_near = hop(down_full, "blk", 2)
    for bit in reversed(spread_bits):
        middle = grad_k[0].shape[0] // 2
        grad_k, grad_v = (
            [
                (one[:middle].astype(FULL) + hop(one[middle:], "blk", bit).astype(FULL)).astype(LOW)
                for one in many
            ]
            for many in (grad_k, grad_v)
        )
    back_outs = [shape((rows + EXTRA, width))] * dp_count + [shape((2, block, width), FULL), shape((2, block, width))]
    back_weights = [pltpu.VMEM((width, 3 * columns), LOW), pltpu.VMEM((width, width), LOW)]
    back_operands = (spread, sums, out_terms, *grad_q, *grad_k, *grad_v, *x_all, *qkv)
    ready = after(meta, gate_sum, down_full)
    if spread_bits:
        made = call(
            functools.partial(projections_back_kernel, heads, dp_count), back_outs,
            [SMEM] + [VMEM] * len(back_operands), back_weights, ready, *back_operands,
        )
    else:
        made = call(
            functools.partial(last_back_kernel, heads, dp_count, q_block), back_outs,
            [SMEM] * 2 + [VMEM] * (6 + len(back_operands)),
            back_weights + [pltpu.VMEM((row_count, WIDE), LOW)] * 3 + back_scratch,
            ready, lengths, table, queries[-1], keys[-1], values[-1], lse[-1], made[-1], *back_operands,
        )
    *qkv_terms, token_keep, token_send = made
    up_sum = after(up_sum, token_keep).astype(FULL)

    first_gate = (gate_full, up_sum, down_near)
    token_got = hop(after(token_send, *first_gate), "blk", 1).astype(FULL)
    up_full = sum_halves(up_sum)
    near_send = (token_keep[1] + token_got[1]).astype(LOW)
    token_near = hop(near_send, "blk", 2)
    qkv_got = send_terms(qkv_terms)
    qkv_sum = sum_terms(qkv_terms, [after(got, token_near) for got in qkv_got]).astype(LOW)
    qkv_full = sum_halves(after(qkv_sum, up_full, token_near))
    pair_full = after(jnp.stack([gate_full, up_full]), qkv_sum)
    pair_core, pair_near = hop(pair_full, "blk", 1), hop(pair_full, "blk", 2)
    down_core, down_far = (hop(after(one, pair_core), "blk", 1) for one in (down_full, down_near))
    grad_rows = after(grad_one, qkv_sum) + token_keep[0] + token_got[0] + token_near.astype(FULL)
    rows_got = hop(grad_rows[local:].astype(LOW), "blk", side).astype(FULL)
    grad_down = call(
        join_rows_kernel, [shape((ff_rows, width), FULL)], [SMEM] + [VMEM] * PARTS, [],
        meta, down_full, down_core, down_near, down_far,
    )[0]
    pair_far = hop(after(pair_near, pair_core, grad_down), "blk", 1)
    qkv_core, qkv_near = (hop(after(qkv_full, pair_near), "blk", bit) for bit in (1, 2))
    grad_gate, grad_up = call(
        join_columns_kernel, [shape((rows, ff), FULL)] * 2, [SMEM] + [VMEM] * PARTS,
        [pltpu.VMEM((PARTS, 2, rows, width), LOW)], meta, pair_full, pair_core, pair_near, pair_far,
    )
    qkv_far = hop(after(qkv_near, qkv_core, grad_gate, rows_got), "blk", 1)
    grad_tokens = jnp.where(
        first, jnp.stack([grad_rows[:local], rows_got]), jnp.stack([rows_got, grad_rows[:local]])
    )[:, None]
    layer_out = jnp.where(first, jnp.stack([layer_own, layer_got]), jnp.stack([layer_got, layer_own]))[:, None]
    grad_query, grad_key, grad_value, grad_output, *vector_sums = call(
        join_projections_kernel, [shape((rows, width), FULL)] * 4 + [shape((rows,), FULL)] * 4,
        [SMEM] + [VMEM] * PARTS, [pltpu.VMEM((PARTS, rows + EXTRA, width), LOW)], meta, qkv_full, qkv_core, qkv_near, qkv_far,
    )
    return (
        layer_out, grad_tokens, grad_query, grad_key, grad_value, grad_output, grad_gate, grad_up, grad_down,
        vector_sums[0], vector_sums[1], vector_sums[2], vector_sums[3],
    )


def solution(mesh):
    slots = P(None, "dp", "blk", None)
    matrix, vector = P("dp", None), P("dp")
    return jax.shard_map(
        shards,
        mesh=mesh,
        in_specs=(slots, P(None, "dp")) + (matrix,) * 7 + (vector,) * 4 + (slots,),
        out_specs=(slots, slots) + (matrix,) * 7 + (vector,) * 4,
        check_vma=False,
    )
```

```python
import functools

import jax
import jax.numpy as jnp
import numpy as np
from jax import lax
from jax.experimental import pallas as pl
from jax.experimental.pallas import tpu as pltpu
from jax.sharding import PartitionSpec as P

HEAD_DIM = 64
WIDE = 128
PARTS = 4
EXTRA = 16
LOW, FULL = jnp.bfloat16, jnp.float32
VMEM_MIB = {"join_rows_kernel": 30, "join_columns_kernel": 30, "join_projections_kernel": 30, "hidden_kernel": 40, "down_kernel": 40, "gate_up_kernel": 40}
VMEM = pl.BlockSpec(memory_space=pltpu.VMEM)
SMEM = pl.BlockSpec(memory_space=pltpu.SMEM)
ANY = pl.BlockSpec(memory_space=pl.ANY)
WHICH, CORE, PART, DP, STARTS = 0, 1, 2, 3, 4


def mm(left, right):
    return jnp.dot(left, right, preferred_element_type=FULL)


def mm_nt(left, right):
    return lax.dot_general(left, right, (((1,), (1,)), ((), ())), preferred_element_type=FULL)


def mm_tn(left, right):
    return lax.dot_general(left, right, (((0,), (0,)), ((), ())), preferred_element_type=FULL)


def hop(value, axis, bit):
    size = lax.axis_size(axis)
    return lax.ppermute(value, axis, [(at, at ^ bit) for at in range(size)])


def after(value, *others):
    return lax.optimization_barrier((value, *others))[0]


def bits_between(low, high):
    bits = []
    while low < high:
        bits.append(low)
        low *= 2
    return bits


def turn_table(seq_len):
    half = HEAD_DIM // 2
    frequency = np.float32(1000.0) ** (
        -(np.arange(half, dtype=np.float32) * np.float32(2.0) / np.float32(HEAD_DIM))
    )
    angles = np.arange(seq_len, dtype=np.float32)[:, None] * frequency[None, :]
    cosine = np.cos(angles).astype(np.float32)
    sine = np.sin(angles).astype(np.float32)
    return np.concatenate([cosine] * 4 + [sine, sine, -sine, -sine], axis=1)


def swap_matrix(heads, total, first, swapped):
    half = HEAD_DIM // 2
    out = np.zeros((total, heads * WIDE), np.float32)
    for h in range(heads):
        for f in range(HEAD_DIM):
            out[first + h * HEAD_DIM + f, h * WIDE + f] = 1.0
        for f in range(half if swapped else 0):
            out[first + h * HEAD_DIM + half + f, h * WIDE + HEAD_DIM + f] = -1.0
            out[first + h * HEAD_DIM + f, h * WIDE + HEAD_DIM + half + f] = 1.0
    return out


def call(body, outs, in_specs, scratch, *operands, late=()):
    if late:
        inner, given, made, own = body, len(operands), len(outs), len(scratch)
        held = [pltpu.VMEM(operands[at].shape, operands[at].dtype) for at in late]
        in_specs = [ANY if at in late else spec for at, spec in enumerate(in_specs)]
        scratch = [*scratch, *held, pltpu.SemaphoreType.DMA((len(late),))]

        def body(*refs):
            refs, sems = list(refs[:-1]), refs[-1]
            places = refs[given + made + own :]
            copies = [pltpu.make_async_copy(refs[at], place, sems.at[n]) for n, (at, place) in enumerate(zip(late, places))]
            for copy in copies:
                copy.start()
            for at, place in zip(late, places):
                refs[at] = place
            inner(lambda: wait_all(copies), *refs[: given + made + own])

        body.__name__ = getattr(inner, "func", inner).__name__
    name = getattr(body, "func", body).__name__
    return pl.pallas_call(
        body,
        out_shape=outs,
        in_specs=in_specs,
        out_specs=[VMEM] * len(outs),
        scratch_shapes=scratch,
        name=getattr(body, "func", body).__name__,
        compiler_params=pltpu.CompilerParams(vmem_limit_bytes=VMEM_MIB.get(name, 60) * 1024 * 1024),
        cost_estimate=pl.CostEstimate(flops=1000, bytes_accessed=1000, transcendentals=0),
    )(*operands)


def shape(dims, dtype=LOW):
    return jax.ShapeDtypeStruct(dims, dtype)


def norm_parts(rows):
    centred = rows - jnp.mean(rows, axis=-1, keepdims=True)
    scale = lax.rsqrt(jnp.mean(centred * centred, axis=-1, keepdims=True) + 1e-05)
    return centred * scale, scale


def norm_back(upstream, gain, unit, scale):
    inner = upstream * gain
    centre = jnp.mean(inner, axis=-1, keepdims=True)
    along = jnp.mean(inner * unit, axis=-1, keepdims=True)
    sums = (jnp.sum(upstream * unit, axis=0, keepdims=True), jnp.sum(upstream, axis=0, keepdims=True))
    return (inner - centre - unit * along) * scale, sums


def pack_first_kernel(
    meta, tokens, cot, w_q, w_k, w_v, w_o, w_down, gain_one, bias_one, gain_two, bias_two, tok_out, cot_out, qkv_out, down_out
):
    rows, columns = w_q.shape[0], qkv_out.shape[1] // 3
    half, third = rows // 2, rows // 6
    other = 1 - meta[0, WHICH]
    tok_out[...] = tokens[other, 0]
    cot_out[...] = cot[other, 0]
    for part in range(PARTS):

        @pl.when(meta[0, PART] == part)
        def _(part=part):
            for at, w in enumerate((w_q, w_k, w_v)):
                qkv_out[:rows, at * columns : (at + 1) * columns] = w[:, part * columns : (part + 1) * columns]

    qkv_out[rows : rows + EXTRA, :] = jnp.zeros((EXTRA, 3 * columns), LOW)
    vectors = [vector[...].reshape(1, rows).astype(FULL) for vector in (gain_one, bias_one, gain_two, bias_two)]
    vectors = jnp.concatenate([*vectors, jnp.zeros((EXTRA - 4, rows), FULL)], axis=0)
    qkv_out[rows : rows + EXTRA, :rows] = vectors.astype(LOW)
    for part in range(PARTS):
        low = pl.multiple_of(part * rows + meta[0, CORE] * half, half)
        down_out[part] = w_down[pl.ds(low, half), :]
    out_rows = w_o[pl.ds(pl.multiple_of(meta[0, CORE] * half, half), half), :]
    at = rows + EXTRA
    qkv_out[at : at + half, :] = out_rows[:, : 3 * columns]
    at += half
    for g in range(3):
        qkv_out[at : at + third, g * columns : (g + 1) * columns] = out_rows[g * third : (g + 1) * third, 3 * columns :]


def pack_second_kernel(meta, w_gate, w_up, out):
    half, width = out.shape[1], out.shape[2]
    step = 2 * half
    low = pl.multiple_of(meta[0, CORE] * half, half)
    for base, w in ((0, w_gate), (PARTS, w_up)):
        for part in range(PARTS):
            for block in range(width // step):
                start = (block * PARTS + part) * step
                out[base + part, :, block * step : (block + 1) * step] = w[pl.ds(low, half), start : start + step]


def project_kernel(heads, pieces, meta, table_ref, swap_q, swap_k, spread_v, *refs):
    x_refs, w_refs, (q_refs, k_refs, v_refs) = refs[:PARTS], refs[PARTS : PARTS + pieces], [refs[-2 - 3 * heads + at * heads : -2 - 2 * heads + at * heads] for at in range(3)]
    w_all, turn = refs[-2:]
    rows = w_all.shape[0] // pieces
    block = x_refs[0].shape[0]
    local = block // 2
    for distance, w in enumerate(w_refs):
        w_all[pl.ds(pl.multiple_of((meta[0, DP] ^ distance) * rows, rows), rows), :] = w[:rows, :]
    for at in range(2 * PARTS):
        start = pl.multiple_of(meta[0, STARTS + at], local)
        turn[at * local : (at + 1) * local, :] = table_ref[pl.ds(start, local), :]
    weights = w_all[...]
    w_q, w_k, w_v = (mm(weights, m[...]).astype(LOW) for m in (swap_q, swap_k, spread_v))
    for r in range(PARTS):
        out_rows = slice(r * block, (r + 1) * block)
        x = x_refs[r][...]
        cosine, sine = turn[out_rows, :WIDE], turn[out_rows, WIDE:]
        for out_refs, w, scale in ((q_refs, w_q, 0.0625), (k_refs, w_k, None)):
            made = mm(x, w)
            for h in range(heads):
                one = made[:, h * WIDE : (h + 1) * WIDE]
                turned = (one * cosine + pltpu.roll(one, HEAD_DIM, 1) * sine).astype(LOW)
                out_refs[h][out_rows, :] = turned if scale is None else turned * jnp.asarray(scale, LOW)
        made = mm(x, w_v).astype(LOW)
        for h in range(heads):
            v_refs[h][out_rows, :] = made[:, h * WIDE : (h + 1) * WIDE]


def fill_bias(meta, length, bias_ref, local):
    for at in range(bias_ref.shape[0] // local):
        place = meta[0, STARTS + at] + lax.broadcasted_iota(jnp.int32, (local, WIDE), 0)
        bias_ref[at * local : (at + 1) * local, :] = jnp.where(place < length, 0.0, -1e30)


def each_block(count, step):
    if count <= 4:
        for number in range(count):
            step(number)
    else:
        lax.fori_loop(0, count, lambda number, carry: step(number) or carry, 0)


def block_rows(number, block):
    if isinstance(number, int):
        return slice(number * block, (number + 1) * block)
    return pl.ds(pl.multiple_of(number * block, block), block)


def attend_kernel(heads, block, meta, lengths, *refs):
    q_refs, k_refs, v_refs, spread_ref = refs[:heads], refs[heads : 2 * heads], refs[2 * heads : 3 * heads], refs[3 * heads]
    out, lse_refs, wide_ref = refs[3 * heads + 1], refs[-1 - heads : -1], refs[-1]
    row_count, key_count = q_refs[0].shape[0], k_refs[0].shape[0]
    span = row_count // PARTS
    local = span // 2
    length = lengths[meta[0, WHICH], 0]
    places = [meta[0, STARTS + at] + lax.broadcasted_iota(jnp.int32, (1, local), 1) for at in range(key_count // local)]
    bias = jnp.where(jnp.concatenate(places, axis=1) < length, 0.0, -1e30)
    for h in range(heads):

        def step(number, h=h):
            rows = block_rows(number, block)
            scores = mm_nt(q_refs[h][rows, :], k_refs[h][...]) + bias
            top = jnp.max(scores, axis=1, keepdims=True)
            weights = jnp.exp(scores - top)
            total = jnp.sum(weights, axis=1, keepdims=True)
            wide_ref[rows, h * WIDE : (h + 1) * WIDE] = (mm(weights.astype(LOW), v_refs[h][...]) / total).astype(LOW)
            lse_refs[h][:, rows] = jnp.broadcast_to(top + jnp.log(total), (block, WIDE)).T[:1, :]

        each_block(row_count // block, step)
    for r in range(PARTS):
        out[r] = mm_nt(wide_ref[r * span : (r + 1) * span, :], spread_ref[...]).astype(LOW)


class Turn:
    def __init__(self, meta, lengths, table_ref, bias_ref, turn, local):
        fill_bias(meta, lengths[meta[0, WHICH], 0], bias_ref, local)
        for at in range(turn.shape[0] // local):
            start = pl.multiple_of(meta[0, STARTS + at], local)
            turn[at * local : (at + 1) * local, :] = table_ref[pl.ds(start, local), :]
        self.turn = turn

    def back(self, value, rows):
        cosine, sine = self.turn[rows, :WIDE], self.turn[rows, WIDE:]
        return (value * cosine - pltpu.roll(value, HEAD_DIM, 1) * sine).astype(LOW)


def back_head(block, turn, bias_ref, sums, q_ref, k_ref, v_ref, lse_ref, grad_ref, dq_ref, dk_ref, dv_ref):
    dk_sum, dv_sum = sums
    keys, values = k_ref[...], v_ref[...]
    keys_t = keys.T
    dk_sum[...] = jnp.zeros_like(dk_sum)
    dv_sum[...] = jnp.zeros_like(dv_sum)

    def step(number):
        rows = block_rows(number, block)
        bias = jnp.concatenate([bias_ref[...]] * (block // WIDE), axis=1)
        queries, grads = q_ref[rows, :], grad_ref[rows, :]
        probs = jnp.exp(mm_nt(keys, queries) + bias - lse_ref[:, rows])
        grad_probs = mm_nt(values, grads)
        delta = jnp.sum(probs * grad_probs, axis=0, keepdims=True)
        grad_scores = (probs * (grad_probs - delta)).astype(LOW)
        dv_sum[...] += mm(probs.astype(LOW), grads)
        dk_sum[...] += mm(grad_scores, queries)
        dq_ref[rows, :] = turn.back(mm(keys_t, grad_scores).T * 0.125, rows)

    each_block(q_ref.shape[0] // block, step)
    dk_ref[...] = turn.back(dk_sum[...] * 2.0, slice(None))
    dv_ref[...] = dv_sum[...].astype(LOW)


def attend_back_kernel(heads, block, wait, meta, lengths, w_o, spread_ref, table_ref, *refs):
    grads_in, att_in, refs = refs[:PARTS], refs[PARTS : 2 * PARTS], refs[2 * PARTS :]
    ins, refs = [refs[at * heads : (at + 1) * heads] for at in range(4)], refs[4 * heads :]
    outs, refs = [refs[at * heads : (at + 1) * heads] for at in range(3)], refs[3 * heads :]
    *later, dw_ref, grad_part, bias_ref, turn_ref, dk_sum, dv_sum = refs[: -heads]
    wide = [*refs[-heads:], *later]
    columns = w_o.shape[0]
    weights = mm_tn(spread_ref[...], w_o[...]).astype(LOW)
    span = grads_in[0].shape[0]
    for r in range(PARTS):
        made = mm_nt(grads_in[r][...], weights).astype(LOW)
        for h, out in enumerate(wide):
            out[r * span : (r + 1) * span, :] = made[:, h * WIDE : (h + 1) * WIDE]
        for part in range(PARTS):

            @pl.when(meta[0, PART] == part)
            def _(r=r, part=part):
                grad_part[r] = grads_in[r][:, part * columns : (part + 1) * columns]

    wait()
    for distance in range(PARTS):
        total = mm_tn(att_in[distance][distance], grad_part[0])
        for r in range(1, PARTS):
            total = total + mm_tn(att_in[distance][r ^ distance], grad_part[r])
        low = pl.multiple_of((meta[0, PART] ^ distance) * columns, columns)
        dw_ref[pl.ds(low, columns), :] = total.astype(LOW)
    turn = Turn(meta, lengths, table_ref, bias_ref, turn_ref, span // 2)
    for h in range(heads):
        q_ref, k_ref, v_ref, lse_ref = (some[h] for some in ins)
        back_head(block, turn, bias_ref, (dk_sum, dv_sum), q_ref, k_ref, v_ref, lse_ref, wide[h], *(o[h] for o in outs))


def place_gate_up(meta, refs, block, target, sems, at):
    half = refs[0].shape[2]
    copies = []
    for side, ref in enumerate(refs):
        low = pl.multiple_of((meta[0, CORE] ^ side) * half, half)
        copy = pltpu.make_async_copy(ref.at[:, block], target.at[:, pl.ds(low, half), :], sems.at[at + side])
        copy.start()
        copies.append(copy)
    return copies, at + 2


def place_down(meta, own, refs, block, target, sems, at):
    count, rows = target.shape[0], target.shape[1]
    half = rows // 2
    low = pl.multiple_of(block * rows, rows)
    copies = [pltpu.make_async_copy(own.at[pl.ds(low, rows), :], target.at[meta[0, DP]], sems.at[at])]
    for number, ref in enumerate(refs):
        distance, side = number % (count - 1) + 1, number // (count - 1)
        low = pl.multiple_of((meta[0, CORE] ^ side) * half, half)
        to = target.at[meta[0, DP] ^ distance, pl.ds(low, half), :]
        copies.append(pltpu.make_async_copy(ref.at[block], to, sems.at[at + 1 + number]))
    for copy in copies:
        copy.start()
    return copies, at + len(copies)


def wait_all(copies):
    for copy in copies:
        copy.wait()


def residual_kernel(pieces, meta, x_ref, w_own, *refs):
    att, w_refs, w_core, refs = refs[:PARTS], refs[PARTS : PARTS + pieces], refs[PARTS + pieces], refs[PARTS + pieces + 1 :]
    residual_out, low_out, vector_out, w_out, w_o, gathered = refs
    columns, rows = att[0].shape[2], w_own.shape[0]
    half, third = rows // 2, rows // 6
    w_o[pl.ds(pl.multiple_of(meta[0, DP] * rows, rows), rows), :] = w_own[...]

    def fill(ref, low):
        w_o[pl.ds(pl.multiple_of(low, half), half), : 3 * columns] = ref[:half, :]
        for g in range(3):
            to = pl.ds(pl.multiple_of(low + g * third, third), third)
            w_o[to, 3 * columns :] = ref[half:, g * columns : (g + 1) * columns]

    for distance, ref in enumerate(w_refs):
        gathered[meta[0, DP] ^ distance] = ref[rows : rows + EXTRA, :]
        if distance:
            low = (meta[0, DP] ^ distance) * rows
            fill(ref[rows + EXTRA :, :], low + meta[0, CORE] * half)
            fill(w_core[distance - 1], low + (1 - meta[0, CORE]) * half)
    vectors = jnp.concatenate([gathered[d][:, :rows] for d in range(pieces)], axis=1).astype(FULL)[:8]
    vector_out[...] = vectors
    residual = x_ref[...].astype(FULL)
    for r in range(PARTS):
        low = pl.multiple_of((meta[0, PART] ^ r) * columns, columns)
        residual = residual + mm(att[r][r], w_o[pl.ds(low, columns), :])
    w_out[...] = w_o[pl.ds(pl.multiple_of(meta[0, PART] * columns, columns), columns), :]
    residual_out[...] = residual
    unit, _ = norm_parts(residual)
    low_out[...] = (unit * vectors[0:1] + vectors[1:2]).astype(LOW)


def feed_kernel(meta, lengths, residual_ref, vectors, cot_ref, cot_got, *refs):
    gu_refs, down_own, down_refs, refs = refs[:2], refs[2], refs[3:-10], refs[-10:]
    grad_ffn_out, grad_branch_out, grad_one_out, own_out, back_out, sums_out, held, gates, ups, sems = refs
    width = residual_ref.shape[1]
    copies, at = [], 0
    for part in range(PARTS):
        gate, at = place_gate_up(meta, gu_refs, part, held.at[part], sems, at)
        up, at = place_gate_up(meta, gu_refs, PARTS + part, held.at[PARTS + part], sems, at)
        down, at = place_down(meta, down_own, down_refs, part, held.at[2 * PARTS + part], sems, at)
        copies.append(gate + up + down)

    def weights(number):
        return held[number].reshape(width, width)

    which = meta[0, WHICH]
    local = cot_got.shape[0]
    unit_one, scale_one = norm_parts(residual_ref[...])
    normed = unit_one * vectors[0:1] + vectors[1:2]
    normed_low = normed.astype(LOW)
    residual = normed

    def pre(part):
        wait_all(copies[part])
        return mm(normed_low, weights(part)), mm(normed_low, weights(PARTS + part))

    ahead = pre(0)
    for part in range(PARTS):
        gate, up = ahead
        if part + 1 < PARTS:
            ahead = pre(part + 1)
        sigma = 0.5 * jnp.tanh(0.5 * gate) + 0.5
        silu = gate * sigma
        residual = residual + mm((silu * up).astype(LOW), weights(2 * PARTS + part))
        gates[part] = up * (sigma + silu * (1.0 - sigma))
        ups[part] = silu
    unit_two, scale_two = norm_parts(residual)
    layer = unit_two * vectors[2:3] + vectors[3:4]
    length = lengths[which, 0]
    upstream = []
    for half, (out, cot) in enumerate(((own_out, cot_ref[which, 0]), (back_out, cot_got[...]))):
        place = meta[0, STARTS + half] + lax.broadcasted_iota(jnp.int32, (local, 1), 0)
        valid = place < length
        out[...] = jnp.where(valid, layer[half * local : (half + 1) * local], 0.0).astype(LOW)
        upstream.append(jnp.where(valid, cot.astype(FULL), 0.0))
    grad_two, sums_two = norm_back(jnp.concatenate(upstream, axis=0), vectors[2:3], unit_two, scale_two)
    grad_ffn = grad_two.astype(LOW)
    grad_ffn_out[...] = grad_ffn
    grad_normed = grad_two
    for part in range(PARTS):
        grad_hidden = mm_nt(grad_ffn, weights(2 * PARTS + part))
        grad_normed = (
            grad_normed
            + mm_nt((grad_hidden * gates[part]).astype(LOW), weights(part))
            + mm_nt((grad_hidden * ups[part]).astype(LOW), weights(PARTS + part))
        )
    grad_one, sums_one = norm_back(grad_normed, vectors[0:1], unit_one, scale_one)
    grad_one_out[...] = grad_one
    grad_branch_out[...] = grad_one.astype(LOW)
    sums_out[...] = jnp.concatenate([*sums_one, *sums_two, jnp.zeros((4, width), FULL)], axis=0)


def hidden_kernel(meta, *refs):
    x_refs, gu_refs, refs = refs[:PARTS], refs[PARTS : PARTS + 2], refs[PARTS + 2 :]
    hidden_out, gate_out, up_out, held_gate, held_up, sems = refs
    part, width = meta[0, PART], hidden_out.shape[1]
    first, at = place_gate_up(meta, gu_refs, part, held_gate, sems, 0)
    second, at = place_gate_up(meta, gu_refs, PARTS + part, held_up, sems, at)
    wait_all(first + second)
    w_gate, w_up = held_gate[...].reshape(width, width), held_up[...].reshape(width, width)
    block = x_refs[0].shape[0]
    for r in range(PARTS):
        rows = slice(r * block, (r + 1) * block)
        x = x_refs[r][...]
        gate, up = mm(x, w_gate), mm(x, w_up)
        sigma = 0.5 * jnp.tanh(0.5 * gate) + 0.5
        silu = gate * sigma
        hidden_out[rows, :] = (silu * up).astype(LOW)
        gate_out[rows, :] = (up * (sigma + silu * (1.0 - sigma))).astype(LOW)
        up_out[rows, :] = silu.astype(LOW)


def split_terms(meta, terms, outs):
    rows = terms.shape[0] // len(outs)
    for distance, out in enumerate(outs):
        low = pl.multiple_of((meta[0, DP] ^ distance) * rows, rows)
        out[:rows, :] = terms[pl.ds(low, rows), :]


def down_kernel(meta, hidden_ref, *refs):
    grads, outs, terms = refs[:PARTS], refs[PARTS:-1], refs[-1]
    block = grads[0].shape[0]
    total = mm_tn(hidden_ref[:block, :], grads[0][...])
    for r in range(1, PARTS):
        total = total + mm_tn(hidden_ref[r * block : (r + 1) * block, :], grads[r][...])
    terms[...] = total.astype(LOW)
    split_terms(meta, terms, outs)


def gate_up_kernel(meta, gate_ref, up_ref, *refs):
    grads, x_refs, down_own, refs = refs[:PARTS], refs[PARTS : 2 * PARTS], refs[2 * PARTS], refs[2 * PARTS + 1 :]
    held, low, terms, sems = refs[-4:]
    count = held.shape[0]
    down_refs, outs = refs[: 2 * count - 2], refs[2 * count - 2 : -4]
    width = terms.shape[0]
    copies, _ = place_down(meta, down_own, down_refs, meta[0, PART], held, sems, 0)
    wait_all(copies)
    w_down = held[...].reshape(terms.shape)
    block = grads[0].shape[0]
    for r in range(PARTS):
        rows = slice(r * block, (r + 1) * block)
        grad_hidden = mm_nt(grads[r][...], w_down)
        low[rows, :width] = (grad_hidden * gate_ref[rows, :].astype(FULL)).astype(LOW)
        low[rows, width:] = (grad_hidden * up_ref[rows, :].astype(FULL)).astype(LOW)
    total = mm_tn(x_refs[0][...], low[:block, :])
    for r in range(1, PARTS):
        total = total + mm_tn(x_refs[r][...], low[r * block : (r + 1) * block, :])
    terms[...] = total[:, :width].astype(LOW)
    split_terms(meta, terms, outs[:-1])
    outs[-1][...] = total[:, width:].astype(LOW)


def last_back_kernel(heads, pieces, block, meta, lengths, table_ref, q_ref, k_ref, v_ref, lse_ref, grad_ref, *refs):
    *refs, dq, dk, dv, bias_ref, turn_ref, dk_sum, dv_sum = refs
    turn = Turn(meta, lengths, table_ref, bias_ref, turn_ref, q_ref.shape[0] // PARTS // 2)
    back_head(block, turn, bias_ref, (dk_sum, dv_sum), q_ref, k_ref, v_ref, lse_ref, grad_ref, dq, dk, dv)
    count = heads - 1
    first = [refs[3 + at * count : 3 + (at + 1) * count] for at in range(3)]
    grads = [ref for some, last in zip(first, (dq, dk, dv)) for ref in (*some, last)]
    projections_back_kernel(heads, pieces, meta, *refs[:3], *grads, *refs[3 + 3 * count :])


def projections_back_kernel(heads, pieces, meta, spread, sums, out_terms, *refs):
    grads, refs = [refs[at * heads : (at + 1) * heads] for at in range(3)], refs[3 * heads :]
    x_refs, w_refs, refs = refs[:PARTS], refs[PARTS : PARTS + pieces], refs[PARTS + pieces :]
    outs, (near_out, far_out, w_all, terms) = refs[:pieces], refs[pieces:]
    rows = w_all.shape[0] // pieces
    for distance, w in enumerate(w_refs):
        w_all[pl.ds(pl.multiple_of((meta[0, DP] ^ distance) * rows, rows), rows), :] = w[:rows, :]
    block = x_refs[0].shape[0]
    columns = w_all.shape[1] // 3
    totals = [None] * 3
    for r in range(PARTS):
        span = slice(r * block, (r + 1) * block)
        x, onward = x_refs[r][...], 0.0
        for at, of_heads in enumerate(grads):
            wide = jnp.concatenate([ref[span, :] for ref in of_heads], axis=1)
            low = mm_nt(wide, spread[...]).astype(LOW)
            term = mm_tn(x, low)
            totals[at] = term if r == 0 else totals[at] + term
            onward = onward + mm_nt(low, w_all[:, at * columns : (at + 1) * columns])
        if r % 2 == 0:
            near_out[r // 2] = onward
        else:
            far_out[r // 2] = onward.astype(LOW)
    for at, total in enumerate(totals):
        terms[:, at * columns : (at + 1) * columns] = total.astype(LOW)
    terms[:, 3 * columns :] = out_terms[...]
    split_terms(meta, terms, outs)
    for distance, out in enumerate(outs):
        out[rows:, :] = jnp.zeros((EXTRA, terms.shape[1]), LOW)
        for block_at in range(pieces):

            @pl.when(meta[0, DP] ^ distance == block_at)
            def _(out=out, block_at=block_at):
                some = sums[:, block_at * rows : (block_at + 1) * rows]
                some = jnp.concatenate([some, jnp.zeros((EXTRA - some.shape[0], rows), FULL)], axis=0)
                out[rows : rows + EXTRA, :rows] = some.astype(LOW)


def join_rows_kernel(meta, *refs):
    out = refs[-1]
    rows = refs[0].shape[0]
    for r in range(PARTS):
        low = pl.multiple_of((meta[0, PART] ^ r) * rows, rows)
        out[pl.ds(low, rows), :] = refs[r][...].astype(FULL)


def join_columns_kernel(meta, *refs):
    outs, held = refs[PARTS:-1], refs[-1]
    step = outs[0].shape[0]
    for r in range(PARTS):
        held[meta[0, PART] ^ r] = refs[r][...]
    for at, out in enumerate(outs):
        for part in range(PARTS):
            value = held[part, at].astype(FULL)
            for block in range(value.shape[1] // step):
                start = (block * PARTS + part) * step
                out[:, start : start + step] = value[:, block * step : (block + 1) * step]


def join_projections_kernel(meta, *refs):
    outs, sum_outs, held = refs[PARTS:-5], refs[-5:-1], refs[-1]
    rows, columns = outs[0].shape[0], refs[0].shape[1] // len(outs)
    for r in range(PARTS):
        held[meta[0, PART] ^ r] = refs[r][...]
    sums = jnp.zeros((8, rows), FULL)
    for part in range(PARTS):
        value = held[part].astype(FULL)
        for at, out in enumerate(outs):
            out[:, part * columns : (part + 1) * columns] = value[:rows, at * columns : (at + 1) * columns]
        sums = sums + value[rows : rows + 8, :rows]
    for at, out in enumerate(sum_outs):
        out[...] = sums[at]


def gather_pieces(own, bits, starts=None, gate=None):
    held = {0: own}
    for bit in bits:
        for distance in list(held):
            source = held[distance]
            if distance == 0 and starts is not None:
                source = after(source, *starts)
            elif distance != 0 and gate is not None:
                source = after(source, gate)
            held[distance | bit] = hop(source, "dp", bit)
    return [held[distance] for distance in range(len(held))]


def send_terms(chunks, gate=None):
    return [
        hop(chunk if gate is None else after(chunk, *gate), "dp", distance)
        for distance, chunk in enumerate(chunks)
        if distance
    ]


def sum_terms(chunks, got):
    total = chunks[0].astype(FULL)
    for one in got:
        total = total + one.astype(FULL)
    return total


def shards(
    tokens, lengths, w_query, w_key, w_value, w_output, w_gate, w_up, w_down,
    first_gain, first_bias, second_gain, second_bias, cotangent,
):
    _, _, local, width = tokens.shape
    dp_count, blk_count = lax.axis_size("dp"), lax.axis_size("blk")
    dp, blk = lax.axis_index("dp"), lax.axis_index("blk")
    side = blk_count // 2
    which = blk // side
    first = which == 0
    core, part = blk % 2, blk % PARTS
    heads = width // HEAD_DIM // PARTS
    columns = heads * HEAD_DIM
    rows, ff_rows = w_query.shape[0], w_down.shape[0]
    half, ff = rows // 2, w_gate.shape[1]
    block = 2 * local
    row_count = PARTS * block
    spread_bits = bits_between(PARTS, side)
    sum_bits = bits_between(PARTS, blk_count)
    dp_bits = bits_between(1, dp_count)
    back_bits = dp_bits[::-1]
    table = jnp.asarray(turn_table(local * blk_count))
    swap_q, swap_k, spread_v = (
        jnp.asarray(swap_matrix(heads, 3 * columns, at * columns, at < 2), LOW) for at in range(3)
    )
    spread = jnp.asarray(swap_matrix(heads, columns, 0, False), LOW)

    starts = [(blk ^ distance ^ away) * local for distance in range(side) for away in (0, side)]
    meta = jnp.stack([which, core, part, dp, *starts]).astype(jnp.int32).reshape(1, -1)

    gate_up_own = call(
        pack_second_kernel, [shape((2 * PARTS, half, width))], [SMEM] + [VMEM] * 2, [], meta, w_gate, w_up
    )[0]
    gate_up_core = lax.all_gather(gate_up_own, "dp", axis=0, tiled=False)
    tok_send, cot_send, qkv_own, down_own = call(
        pack_first_kernel,
        [shape((local, width)), shape((local, width)), shape((rows + EXTRA + half + half // 3, 3 * columns))]
        + [shape((PARTS, half, width))],
        [SMEM] + [VMEM] * 11, [], after(meta, gate_up_own), tokens, cotangent, w_query, w_key, w_value, w_output, w_down,
        first_gain, first_bias, second_gain, second_bias,
    )
    tok_got = hop(tok_send, "blk", side)
    qkv = gather_pieces(qkv_own, dp_bits)
    x_own = jnp.concatenate([jnp.where(first, tokens[0, 0], tokens[1, 0]), tok_got])
    x_core, x_near = hop(x_own, "blk", 1), hop(x_own, "blk", 2)
    x_far = hop(after(x_near, x_core, *(qkv[bit] for bit in dp_bits)), "blk", 1)
    x_all = [x_own, x_core, x_near, x_far]
    down_pieces = {0: down_own}
    for bit in dp_bits[:2]:
        down_pieces[bit] = hop(after(down_own, *qkv[1:]), "dp", bit)
    cot_got = hop(after(cot_send, x_near), "blk", side)

    wide_shape = shape((row_count, WIDE))
    made = call(
        functools.partial(project_kernel, heads, dp_count), [wide_shape] * (3 * heads),
        [SMEM] + [VMEM] * (4 + PARTS + dp_count),
        [pltpu.VMEM((width, 3 * columns), LOW), pltpu.VMEM((row_count, 2 * WIDE), FULL)],
        after(meta, cot_got), table, swap_q, swap_k, spread_v, *x_all, *qkv,
    )
    queries, keys, values = (made[at * heads : (at + 1) * heads] for at in range(3))
    out_rows = rows + EXTRA
    qkv_core = hop(after(jnp.stack([piece[out_rows:] for piece in qkv[1:]]), queries[0]), "blk", 1)
    for bit in spread_bits:
        keys, values = ([jnp.concatenate([one, hop(one, "blk", bit)]) for one in many] for many in (keys, values))
    key_count = keys[0].shape[0]
    q_block = max(WIDE, min(row_count, 512 * 1024 // key_count))
    attended = call(
        functools.partial(attend_kernel, heads, q_block),
        [shape((PARTS, block, columns))] + [shape((1, row_count), FULL)] * heads,
        [SMEM] * 2 + [VMEM] * (1 + 3 * heads),
        [pltpu.VMEM((row_count, heads * WIDE), LOW)],
        meta, lengths, *queries, *keys, *values, spread,
    )
    attended, lse = attended[0], attended[1:]
    att_send = after(attended, qkv_core, *(down_pieces[bit] for bit in dp_bits[:2]))
    att_core, att_near = hop(att_send, "blk", 1), hop(att_send, "blk", 2)
    att_all = [attended, att_core, att_near, hop(after(att_near, att_core), "blk", 1)]
    middle = PARTS // 2
    down_pieces[3] = jnp.concatenate(
        [hop(down_pieces[1][:middle], "dp", 2), hop(down_pieces[2][middle:], "dp", 1)]
    )
    for bit in dp_bits[2:]:
        for distance in range(bit):
            down_pieces[distance | bit] = hop(down_pieces[distance], "dp", bit)
    down_pieces = [down_pieces[distance] for distance in range(dp_count)]
    residual_one, normed_low, all_vectors, w_o = call(
        functools.partial(residual_kernel, dp_count),
        [shape((block, width), FULL), shape((block, width)), shape((8, width), FULL), shape((columns, width))],
        [SMEM] + [VMEM] * (2 + PARTS + dp_count + 1),
        [pltpu.VMEM((width, width), LOW), pltpu.VMEM((dp_count, EXTRA, 3 * columns), LOW)],
        after(meta, down_pieces[3]), x_own, w_output, *att_all, *qkv, qkv_core,
    )
    normed_core, normed_near = hop(normed_low, "blk", 1), hop(normed_low, "blk", 2)
    down_core = [hop(after(piece, normed_low), "blk", 1) for piece in down_pieces[1:]]
    down_all = (w_down, *down_pieces[1:], *down_core)
    gate_up_all = (gate_up_core, hop(after(gate_up_core, att_all[3], down_pieces[3]), "blk", 1))

    part_shape, w_shape = (PARTS, block, width), (dp_count, rows, width)
    down_copies = 2 * dp_count - 1
    grad_ffn, grad_branch, grad_one, layer_own, layer_back, sums = call(
        feed_kernel,
        [shape((block, width))] * 2 + [shape((block, width), FULL)] + [shape((local, width))] * 2
        + [shape((8, width), FULL)],
        [SMEM] * 2 + [VMEM] * 4 + [ANY] * (2 + len(down_all)),
        [
            pltpu.VMEM((3 * PARTS, *w_shape), LOW),
            pltpu.VMEM(part_shape, FULL),
            pltpu.VMEM(part_shape, FULL),
            pltpu.SemaphoreType.DMA((PARTS * (4 + down_copies),)),
        ],
        after(meta, normed_core), lengths, residual_one, all_vectors, cotangent, cot_got, *gate_up_all, *down_all,
    )
    ffn_core, ffn_near = hop(grad_ffn, "blk", 1), hop(grad_ffn, "blk", 2)
    normed_all = [normed_low, normed_core, normed_near, hop(after(normed_near, grad_ffn), "blk", 1)]

    long, chunk = shape((row_count, width)), shape((rows, width))
    hidden, gate_factor, up_factor = call(
        hidden_kernel, [long] * 3,
        [SMEM] + [VMEM] * PARTS + [ANY] * 2,
        [pltpu.VMEM(w_shape, LOW), pltpu.VMEM(w_shape, LOW), pltpu.SemaphoreType.DMA((4,))],
        after(meta, grad_ffn), *normed_all, *gate_up_all,
    )
    ffn_all = [grad_ffn, ffn_core, ffn_near, hop(after(ffn_near, hidden, ffn_core), "blk", 1)]
    branch_core, branch_near = (hop(after(grad_branch, ffn_near, hidden), "blk", bit) for bit in (1, 2))
    down_terms = call(
        down_kernel, [chunk] * dp_count, [SMEM] + [VMEM] * (1 + PARTS), [pltpu.VMEM((width, width), LOW)],
        after(meta, branch_core), hidden, *ffn_all,
    )
    down_got = send_terms(down_terms)
    gate_up_terms = call(
        gate_up_kernel, [chunk] * dp_count + [shape((width, width))],
        [SMEM] + [VMEM] * (2 + 2 * PARTS) + [ANY] * len(down_all),
        [pltpu.VMEM(w_shape, LOW), pltpu.VMEM((row_count, 2 * width), LOW)]
        + [pltpu.VMEM((width, width), LOW), pltpu.SemaphoreType.DMA((down_copies,))],
        after(meta, down_terms[0]), gate_factor, up_factor, *ffn_all, *normed_all, *down_all,
    )

    def sum_halves(total):
        for bit in sum_bits:
            low = total.astype(LOW)
            total = low.astype(FULL) + hop(low, "blk", bit).astype(FULL)
        return total.astype(LOW)

    branch_far = hop(after(branch_near, gate_up_terms[0], *(down_got[bit - 1] for bit in dp_bits)), "blk", 1)
    layer_got = hop(after(layer_back, branch_far), "blk", side)
    down_sum = sum_terms(down_terms, down_got)
    down_full = sum_halves(down_sum)
    gate_got = send_terms(gate_up_terms[:dp_count])
    up_sum = lax.psum_scatter(
        after(gate_up_terms[-1], branch_far).reshape(dp_count, rows, width), "dp", scatter_dimension=0, tiled=False
    )
    early = heads if spread_bits else heads - 1
    key_shape = shape((key_count, WIDE))
    back_scratch = [pltpu.VMEM((key_count, WIDE), FULL), pltpu.VMEM((key_count, 2 * WIDE), FULL)]
    back_scratch += [pltpu.VMEM((key_count, WIDE), FULL)] * 2
    *made, out_terms = call(
        functools.partial(attend_back_kernel, early, q_block),
        [wide_shape] * early + [key_shape] * (2 * early) + [wide_shape] * (heads - early) + [shape((width, columns))],
        [SMEM] * 2 + [VMEM] * (3 + 2 * PARTS + 4 * early),
        [pltpu.VMEM((PARTS, block, columns), LOW), *back_scratch] + [pltpu.VMEM((row_count, WIDE), LOW)] * early,
        after(meta, down_sum), lengths, w_o, spread, table,
        grad_branch, branch_core, branch_near, branch_far, *att_all,
        *queries[:early], *keys[:early], *values[:early], *lse[:early],
        late=[4, *range(9, 13 + 3 * early)],
    )
    grad_q, grad_k, grad_v = (made[at * early : (at + 1) * early] for at in range(3))
    gate_sum = sum_terms(gate_up_terms, [after(got, grad_q[0], layer_got) for got in gate_got])
    gate_full = sum_halves(gate_sum)
    down_near = hop(down_full, "blk", 2)
    for bit in reversed(spread_bits):
        middle = grad_k[0].shape[0] // 2
        grad_k, grad_v = (
            [
                (one[:middle].astype(FULL) + hop(one[middle:], "blk", bit).astype(FULL)).astype(LOW)
                for one in many
            ]
            for many in (grad_k, grad_v)
        )
    back_outs = [shape((rows + EXTRA, width))] * dp_count + [shape((2, block, width), FULL), shape((2, block, width))]
    back_weights = [pltpu.VMEM((width, 3 * columns), LOW), pltpu.VMEM((width, width), LOW)]
    back_operands = (spread, sums, out_terms, *grad_q, *grad_k, *grad_v, *x_all, *qkv)
    ready = after(meta, gate_sum, down_full)
    if spread_bits:
        made = call(
            functools.partial(projections_back_kernel, heads, dp_count), back_outs,
            [SMEM] + [VMEM] * len(back_operands), back_weights, ready, *back_operands,
        )
    else:
        made = call(
            functools.partial(last_back_kernel, heads, dp_count, q_block), back_outs,
            [SMEM] * 2 + [VMEM] * (6 + len(back_operands)),
            back_weights + [pltpu.VMEM((row_count, WIDE), LOW)] * 3 + back_scratch,
            ready, lengths, table, queries[-1], keys[-1], values[-1], lse[-1], made[-1], *back_operands,
        )
    *qkv_terms, token_keep, token_send = made
    up_sum = after(up_sum, token_keep).astype(FULL)

    first_gate = (gate_full, up_sum, down_near)
    token_got = hop(after(token_send, *first_gate), "blk", 1).astype(FULL)
    up_full = sum_halves(up_sum)
    near_send = (token_keep[1] + token_got[1]).astype(LOW)
    token_near = hop(near_send, "blk", 2)
    qkv_got = send_terms(qkv_terms)
    qkv_sum = sum_terms(qkv_terms, [after(got, token_near) for got in qkv_got]).astype(LOW)
    qkv_full = sum_halves(after(qkv_sum, up_full, token_near))
    pair_full = after(jnp.stack([gate_full, up_full]), qkv_sum)
    pair_core, pair_near = hop(pair_full, "blk", 1), hop(pair_full, "blk", 2)
    down_core, down_far = (hop(after(one, pair_core), "blk", 1) for one in (down_full, down_near))
    grad_rows = after(grad_one, qkv_sum) + token_keep[0] + token_got[0] + token_near.astype(FULL)
    rows_got = hop(grad_rows[local:].astype(LOW), "blk", side).astype(FULL)
    grad_down = call(
        join_rows_kernel, [shape((ff_rows, width), FULL)], [SMEM] + [VMEM] * PARTS, [],
        meta, down_full, down_core, down_near, down_far,
    )[0]
    pair_far = hop(after(pair_near, pair_core, grad_down), "blk", 1)
    qkv_core, qkv_near = (hop(after(qkv_full, pair_near), "blk", bit) for bit in (1, 2))
    grad_gate, grad_up = call(
        join_columns_kernel, [shape((rows, ff), FULL)] * 2, [SMEM] + [VMEM] * PARTS,
        [pltpu.VMEM((PARTS, 2, rows, width), LOW)], meta, pair_full, pair_core, pair_near, pair_far,
    )
    qkv_far = hop(after(qkv_near, qkv_core, grad_gate, rows_got), "blk", 1)
    grad_tokens = jnp.where(
        first, jnp.stack([grad_rows[:local], rows_got]), jnp.stack([rows_got, grad_rows[:local]])
    )[:, None]
    layer_out = jnp.where(first, jnp.stack([layer_own, layer_got]), jnp.stack([layer_got, layer_own]))[:, None]
    grad_query, grad_key, grad_value, grad_output, *vector_sums = call(
        join_projections_kernel, [shape((rows, width), FULL)] * 4 + [shape((rows,), FULL)] * 4,
        [SMEM] + [VMEM] * PARTS, [pltpu.VMEM((PARTS, rows + EXTRA, width), LOW)], meta, qkv_full, qkv_core, qkv_near, qkv_far,
    )
    return (
        layer_out, grad_tokens, grad_query, grad_key, grad_value, grad_output, grad_gate, grad_up, grad_down,
        vector_sums[0], vector_sums[1], vector_sums[2], vector_sums[3],
    )


def solution(mesh):
    slots = P(None, "dp", "blk", None)
    matrix, vector = P("dp", None), P("dp")
    return jax.shard_map(
        shards,
        mesh=mesh,
        in_specs=(slots, P(None, "dp")) + (matrix,) * 7 + (vector,) * 4 + (slots,),
        out_specs=(slots, slots) + (matrix,) * 7 + (vector,) * 4,
        check_vma=False,
    )
```
